32 devices in a mesh: grp: 4 (over y, core), fsdp: 8 (over z, x).
Axes of the slice: x: 2, y: 2, z: 4, core: 2. Of those that a mesh axis runs over, the one named last changes fastest.
Arguments:
- tokens: bfloat16 [6144, 8192], P(('grp', 'fsdp')), may hold values from -6 to 6
- targets: bfloat16 [6144, 1024], P(('grp', 'fsdp')), may hold values from -6 to 6
- row_owner_user: int32 [6144, 1], P(('grp', 'fsdp')), may hold values from 0 to 31; in each aligned block of 192 rows (0 to 191, 192 to 383, ...) at most 9 rows name the same one
- device_row_count: int32 [32], P(('grp', 'fsdp')), may hold values from 1 to 192, 4608 in all
- user_row_cap: int32 [32], replicated, may hold values from 48 to 383
- value_weight: bfloat16 [8192, 1024], P('fsdp'), may hold values from -0.0625 to 0.0625
- adapter_down: bfloat16 [8192, 64], replicated, may hold values from -0.0625 to 0.0625
- adapter_up: bfloat16 [64, 1024], replicated, may hold values from -0.75 to 0.75
- clip_norm_bound: float32 [1], replicated, may hold values from 2 to 6
- down_noise: float32 [8192, 64], P(('grp', 'fsdp')), may hold values from -0.12 to 0.12
- up_noise: float32 [64, 1024], P(None, ('grp', 'fsdp')), may hold values from -0.12 to 0.12
Outputs:
- update_a: float32 [8192, 64], P(('grp', 'fsdp'))
- update_b: float32 [64, 1024], P(None, ('grp', 'fsdp'))
The draws below stay inside these ranges and needn't reach their ends.
Inputs may be any that keep to these rules, and one draw needn't show every extreme that they name: `row_owner_user`: within the rows of one device (aligned blocks of 192 rows) no user is named by more than 9 rows, a bound that some block reaches. `device_row_count`: the counts sum to 4608.
All inputs are finite; a program needn't handle non-finite values. No bound on the sum of `device_row_count` on one device may be relied on, other than what follows from the above.
Results may differ from the reference program's by a relative error of at most 0.00084.
Values may be sent and summed in bfloat16 or wider, within the bound.
No kernel may reach another device: no remote copies, remote signals or barrier semaphores. Data moves between devices by JAX's collectives and lax.ppermute only.
A program may use at most 128 MiB of HBM per device.

```python
import math
import jax
import jax.numpy as jnp
import numpy as np
from jax import lax

MODEL_WIDTH = 8192
VALUE_WIDTH = 1024
ADAPTER_RANK = 64
STEPS = 2
TOK_DEV = 192
USERS = 32
MOST = 9
SLOTS = 288
TOKENS = 6144
N_GRP = 4
N_FSDP = 8
DEVICES = 32


def with_ends(drawn, own_key, low, high):
    spot = [jax.random.randint(jax.random.fold_in(own_key, axis), (), 0, length) for axis, length in enumerate(drawn.shape)]
    longest = drawn.shape.index(max(drawn.shape))
    neighbour = spot[:longest] + [(spot[longest] + 1) % drawn.shape[longest]] + spot[longest + 1:]
    return drawn.at[tuple(spot)].set(low).at[tuple(neighbour)].set(high)


def levels(rng, dims, pieces, least, largest):
    def one(axis_at, shards_of):
        heights = jax.random.uniform(jax.random.fold_in(jax.random.fold_in(rng, 6), axis_at), (shards_of,), jnp.float32, least / len(pieces), largest / len(pieces))
        return jnp.repeat(jnp.exp(heights), dims[axis_at] // shards_of).reshape((-1,) + (1,) * (len(dims) - axis_at - 1))

    level = one(*pieces[0])
    for cut in pieces[1:]:
        level = level * one(*cut)
    return level


def length_profile(count, total, bound, lean):
    weights = [(1 << 20) // math.isqrt(grade ** lean) + 1 for grade in range(2, count + 1)]
    surplus, holding = total - bound - (count - 1), [1] * (count - 1)
    while surplus > 0:
        free = [i for i in range(count - 1) if holding[i] < bound]
        pool, budget = sum([weights[i] for i in free]), surplus
        for i in free:
            addition = min(bound - holding[i], max(1, budget * weights[i] // pool), surplus)
            holding[i] = holding[i] + addition
            surplus = surplus - addition
    return np.array([bound] + holding)


def ragged(key, number_of, total, reach, lean):
    if number_of == 2:
        one = jax.random.randint(key, (), max(1, total - reach), min(reach, total - 1) + 1)
        return jnp.stack([one, total - one])
    sizes = jnp.asarray(length_profile(number_of, total, reach, lean), jnp.int32)
    pairs = (number_of - 1) // 2
    source_of, sink = sizes[1:1 + 2 * pairs:2], sizes[2:2 + 2 * pairs:2]
    slack = jnp.minimum(source_of - 1, reach - sink)
    passed = jax.random.randint(jax.random.fold_in(key, 1), (pairs,), 0, 1 << 20) % (slack + 1)
    sizes = sizes.at[1:1 + 2 * pairs:2].set(source_of - passed).at[2:2 + 2 * pairs:2].set(sink + passed)
    return sizes[jax.random.permutation(jax.random.fold_in(key, 2), number_of)]


def routed_block(stream_key, own, number, rows, amount, top, limit, skew):
    sequence = jax.random.permutation(stream_key, amount)
    crowded, usual = load_shares(amount, rows * top, limit, skew, True), load_shares(amount, rows * top, limit, skew, False)
    places = jnp.arange(amount)

    def named(lengths, offset_by):
        used = int((lengths > 0).sum())
        fixed = max(1, used // 4)
        shifted = fixed + (places - fixed + offset_by * (used - fixed)) % max(1, amount - fixed)
        return jnp.zeros((amount,), jnp.int32).at[sequence[jnp.where(places < fixed, places, shifted)]].set(jnp.asarray(lengths, jnp.int32))

    lengths = jnp.where(number % 4 == 0, named(crowded, number // 4), named(usual, number - number // 4 - 1))
    mixed = jax.random.permutation(jax.random.fold_in(own, 3), amount)
    giver, sink = mixed[0:amount // 2 * 2:2], mixed[1:amount // 2 * 2:2]
    room = jnp.minimum(lengths[giver] - 1, limit - lengths[sink]) // 2
    room = jnp.where((giver == sequence[0]) | (sink == sequence[0]) | (lengths[sink] == 0), 0, jnp.maximum(room, 0))
    shifted = jax.random.randint(jax.random.fold_in(own, 4), (amount // 2,), 0, 1 << 20) % (room + 1)
    lengths = lengths.at[giver].add(-shifted).at[sink].add(shifted)
    members = jnp.searchsorted(jnp.cumsum(lengths), jnp.arange(rows * top), side="right").astype(jnp.int32)
    table = members.reshape(top, rows).T
    table = table[jax.random.permutation(jax.random.fold_in(own, 1), rows)]
    offset_by = jax.random.randint(jax.random.fold_in(own, 2), (rows, 1), 0, top)
    return jnp.take_along_axis(table, (jnp.arange(top)[None, :] + offset_by) % top, axis=1)


def load_shares(amount, total, limit, skew, full):
    weights = [(1 << 20) // math.isqrt(standing ** skew) + 1 for standing in range(1, amount + 1)]
    largest = limit if full else min(limit, max(-(-total // amount), total * weights[0] // sum(weights)))
    least = 1 if total - largest >= amount - 1 else 0
    given, rest = [largest] + [least] * (amount - 1), total - largest - least * (amount - 1)
    while rest > 0:
        candidates = [i for i in range(1, amount) if given[i] < largest] or [i for i in range(1, amount) if given[i] < limit]
        whole, left = sum([weights[i] for i in candidates]), rest
        for i in candidates:
            addition = min(limit - given[i], max(1, left * weights[i] // whole), rest)
            given[i] = given[i] + addition
            rest = rest - addition
    return np.array(given)


def gaussian(own_key, shape, width, reach, shards=(), held_as=jnp.bfloat16):
    array = width * jax.random.normal(own_key, shape, jnp.float32)
    if shards:
        array = array * levels(own_key, shape, shards, -0.22, 0.18)
    return jnp.clip(array, -reach, reach).astype(held_as)


def setup_inputs(seed: int = 0) -> dict:
    streams_of = jax.random.split(jax.random.key(seed), 12)
    tokens = gaussian(streams_of[0], (TOKENS, MODEL_WIDTH), 1.0, 6.0, ((0, 32),))
    targets = gaussian(streams_of[1], (TOKENS, VALUE_WIDTH), 1.0, 6.0, ((0, 32),))
    row_owner_user_keys = jax.random.split(jax.random.fold_in(streams_of[2], 1), TOKENS // TOK_DEV)
    row_owner_user_turns = jax.random.permutation(jax.random.fold_in(streams_of[2], 3), TOKENS // TOK_DEV)
    row_owner_user = jax.vmap(lambda own, number: routed_block(jax.random.fold_in(streams_of[2], 2), own, number, TOK_DEV, USERS, 1, MOST, 2))(row_owner_user_keys, row_owner_user_turns).reshape((TOKENS, 1))
    device_row_count = ragged(streams_of[3], DEVICES, 3 * TOKENS // 4, TOK_DEV, 2).astype(jnp.int32)
    user_row_cap = with_ends(jax.random.randint(streams_of[4], (USERS,), TOK_DEV // 4, 2 * TOK_DEV), jax.random.fold_in(streams_of[4], 1), TOK_DEV // 4, (2 * TOK_DEV) - 1).astype(jnp.int32)
    value_weight = gaussian(streams_of[5], (MODEL_WIDTH, VALUE_WIDTH), MODEL_WIDTH ** -0.5, 0.0625, ((0, 8),))
    adapter_down = gaussian(streams_of[6], (MODEL_WIDTH, ADAPTER_RANK), MODEL_WIDTH ** -0.5, 0.0625)
    adapter_up = gaussian(streams_of[7], (ADAPTER_RANK, VALUE_WIDTH), ADAPTER_RANK ** -0.5, 0.75)
    clip_norm_bound = jnp.clip(jax.random.uniform(streams_of[8], (1,), jnp.float32, 2.0, 6.0), 2.0, 6.0)
    down_noise = gaussian(streams_of[9], (MODEL_WIDTH, ADAPTER_RANK), 0.02, 0.12, ((0, 32),), jnp.float32)
    up_noise = gaussian(streams_of[10], (ADAPTER_RANK, VALUE_WIDTH), 0.02, 0.12, ((1, 32),), jnp.float32)
    return {"tokens": tokens, "targets": targets, "row_owner_user": row_owner_user, "device_row_count": device_row_count, "user_row_cap": user_row_cap, "value_weight": value_weight, "adapter_down": adapter_down, "adapter_up": adapter_up, "clip_norm_bound": clip_norm_bound, "down_noise": down_noise, "up_noise": up_noise}


adapter_scale = 2.0
learn_rate = 0.05
epsilon = 1e-06

def adapter_step(input_rows, frozen_output, target_value, live_mask, capped_value, adapter_down, adapter_up, clipped_value_rows):
    current_down = adapter_down.astype(jnp.float32)
    current_up = adapter_up.astype(jnp.float32)
    for repeat in range(STEPS):
        a_half = current_down.astype(jnp.bfloat16)
        half_up_matrix = current_up.astype(jnp.bfloat16)
        hidden_input = jnp.dot(input_rows, a_half, preferred_element_type=jnp.float32).astype(jnp.bfloat16)
        value_output = frozen_output + adapter_scale * jnp.dot(hidden_input, half_up_matrix, preferred_element_type=jnp.float32)
        residual_error = (live_mask[:, None] * (value_output - target_value.astype(jnp.float32)) / capped_value).astype(jnp.bfloat16)
        up_gradient = adapter_scale * lax.dot_general(hidden_input, residual_error, (((0,), (0,)), ((), ())), preferred_element_type=jnp.float32)
        backward_pass = jnp.dot(residual_error, half_up_matrix.T, preferred_element_type=jnp.float32).astype(jnp.bfloat16)
        down_gradient = adapter_scale * lax.dot_general(input_rows, backward_pass, (((0,), (0,)), ((), ())), preferred_element_type=jnp.float32)
        current_down = current_down - learn_rate * down_gradient
        current_up = current_up - learn_rate * up_gradient
    down_delta = current_down - adapter_down.astype(jnp.float32)
    up_delta = current_up - adapter_up.astype(jnp.float32)
    total = jnp.sum(down_delta * down_delta) + jnp.sum(up_delta * up_delta)
    factor = jnp.minimum(1.0, clipped_value_rows / jnp.sqrt(total + epsilon))
    return (factor * down_delta, factor * up_delta)

def reference(tokens, targets, row_owner_user, device_row_count, user_row_cap, value_weight, adapter_down, adapter_up, clip_norm_bound, down_noise, up_noise):
    devices = N_GRP * N_FSDP
    user_of = row_owner_user[:, 0].reshape(devices, TOK_DEV)
    position = jnp.arange(TOK_DEV, dtype=jnp.int32)
    valid = position[None, :] < device_row_count[:, None]
    onehot = (user_of[:, :, None] == jnp.arange(USERS, dtype=jnp.int32)[None, None, :]).astype(jnp.int32)
    before_all = jnp.cumsum(onehot, axis=1) - onehot
    row_rank = lax.optimization_barrier(jnp.sum(before_all * onehot, axis=2))
    valid_hot = onehot * valid[:, :, None].astype(jnp.int32)
    flat = valid_hot.reshape(devices * TOK_DEV, USERS)
    before_valid = (jnp.cumsum(flat, axis=0) - flat).reshape(devices, TOK_DEV, USERS)
    earlier = lax.optimization_barrier(jnp.sum(before_valid * onehot, axis=2))
    cap_row = user_row_cap[user_of]
    kept = valid & (earlier < cap_row)
    source = jnp.arange(devices, dtype=jnp.int32)[:, None]
    slot_key = user_of * SLOTS + source * MOST + row_rank
    slot_key = jnp.where(kept, slot_key, USERS * SLOTS).reshape(-1).astype(jnp.int32)
    row_index = jnp.arange(TOKENS, dtype=jnp.int32)
    table = jnp.full((USERS * SLOTS,), TOKENS, dtype=jnp.int32).at[slot_key].set(row_index, mode='drop')
    table = table.reshape(USERS, SLOTS)
    tokens_pad = jnp.concatenate([tokens, jnp.zeros((1, MODEL_WIDTH), tokens.dtype)], axis=0)
    targets_pad = jnp.concatenate([targets, jnp.zeros((1, VALUE_WIDTH), targets.dtype)], axis=0)
    clipped_value_rows = clip_norm_bound[0]

    def one_user(carry, inputs):
        indices, capped_value = inputs
        input_rows = tokens_pad[indices]
        target_value = targets_pad[indices]
        live_mask = (indices < TOKENS).astype(jnp.float32)
        frozen_output = jnp.dot(input_rows, value_weight, preferred_element_type=jnp.float32)
        down_partial, up_partial = adapter_step(input_rows, frozen_output, target_value, live_mask, capped_value.astype(jnp.float32), adapter_down, adapter_up, clipped_value_rows)
        return ((carry[0] + down_partial, carry[1] + up_partial), None)
    start = (jnp.zeros((MODEL_WIDTH, ADAPTER_RANK), jnp.float32), jnp.zeros((ADAPTER_RANK, VALUE_WIDTH), jnp.float32))
    sums, unused = lax.scan(one_user, start, (table, user_row_cap))
    update_a = sums[0] + clipped_value_rows * down_noise
    update_b = sums[1] + clipped_value_rows * up_noise
    return (update_a, update_b)
```

```python
import jax
import jax.numpy as jnp
from jax import lax
from jax.experimental import pallas as pl
from jax.experimental.pallas import tpu as pltpu
from jax.sharding import PartitionSpec as P

STEPS = 2
ADAPTER_SCALE = 2.0
LEARN_RATE = 0.05
EPSILON = 1e-06

SUB = 8
LANES = 128
BOTH = ("grp", "fsdp")
VMEM_BYTES = 56 * 1024 * 1024

F32 = jnp.float32
BF16 = jnp.bfloat16


def dot(left, right, contract=((1,), (0,))):
    return lax.dot_general(left, right, (contract, ((), ())), preferred_element_type=F32)


def iota(shape, axis):
    return lax.broadcasted_iota(jnp.int32, shape, axis)


def pack_kernel(users, most, count_ref, owner_ref, tokens_ref, targets_ref, out_ref):
    rows = tokens_ref.shape[0]
    groups, rest = divmod(most, SUB)
    owner = owner_ref[...]
    first, second = (iota((rows, rows), 0), iota((rows, rows), 1))
    owner_row = jnp.sum(jnp.where(first == second, owner, 0), axis=0, keepdims=True)
    same = (owner == owner_row) & (first < second)
    rank = jnp.sum(same.astype(jnp.int32), axis=0, keepdims=True)
    line = iota((users * SUB, rows), 0)
    mine = line // SUB == owner_row
    slot = line % SUB
    column = 0
    for source in (tokens_ref, targets_ref):
        width = source.shape[1]
        for group in range(groups):
            pick = (mine & (rank == slot + group * SUB)).astype(BF16)
            step = min(width, 1024)
            for at in range(0, width, step):
                out_ref[:, column + at : column + at + step] = dot(
                    pick, source[:, at : at + step]
                ).astype(BF16)
            column += width
        piece = width // SUB
        for extra in range(rest):
            here = mine & (rank == groups * SUB + extra)
            total = None
            for part in range(SUB):
                pick = (here & (slot == part)).astype(BF16)
                term = dot(pick, source[:, part * piece : (part + 1) * piece])
                total = term if total is None else total + term
            out_ref[:, column : column + piece] = total.astype(BF16)
            column += piece
    used = mine & (iota((users * SUB, rows), 1) < count_ref[0])
    number = jnp.sum(used.astype(F32), axis=1, keepdims=True)
    out_ref[:, column : column + LANES] = jnp.broadcast_to(number, (users * SUB, LANES)).astype(
        BF16
    )


def user_kernel(
    devices,
    most,
    where_ref,
    clip_ref,
    got_ref,
    near_ref,
    far_ref,
    down_ref,
    up_ref,
    out_ref,
    x_ref,
    goal_ref,
    cut_ref,
    cut_goal_ref,
    used_ref,
    w_ref,
    frozen_ref,
    hidden_ref,
    a_half_ref,
    delta_ref,
    got_sem,
    w_sem,
):
    groups, rest = divmod(most, SUB)
    rank, width = down_ref.shape
    kv_width = up_ref.shape[1]
    whole = devices * SUB
    shards, half = (near_ref.shape[0], near_ref.shape[1])
    copies = []
    column = 0
    for full, cut in ((x_ref, cut_ref), (goal_ref, cut_goal_ref)):
        size = full.shape[1]
        for group in range(groups):
            copies.append(
                (got_ref.at[:, pl.ds(column, size)], full.at[pl.ds(group * whole, whole), :])
            )
            column += size
        for extra in range(rest):
            copies.append((got_ref.at[:, pl.ds(column, size // SUB)], cut.at[extra]))
            column += size // SUB
    copies.append((got_ref.at[:, pl.ds(column, LANES)], used_ref))
    copies = [
        pltpu.make_async_copy(source, target, got_sem.at[place])
        for place, (source, target) in enumerate(copies)
    ]
    for copy in copies:
        copy.start()

    def weight_copy(shard, side):
        source = (near_ref, far_ref)[side]
        return pltpu.make_async_copy(
            source.at[shard], w_ref.at[side, shard], w_sem.at[side, shard]
        )

    for shard in range(shards):
        weight_copy(shard, 0).start()
        weight_copy(shard, 1).start()
    for copy in copies:
        copy.wait()

    line, other = (iota((devices, whole), 0), iota((devices, whole), 1))
    for extra in range(rest):
        bottom = groups * whole + extra * devices
        for full, cut in ((x_ref, cut_ref), (goal_ref, cut_goal_ref)):
            piece = full.shape[1] // SUB
            for part in range(SUB):
                pick = (other == line * SUB + part).astype(BF16)
                full[bottom : bottom + devices, part * piece : (part + 1) * piece] = dot(
                    pick, cut[extra]
                ).astype(BF16)

    cap = where_ref[0].astype(F32)
    used = used_ref[...]
    pieces = []
    if groups:
        line, other = (iota((whole, whole), 0), iota((whole, whole), 1))
        earlier = dot(((other // SUB < line // SUB) & (other % SUB == 0)).astype(BF16), used)
        own = used.astype(F32)
        for group in range(groups):
            spot = (iota((whole, LANES), 0) % SUB + group * SUB).astype(F32)
            live = (spot < own) & (earlier + spot < cap)
            pieces.append(jnp.where(live, 1.0 / cap, 0.0)[:, :1])
    line, other = (iota((devices, whole), 0), iota((devices, whole), 1))
    earlier = dot((other < line * SUB).astype(BF16) * (other % SUB == 0).astype(BF16), used)
    own = dot((other == line * SUB).astype(BF16), used)
    for extra in range(rest):
        spot = float(groups * SUB + extra)
        live = (own > spot) & (earlier + spot < cap)
        pieces.append(jnp.where(live, 1.0 / cap, 0.0)[:, :1])
    scale = jnp.concatenate(pieces, axis=0) if len(pieces) > 1 else pieces[0]

    frozen_ref[...] = jnp.zeros_like(frozen_ref)
    hidden_ref[...] = jnp.zeros_like(hidden_ref)
    side = where_ref[1]

    def add_shard(shard, unused):
        weight_copy(shard, 0).wait()
        weight_copy(shard, 1).wait()
        near = pl.ds(pl.multiple_of((2 * shard + side) * half, half), half)
        far = pl.ds(pl.multiple_of((2 * shard + 1 - side) * half, half), half)
        near_x, far_x = (x_ref[:, near], x_ref[:, far])
        frozen_ref[...] += dot(near_x, w_ref[0, shard]) + dot(far_x, w_ref[1, shard])
        lanes = ((1,), (1,))
        hidden_ref[...] += dot(near_x, down_ref[:, near], lanes) + dot(
            far_x, down_ref[:, far], lanes
        )
        return unused

    lax.fori_loop(0, shards, add_shard, 0)

    rate = ADAPTER_SCALE * LEARN_RATE
    block = min(width, 1024)
    up = up_ref[...].astype(F32)
    up_half = up_ref[...]
    up_delta = jnp.zeros((rank, kv_width), F32)
    for step in range(STEPS):
        hidden = hidden_ref[...].astype(BF16)
        error = frozen_ref[...] + ADAPTER_SCALE * dot(hidden, up_half) - goal_ref[...].astype(F32)
        residual = (scale * error).astype(BF16)
        back = dot(residual, up_half, ((1,), (1,))).astype(BF16)
        up_delta = up_delta - rate * dot(hidden, residual, ((0,), (0,)))
        last = step == STEPS - 1
        if not last:
            up_half = (up + up_delta).astype(BF16)
            hidden_ref[...] = jnp.zeros_like(hidden_ref)

        def down_block(at, unused):
            lanes = pl.ds(pl.multiple_of(at * block, block), block)
            moved = -rate * dot(back, x_ref[:, lanes], ((0,), (0,)))
            if step:
                moved = moved + delta_ref[:, lanes]
            delta_ref[:, lanes] = moved
            if not last:
                half_down = (down_ref[:, lanes].astype(F32) + moved).astype(BF16)
                hidden_ref[...] += dot(x_ref[:, lanes], half_down, ((1,), (1,)))
                return unused
            return unused + jnp.sum(moved * moved)

        squares = lax.fori_loop(0, width // block, down_block, jnp.zeros((), F32))

    total = squares + jnp.sum(up_delta * up_delta) + EPSILON
    total = jnp.full((1, LANES), total, F32)
    factor = jnp.minimum(1.0, clip_ref[0] / jnp.sqrt(total))[:, :1]
    share = width // devices
    up_share = kv_width // devices
    up_turned = (factor * up_delta).T
    pieces = share // rank
    tall = up_share // pieces
    for device in range(devices):
        out_ref[device, :rank, :] = factor * delta_ref[:, device * share : (device + 1) * share]
        parts = [
            up_turned[device * up_share + at * tall : device * up_share + (at + 1) * tall]
            for at in range(pieces)
        ]
        out_ref[device, rank:, :] = (
            jnp.concatenate(parts, axis=1) if pieces > 1 else parts[0]
        )


def body(
    tokens,
    targets,
    row_owner_user,
    device_row_count,
    user_row_cap,
    value_weight,
    adapter_down,
    adapter_up,
    clip_norm_bound,
    down_noise,
    up_noise,
):
    groups, members = (lax.axis_size("grp"), lax.axis_size("fsdp"))
    devices = groups * members
    myself = lax.axis_index(BOTH)
    side = lax.axis_index("grp") % 2
    per_dev, width = tokens.shape
    kv_width = targets.shape[1]
    rank = adapter_down.shape[1]
    users = user_row_cap.shape[0]
    most = 3 * per_dev // (2 * devices)
    slots = devices * most
    whole = devices * SUB
    whole_groups, rest = divmod(most, SUB)
    smem = pl.BlockSpec(memory_space=pltpu.SMEM)
    vmem = pl.BlockSpec(memory_space=pltpu.VMEM)
    anywhere = pl.BlockSpec(memory_space=pl.ANY)

    half = value_weight.shape[0] // 2
    mine = lax.dynamic_slice_in_dim(value_weight, side * half, half, axis=0)
    near = lax.all_gather(mine, "fsdp", axis=0)
    far = lax.ppermute(near, "grp", [(at, at ^ 1) for at in range(groups)])

    columns = whole_groups * (width + kv_width) + rest * (width + kv_width) // SUB + LANES
    packed = pl.pallas_call(
        lambda *refs: pack_kernel(users, most, *refs),
        out_shape=jax.ShapeDtypeStruct((users * SUB, columns), BF16),
        in_specs=[smem, vmem, vmem, vmem],
        out_specs=vmem,
        compiler_params=pltpu.CompilerParams(vmem_limit_bytes=VMEM_BYTES),
        name="pack_rows",
    )(device_row_count, row_owner_user, tokens, targets)
    got = lax.all_to_all(
        packed.reshape(users, SUB, columns), BOTH, split_axis=0, concat_axis=0, tiled=True
    ).reshape(whole, columns)

    cap = lax.dynamic_slice_in_dim(user_row_cap, myself, 1)
    where = jnp.concatenate([cap, side[None].astype(jnp.int32)])
    share = width // devices
    tall = rank + kv_width // devices * rank // share
    package = pl.pallas_call(
        lambda *refs: user_kernel(devices, most, *refs),
        out_shape=jax.ShapeDtypeStruct((devices, tall, share), F32),
        in_specs=[smem, smem, anywhere, anywhere, anywhere, vmem, vmem],
        out_specs=vmem,
        scratch_shapes=[
            pltpu.VMEM((slots, width), BF16),
            pltpu.VMEM((slots, kv_width), BF16),
            pltpu.VMEM((max(rest, 1), whole, width // SUB), BF16),
            pltpu.VMEM((max(rest, 1), whole, kv_width // SUB), BF16),
            pltpu.VMEM((whole, LANES), BF16),
            pltpu.VMEM((2, members, half, kv_width), BF16),
            pltpu.VMEM((slots, kv_width), F32),
            pltpu.VMEM((slots, rank), F32),
            pltpu.VMEM((rank, width), BF16),
            pltpu.VMEM((rank, width), F32),
            pltpu.SemaphoreType.DMA((2 * (whole_groups + rest) + 1,)),
            pltpu.SemaphoreType.DMA((2, members)),
        ],
        compiler_params=pltpu.CompilerParams(vmem_limit_bytes=VMEM_BYTES),
        name="user_steps",
    )(where, clip_norm_bound, got, near, far, adapter_down.T, adapter_up)

    package = package.reshape(groups, members, tall, share)
    package = lax.all_to_all(package, "grp", split_axis=0, concat_axis=0, tiled=True)
    package = jnp.sum(package, axis=0)
    package = lax.all_to_all(package, "fsdp", split_axis=0, concat_axis=0, tiled=True)
    package = jnp.sum(package, axis=0)
    clip = clip_norm_bound[0]
    update_a = package[:rank].T + clip * down_noise
    pieces = share // rank
    up_sum = package[rank:].reshape(tall - rank, pieces, rank).transpose(1, 0, 2)
    update_b = up_sum.reshape(kv_width // devices, rank).T + clip * up_noise
    return (update_a, update_b)


def solution(mesh):
    in_specs = (
        P(BOTH, None),
        P(BOTH, None),
        P(BOTH, None),
        P(BOTH),
        P(),
        P("fsdp", None),
        P(),
        P(),
        P(),
        P(BOTH, None),
        P(None, BOTH),
    )
    out_specs = (P(BOTH, None), P(None, BOTH))
    return jax.shard_map(body, mesh=mesh, in_specs=in_specs, out_specs=out_specs, check_vma=False)
```

```python
import jax
import jax.numpy as jnp
from jax import lax
from jax.experimental import pallas as pl
from jax.experimental.pallas import tpu as pltpu
from jax.sharding import PartitionSpec as P

STEPS = 2
ADAPTER_SCALE = 2.0
LEARN_RATE = 0.05
EPSILON = 1e-06

SUB = 8
LANES = 128
BOTH = ("grp", "fsdp")
VMEM_BYTES = 56 * 1024 * 1024

F32 = jnp.float32
BF16 = jnp.bfloat16


def dot(left, right, contract=((1,), (0,))):
    return lax.dot_general(left, right, (contract, ((), ())), preferred_element_type=F32)


def iota(shape, axis):
    return lax.broadcasted_iota(jnp.int32, shape, axis)


def pack_kernel(users, most, count_ref, owner_ref, tokens_ref, targets_ref, out_ref):
    rows = tokens_ref.shape[0]
    groups, rest = divmod(most, SUB)
    owner = owner_ref[...]
    first, second = (iota((rows, rows), 0), iota((rows, rows), 1))
    owner_row = jnp.sum(jnp.where(first == second, owner, 0), axis=0, keepdims=True)
    same = (owner == owner_row) & (first < second)
    rank = jnp.sum(same.astype(jnp.int32), axis=0, keepdims=True)
    line = iota((users * SUB, rows), 0)
    mine = line // SUB == owner_row
    slot = line % SUB
    column = 0
    for source in (tokens_ref, targets_ref):
        width = source.shape[1]
        for group in range(groups):
            pick = (mine & (rank == slot + group * SUB)).astype(BF16)
            step = min(width, 1024)
            for at in range(0, width, step):
                out_ref[:, column + at : column + at + step] = dot(
                    pick, source[:, at : at + step]
                ).astype(BF16)
            column += width
        piece = width // SUB
        for extra in range(rest):
            here = mine & (rank == groups * SUB + extra)
            total = None
            for part in range(SUB):
                pick = (here & (slot == part)).astype(BF16)
                term = dot(pick, source[:, part * piece : (part + 1) * piece])
                total = term if total is None else total + term
            out_ref[:, column : column + piece] = total.astype(BF16)
            column += piece
    used = mine & (iota((users * SUB, rows), 1) < count_ref[0])
    number = jnp.sum(used.astype(F32), axis=1, keepdims=True)
    out_ref[:, column : column + LANES] = jnp.broadcast_to(number, (users * SUB, LANES)).astype(
        BF16
    )


def user_kernel(
    devices,
    members,
    most,
    where_ref,
    clip_ref,
    got_ref,
    down_ref,
    up_ref,
    *refs,
):
    shards = members
    near_refs, far_refs = (refs[:shards], refs[shards : 2 * shards])
    (
        keep_ref,
        send_ref,
        x_ref,
        goal_ref,
        cut_ref,
        cut_goal_ref,
        used_ref,
        w_ref,
        frozen_ref,
        hidden_ref,
        delta_ref,
        got_sem,
        w_sem,
    ) = refs[2 * shards :]
    groups, rest = divmod(most, SUB)
    rank, width = down_ref.shape
    kv_width = up_ref.shape[1]
    whole = devices * SUB
    half = near_refs[0].shape[0]
    copies = []
    column = 0
    for full, cut in ((x_ref, cut_ref), (goal_ref, cut_goal_ref)):
        size = full.shape[1]
        for group in range(groups):
            copies.append(
                (got_ref.at[:, pl.ds(column, size)], full.at[pl.ds(group * whole, whole), :])
            )
            column += size
        for extra in range(rest):
            copies.append((got_ref.at[:, pl.ds(column, size // SUB)], cut.at[extra]))
            column += size // SUB
    copies.append((got_ref.at[:, pl.ds(column, LANES)], used_ref))
    copies = [
        pltpu.make_async_copy(source, target, got_sem.at[place])
        for place, (source, target) in enumerate(copies)
    ]
    for copy in copies:
        copy.start()

    for place in range(shards):
        for at, source in enumerate((near_refs[place], far_refs[place])):
            pltpu.make_async_copy(source, w_ref.at[at, place], w_sem.at[at, place]).start()
    for copy in copies:
        copy.wait()

    line, other = (iota((devices, whole), 0), iota((devices, whole), 1))
    for extra in range(rest):
        bottom = groups * whole + extra * devices
        for full, cut in ((x_ref, cut_ref), (goal_ref, cut_goal_ref)):
            piece = full.shape[1] // SUB
            for part in range(SUB):
                pick = (other == line * SUB + part).astype(BF16)
                full[bottom : bottom + devices, part * piece : (part + 1) * piece] = dot(
                    pick, cut[extra]
                ).astype(BF16)

    cap = where_ref[0].astype(F32)
    used = used_ref[...]
    pieces = []
    if groups:
        line, other = (iota((whole, whole), 0), iota((whole, whole), 1))
        earlier = dot(((other // SUB < line // SUB) & (other % SUB == 0)).astype(BF16), used)
        own = used.astype(F32)
        for group in range(groups):
            spot = (iota((whole, LANES), 0) % SUB + group * SUB).astype(F32)
            live = (spot < own) & (earlier + spot < cap)
            pieces.append(jnp.where(live, 1.0 / cap, 0.0)[:, :1])
    line, other = (iota((devices, whole), 0), iota((devices, whole), 1))
    earlier = dot((other < line * SUB).astype(BF16) * (other % SUB == 0).astype(BF16), used)
    own = dot((other == line * SUB).astype(BF16), used)
    for extra in range(rest):
        spot = float(groups * SUB + extra)
        live = (own > spot) & (earlier + spot < cap)
        pieces.append(jnp.where(live, 1.0 / cap, 0.0)[:, :1])
    scale = jnp.concatenate(pieces, axis=0) if len(pieces) > 1 else pieces[0]

    frozen_ref[...] = jnp.zeros_like(frozen_ref)
    hidden_ref[...] = jnp.zeros_like(hidden_ref)
    side = where_ref[1]

    def add_shard(place, unused):
        for at in range(2):
            block = w_ref.at[at, place]
            pltpu.make_async_copy(block, block, w_sem.at[at, place]).wait()
        shard = where_ref[3 + place]
        near = pl.ds(pl.multiple_of((2 * shard + side) * half, half), half)
        far = pl.ds(pl.multiple_of((2 * shard + 1 - side) * half, half), half)
        near_x, far_x = (x_ref[:, near], x_ref[:, far])
        frozen_ref[...] += dot(near_x, w_ref[0, place]) + dot(far_x, w_ref[1, place])
        lanes = ((1,), (1,))
        hidden_ref[...] += dot(near_x, down_ref[:, near], lanes) + dot(
            far_x, down_ref[:, far], lanes
        )
        return unused

    lax.fori_loop(0, shards, add_shard, 0)

    rate = ADAPTER_SCALE * LEARN_RATE
    block = min(width, 1024)
    up = up_ref[...].astype(F32)
    up_half = up_ref[...]
    up_delta = jnp.zeros((rank, kv_width), F32)
    for step in range(STEPS):
        hidden = hidden_ref[...].astype(BF16)
        error = frozen_ref[...] + ADAPTER_SCALE * dot(hidden, up_half) - goal_ref[...].astype(F32)
        residual = (scale * error).astype(BF16)
        back = dot(residual, up_half, ((1,), (1,))).astype(BF16)
        up_delta = up_delta - rate * dot(hidden, residual, ((0,), (0,)))
        last = step == STEPS - 1
        if not last:
            up_half = (up + up_delta).astype(BF16)
            hidden_ref[...] = jnp.zeros_like(hidden_ref)

        def down_block(at, unused):
            lanes = pl.ds(pl.multiple_of(at * block, block), block)
            moved = -rate * dot(back, x_ref[:, lanes], ((0,), (0,)))
            if step:
                moved = moved + delta_ref[:, lanes]
            delta_ref[:, lanes] = moved
            if not last:
                half_down = (down_ref[:, lanes].astype(F32) + moved).astype(BF16)
                hidden_ref[...] += dot(x_ref[:, lanes], half_down, ((1,), (1,)))
                return unused
            return unused + jnp.sum(moved * moved)

        squares = lax.fori_loop(0, width // block, down_block, jnp.zeros((), F32))

    total = squares + jnp.sum(up_delta * up_delta) + EPSILON
    total = jnp.full((1, LANES), total, F32)
    factor = jnp.minimum(1.0, clip_ref[0] / jnp.sqrt(total))[:, :1]
    share = width // devices
    up_share = kv_width // devices
    up_turned = (factor * up_delta).T
    pieces = share // rank
    tall = up_share // pieces

    def write(core, target):
        for pair in range(devices // members // 2):
            for member in range(members):
                device = (2 * pair + core) * members + member
                spot = lax.bitwise_xor(where_ref[2], pair)
                moved = delta_ref[:, device * share : (device + 1) * share]
                target[spot, member, :rank, :] = factor * moved
                first = device * up_share
                parts = [
                    up_turned[first + at * tall : first + (at + 1) * tall] for at in range(pieces)
                ]
                target[spot, member, rank:, :] = (
                    jnp.concatenate(parts, axis=1) if pieces > 1 else parts[0]
                )

    for core in range(2):
        mine = side == core

        @pl.when(mine)
        def _():
            write(core, keep_ref)

        @pl.when(jnp.logical_not(mine))
        def _():
            write(core, send_ref)


def gather_weight(mine, members):
    line = members // 2
    index = lax.axis_index("fsdp")
    spot, inner = (index // 2, index % 2)

    def hop(value, way):
        pairs = [
            (2 * at + one, 2 * (at + way) + one)
            for at in range(line)
            for one in range(2)
            if 0 <= at + way < line
        ]
        return lax.ppermute(value, "fsdp", pairs)

    def across(value):
        return lax.ppermute(value, "fsdp", [(at, at ^ 1) for at in range(members)])

    blocks = [(mine, spot)]
    ups, downs = ({0: mine}, {0: mine})
    for step in range(1, line):
        ups[step] = hop(ups[step - 1], 1)
        downs[step] = hop(downs[step - 1], -1)
    for step in range(1, line // 2 + 1):
        above = spot >= step
        blocks.append(
            (jnp.where(above, ups[step], downs[step]), jnp.where(above, spot - step, spot + step))
        )
    for step in range(1, line // 2):
        both = (spot >= step) & (spot < line - step)
        late = line - step
        value = jnp.where(both, downs[step], jnp.where(spot < step, downs[late], ups[late]))
        number = jnp.where(
            both, spot + step, jnp.where(spot < step, spot + late, spot - late)
        )
        blocks.append((value, number))
    values, numbers = ([], [])
    for value, number in blocks:
        values += [value, across(value)]
        numbers += [2 * number + inner, 2 * number + 1 - inner]
    return values, jnp.stack(numbers).astype(jnp.int32)


def body(
    tokens,
    targets,
    row_owner_user,
    device_row_count,
    user_row_cap,
    value_weight,
    adapter_down,
    adapter_up,
    clip_norm_bound,
    down_noise,
    up_noise,
):
    groups, members = (lax.axis_size("grp"), lax.axis_size("fsdp"))
    devices = groups * members
    myself = lax.axis_index(BOTH)
    side = lax.axis_index("grp") % 2
    per_dev, width = tokens.shape
    kv_width = targets.shape[1]
    rank = adapter_down.shape[1]
    users = user_row_cap.shape[0]
    most = 3 * per_dev // (2 * devices)
    slots = devices * most
    whole = devices * SUB
    whole_groups, rest = divmod(most, SUB)
    smem = pl.BlockSpec(memory_space=pltpu.SMEM)
    vmem = pl.BlockSpec(memory_space=pltpu.VMEM)
    anywhere = pl.BlockSpec(memory_space=pl.ANY)

    half = value_weight.shape[0] // 2
    mine = lax.dynamic_slice_in_dim(value_weight, side * half, half, axis=0)
    near, numbers = gather_weight(mine, members)
    far = [lax.ppermute(block, "grp", [(at, at ^ 1) for at in range(groups)]) for block in near]

    columns = whole_groups * (width + kv_width) + rest * (width + kv_width) // SUB + LANES
    packed = pl.pallas_call(
        lambda *refs: pack_kernel(users, most, *refs),
        out_shape=jax.ShapeDtypeStruct((users * SUB, columns), BF16),
        in_specs=[smem, vmem, vmem, vmem],
        out_specs=vmem,
        compiler_params=pltpu.CompilerParams(vmem_limit_bytes=VMEM_BYTES),
        name="pack_rows",
    )(device_row_count, row_owner_user, tokens, targets)
    got = lax.all_to_all(
        packed.reshape(users, SUB, columns), BOTH, split_axis=0, concat_axis=0, tiled=True
    ).reshape(whole, columns)

    cap = lax.dynamic_slice_in_dim(user_row_cap, myself, 1)
    pair = lax.axis_index("grp") // 2
    where = jnp.concatenate([cap, jnp.stack([side, pair]).astype(jnp.int32), numbers])
    share = width // devices
    tall = rank + kv_width // devices * rank // share
    package = jax.ShapeDtypeStruct((groups // 2, members, tall, share), F32)
    keep, send = pl.pallas_call(
        lambda *refs: user_kernel(devices, members, most, *refs),
        out_shape=[package] * 2,
        in_specs=[smem, smem, anywhere, vmem, vmem] + [anywhere] * (2 * members),
        out_specs=[vmem] * 2,
        scratch_shapes=[
            pltpu.VMEM((slots, width), BF16),
            pltpu.VMEM((slots, kv_width), BF16),
            pltpu.VMEM((max(rest, 1), whole, width // SUB), BF16),
            pltpu.VMEM((max(rest, 1), whole, kv_width // SUB), BF16),
            pltpu.VMEM((whole, LANES), BF16),
            pltpu.VMEM((2, members, half, kv_width), BF16),
            pltpu.VMEM((slots, kv_width), F32),
            pltpu.VMEM((slots, rank), F32),
            pltpu.VMEM((rank, width), F32),
            pltpu.SemaphoreType.DMA((2 * (whole_groups + rest) + 1,)),
            pltpu.SemaphoreType.DMA((2, members)),
        ],
        compiler_params=pltpu.CompilerParams(vmem_limit_bytes=VMEM_BYTES),
        name="user_steps",
    )(where, clip_norm_bound, got, adapter_down.T, adapter_up, *near, *far)

    package = keep + lax.ppermute(send, "grp", [(at, at ^ 1) for at in range(groups)])
    bit = groups // 4
    while bit:
        partner = [(at, at ^ (2 * bit)) for at in range(groups)]
        package = package[:bit] + lax.ppermute(package[bit:], "grp", partner)
        bit //= 2
    package = package[0]
    package = lax.all_to_all(package, "fsdp", split_axis=0, concat_axis=0, tiled=True)
    package = jnp.sum(package, axis=0)
    clip = clip_norm_bound[0]
    update_a = package[:rank].T + clip * down_noise
    pieces = share // rank
    up_sum = package[rank:].reshape(tall - rank, pieces, rank).transpose(1, 0, 2)
    update_b = up_sum.reshape(kv_width // devices, rank).T + clip * up_noise
    return (update_a, update_b)


def solution(mesh):
    in_specs = (
        P(BOTH, None),
        P(BOTH, None),
        P(BOTH, None),
        P(BOTH),
        P(),
        P("fsdp", None),
        P(),
        P(),
        P(),
        P(BOTH, None),
        P(None, BOTH),
    )
    out_specs = (P(BOTH, None), P(None, BOTH))
    return jax.shard_map(body, mesh=mesh, in_specs=in_specs, out_specs=out_specs, check_vma=False)
```

```python
import jax
import jax.numpy as jnp
from jax import lax
from jax.experimental import pallas as pl
from jax.experimental.pallas import tpu as pltpu
from jax.sharding import PartitionSpec as P

STEPS = 2
ADAPTER_SCALE = 2.0
LEARN_RATE = 0.05
EPSILON = 1e-06

SUB = 8
LANES = 128
BOTH = ("grp", "fsdp")
VMEM_BYTES = 56 * 1024 * 1024

F32 = jnp.float32
BF16 = jnp.bfloat16


def dot(left, right, contract=((1,), (0,))):
    return lax.dot_general(left, right, (contract, ((), ())), preferred_element_type=F32)


def iota(shape, axis):
    return lax.broadcasted_iota(jnp.int32, shape, axis)


def pack_kernel(users, most, count_ref, owner_ref, tokens_ref, targets_ref, out_ref):
    rows = tokens_ref.shape[0]
    groups, rest = divmod(most, SUB)
    owner = owner_ref[...]
    first, second = (iota((rows, rows), 0), iota((rows, rows), 1))
    owner_row = jnp.sum(jnp.where(first == second, owner, 0), axis=0, keepdims=True)
    same = (owner == owner_row) & (first < second)
    rank = jnp.sum(same.astype(jnp.int32), axis=0, keepdims=True)
    line = iota((users * SUB, rows), 0)
    mine = line // SUB == owner_row
    slot = line % SUB
    column = 0
    for source in (tokens_ref, targets_ref):
        width = source.shape[1]
        for group in range(groups):
            pick = (mine & (rank == slot + group * SUB)).astype(BF16)
            step = min(width, 1024)
            for at in range(0, width, step):
                out_ref[:, column + at : column + at + step] = dot(
                    pick, source[:, at : at + step]
                ).astype(BF16)
            column += width
        piece = width // SUB
        for extra in range(rest):
            here = mine & (rank == groups * SUB + extra)
            total = None
            for part in range(SUB):
                pick = (here & (slot == part)).astype(BF16)
                term = dot(pick, source[:, part * piece : (part + 1) * piece])
                total = term if total is None else total + term
            out_ref[:, column : column + piece] = total.astype(BF16)
            column += piece
    used = mine & (iota((users * SUB, rows), 1) < count_ref[0])
    number = jnp.sum(used.astype(F32), axis=1, keepdims=True)
    out_ref[:, column : column + LANES] = jnp.broadcast_to(number, (users * SUB, LANES)).astype(
        BF16
    )


def user_kernel(
    devices,
    members,
    most,
    where_ref,
    clip_ref,
    got_ref,
    down_ref,
    up_ref,
    *refs,
):
    (
        near_ref,
        far_ref,
        keep_refs,
        send_refs,
        x_ref,
        goal_ref,
        cut_ref,
        cut_goal_ref,
        used_ref,
        w_ref,
        frozen_ref,
        hidden_ref,
        delta_ref,
        got_sem,
        w_sem,
    ) = refs[:2] + (refs[2:4], refs[4:6]) + refs[6:]
    groups, rest = divmod(most, SUB)
    rank, width = down_ref.shape
    kv_width = up_ref.shape[1]
    whole = devices * SUB
    shards, half, unused = near_ref.shape
    copies = []
    column = 0
    for full, cut in ((x_ref, cut_ref), (goal_ref, cut_goal_ref)):
        size = full.shape[1]
        for group in range(groups):
            copies.append(
                (got_ref.at[:, pl.ds(column, size)], full.at[pl.ds(group * whole, whole), :])
            )
            column += size
        for extra in range(rest):
            copies.append((got_ref.at[:, pl.ds(column, size // SUB)], cut.at[extra]))
            column += size // SUB
    copies.append((got_ref.at[:, pl.ds(column, LANES)], used_ref))
    copies = [
        pltpu.make_async_copy(source, target, got_sem.at[place])
        for place, (source, target) in enumerate(copies)
    ]
    for copy in copies:
        copy.start()

    def weight_copy(at, place):
        source = (near_ref, far_ref)[at].at[place]
        return pltpu.make_async_copy(source, w_ref.at[at, place], w_sem.at[at, place])

    ahead = min(2, shards)
    for place in range(ahead):
        weight_copy(0, place).start()
        weight_copy(1, place).start()
    for copy in copies:
        copy.wait()
    for place in range(ahead, shards):
        weight_copy(0, place).start()
        weight_copy(1, place).start()

    line, other = (iota((devices, whole), 0), iota((devices, whole), 1))
    for extra in range(rest):
        bottom = groups * whole + extra * devices
        for full, cut in ((x_ref, cut_ref), (goal_ref, cut_goal_ref)):
            piece = full.shape[1] // SUB
            for part in range(SUB):
                pick = (other == line * SUB + part).astype(BF16)
                full[bottom : bottom + devices, part * piece : (part + 1) * piece] = dot(
                    pick, cut[extra]
                ).astype(BF16)

    cap = where_ref[0].astype(F32)
    used = used_ref[...]
    pieces = []
    if groups:
        line, other = (iota((whole, whole), 0), iota((whole, whole), 1))
        earlier = dot(((other // SUB < line // SUB) & (other % SUB == 0)).astype(BF16), used)
        own = used.astype(F32)
        for group in range(groups):
            spot = (iota((whole, LANES), 0) % SUB + group * SUB).astype(F32)
            live = (spot < own) & (earlier + spot < cap)
            pieces.append(jnp.where(live, 1.0 / cap, 0.0)[:, :1])
    line, other = (iota((devices, whole), 0), iota((devices, whole), 1))
    earlier = dot((other < line * SUB).astype(BF16) * (other % SUB == 0).astype(BF16), used)
    own = dot((other == line * SUB).astype(BF16), used)
    for extra in range(rest):
        spot = float(groups * SUB + extra)
        live = (own > spot) & (earlier + spot < cap)
        pieces.append(jnp.where(live, 1.0 / cap, 0.0)[:, :1])
    scale = jnp.concatenate(pieces, axis=0) if len(pieces) > 1 else pieces[0]

    frozen_ref[...] = jnp.zeros_like(frozen_ref)
    hidden_ref[...] = jnp.zeros_like(hidden_ref)
    side = where_ref[1]

    def add_shard(place, unused):
        weight_copy(0, place).wait()
        weight_copy(1, place).wait()
        shard = where_ref[4 + place]
        near = pl.ds(pl.multiple_of((2 * shard + side) * half, half), half)
        far = pl.ds(pl.multiple_of((2 * shard + 1 - side) * half, half), half)
        near_x, far_x = (x_ref[:, near], x_ref[:, far])
        frozen_ref[...] += dot(near_x, w_ref[0, place]) + dot(far_x, w_ref[1, place])
        lanes = ((1,), (1,))
        hidden_ref[...] += dot(near_x, down_ref[:, near], lanes) + dot(
            far_x, down_ref[:, far], lanes
        )
        return unused

    lax.fori_loop(0, shards, add_shard, 0)

    rate = ADAPTER_SCALE * LEARN_RATE
    block = min(width, 1024)
    up = up_ref[...].astype(F32)
    up_half = up_ref[...]
    up_delta = jnp.zeros((rank, kv_width), F32)
    for step in range(STEPS):
        hidden = hidden_ref[...].astype(BF16)
        error = frozen_ref[...] + ADAPTER_SCALE * dot(hidden, up_half) - goal_ref[...].astype(F32)
        residual = (scale * error).astype(BF16)
        back = dot(residual, up_half, ((1,), (1,))).astype(BF16)
        up_delta = up_delta - rate * dot(hidden, residual, ((0,), (0,)))
        last = step == STEPS - 1
        if not last:
            up_half = (up + up_delta).astype(BF16)
            hidden_ref[...] = jnp.zeros_like(hidden_ref)

        def down_block(at, unused):
            lanes = pl.ds(pl.multiple_of(at * block, block), block)
            moved = -rate * dot(back, x_ref[:, lanes], ((0,), (0,)))
            if step:
                moved = moved + delta_ref[:, lanes]
            delta_ref[:, lanes] = moved
            if not last:
                half_down = (down_ref[:, lanes].astype(F32) + moved).astype(BF16)
                hidden_ref[...] += dot(x_ref[:, lanes], half_down, ((1,), (1,)))
                return unused
            return unused + jnp.sum(moved * moved)

        squares = lax.fori_loop(0, width // block, down_block, jnp.zeros((), F32))

    total = squares + jnp.sum(up_delta * up_delta) + EPSILON
    total = jnp.full((1, LANES), total, F32)
    factor = jnp.minimum(1.0, clip_ref[0] / jnp.sqrt(total))[:, :1]
    share = width // devices
    up_share = kv_width // devices
    up_turned = (factor * up_delta).T
    pieces = share // rank
    tall = up_share // pieces

    def write(core, targets):
        edge = targets[0].shape[3]
        for pair in range(devices // members // 2):
            for member in range(members):
                device = (2 * pair + core) * members + member
                spot = lax.bitwise_xor(where_ref[2], pair)
                inner = lax.bitwise_xor(where_ref[3], member % 2)
                outer = member // 2
                moved = factor * delta_ref[:, device * share : (device + 1) * share]
                targets[0][spot, inner, outer] = moved[:edge]
                targets[1][spot, inner, outer, : rank - edge, :] = moved[edge:]
                first = device * up_share
                parts = [
                    up_turned[first + at * tall : first + (at + 1) * tall] for at in range(pieces)
                ]
                targets[1][spot, inner, outer, rank - edge :, :] = (
                    jnp.concatenate(parts, axis=1) if pieces > 1 else parts[0]
                )

    for core in range(2):
        mine = side == core

        @pl.when(mine)
        def _():
            write(core, keep_refs)

        @pl.when(jnp.logical_not(mine))
        def _():
            write(core, send_refs)


def halve(package, axis, bits, partner):
    bit = package.shape[bits] // 2
    while bit:
        keep = lax.slice_in_dim(package, 0, bit, axis=bits)
        send = lax.slice_in_dim(package, bit, 2 * bit, axis=bits)
        pairs = [(at, at ^ (partner * bit)) for at in range(lax.axis_size(axis))]
        package = lax.ppermute(send, axis, pairs) + keep
        bit //= 2
    return package


def body(
    tokens,
    targets,
    row_owner_user,
    device_row_count,
    user_row_cap,
    value_weight,
    adapter_down,
    adapter_up,
    clip_norm_bound,
    down_noise,
    up_noise,
):
    groups, members = (lax.axis_size("grp"), lax.axis_size("fsdp"))
    devices = groups * members
    myself = lax.axis_index(BOTH)
    side = lax.axis_index("grp") % 2
    per_dev, width = tokens.shape
    kv_width = targets.shape[1]
    rank = adapter_down.shape[1]
    users = user_row_cap.shape[0]
    most = 3 * per_dev // (2 * devices)
    slots = devices * most
    whole = devices * SUB
    whole_groups, rest = divmod(most, SUB)
    smem = pl.BlockSpec(memory_space=pltpu.SMEM)
    vmem = pl.BlockSpec(memory_space=pltpu.VMEM)
    anywhere = pl.BlockSpec(memory_space=pl.ANY)

    half = value_weight.shape[0] // 2
    mine = lax.dynamic_slice_in_dim(value_weight, side * half, half, axis=0)
    path = list(range(0, members, 2)) + list(range(1, members, 2))[::-1]
    near = lax.all_gather(mine, "fsdp", axis=0, axis_index_groups=[path])
    swap = [(at, at ^ 1) for at in range(groups)]
    far = lax.ppermute(near, "grp", swap)

    columns = whole_groups * (width + kv_width) + rest * (width + kv_width) // SUB + LANES
    packed = pl.pallas_call(
        lambda *refs: pack_kernel(users, most, *refs),
        out_shape=jax.ShapeDtypeStruct((users * SUB, columns), BF16),
        in_specs=[smem, vmem, vmem, vmem],
        out_specs=vmem,
        compiler_params=pltpu.CompilerParams(vmem_limit_bytes=VMEM_BYTES),
        name="pack_rows",
    )(device_row_count, row_owner_user, tokens, targets)
    cap = lax.dynamic_slice_in_dim(user_row_cap, myself, 1)
    pair = lax.axis_index("grp") // 2
    inner = lax.axis_index("fsdp") % 2
    spots = jnp.stack([side, pair, inner] + [jnp.int32(place) for place in path])
    where = jnp.concatenate([cap, spots.astype(jnp.int32)])
    packed, where = lax.optimization_barrier((packed, where))
    got = lax.all_to_all(
        packed.reshape(users, SUB, columns), BOTH, split_axis=0, concat_axis=0, tiled=True
    ).reshape(whole, columns)
    share = width // devices
    tall = rank + kv_width // devices * rank // share
    edge = tall // (2 * SUB) * SUB
    grid = (groups // 2, 2, members // 2)
    streams = [jax.ShapeDtypeStruct(grid + (size, share), F32) for size in (edge, tall - edge)]
    kept_y, kept_x, sent_y, sent_x = pl.pallas_call(
        lambda *refs: user_kernel(devices, members, most, *refs),
        out_shape=streams * 2,
        in_specs=[smem, smem, anywhere, vmem, vmem, anywhere, anywhere],
        out_specs=[vmem] * 4,
        scratch_shapes=[
            pltpu.VMEM((slots, width), BF16),
            pltpu.VMEM((slots, kv_width), BF16),
            pltpu.VMEM((max(rest, 1), whole, width // SUB), BF16),
            pltpu.VMEM((max(rest, 1), whole, kv_width // SUB), BF16),
            pltpu.VMEM((whole, LANES), BF16),
            pltpu.VMEM((2, members, half, kv_width), BF16),
            pltpu.VMEM((slots, kv_width), F32),
            pltpu.VMEM((slots, rank), F32),
            pltpu.VMEM((rank, width), F32),
            pltpu.SemaphoreType.DMA((2 * (whole_groups + rest) + 1,)),
            pltpu.SemaphoreType.DMA((2, members)),
        ],
        compiler_params=pltpu.CompilerParams(vmem_limit_bytes=VMEM_BYTES),
        name="user_steps",
    )(where, clip_norm_bound, got, adapter_down.T, adapter_up, near, far)

    first = kept_y + lax.ppermute(sent_y, "grp", swap)
    second = kept_x + lax.ppermute(sent_x, "grp", swap)
    first = halve(halve(first, "grp", 0, 2), "fsdp", 1, 1)
    second = halve(halve(second, "fsdp", 1, 1), "grp", 0, 2)
    package = jnp.concatenate([first[0, 0], second[0, 0]], axis=1)
    lines = [list(range(one, members, 2)) for one in range(2)]
    package = lax.all_to_all(
        package, "fsdp", split_axis=0, concat_axis=0, axis_index_groups=lines, tiled=True
    )
    package = jnp.sum(package, axis=0)
    clip = clip_norm_bound[0]
    update_a = package[:rank].T + clip * down_noise
    pieces = share // rank
    up_sum = package[rank:].reshape(tall - rank, pieces, rank).transpose(1, 0, 2)
    update_b = up_sum.reshape(kv_width // devices, rank).T + clip * up_noise
    return (update_a, update_b)


def solution(mesh):
    in_specs = (
        P(BOTH, None),
        P(BOTH, None),
        P(BOTH, None),
        P(BOTH),
        P(),
        P("fsdp", None),
        P(),
        P(),
        P(),
        P(BOTH, None),
        P(None, BOTH),
    )
    out_specs = (P(BOTH, None), P(None, BOTH))
    return jax.shard_map(body, mesh=mesh, in_specs=in_specs, out_specs=out_specs, check_vma=False)
```

```python
import jax
import jax.numpy as jnp
from jax import lax
from jax.experimental import pallas as pl
from jax.experimental.pallas import tpu as pltpu
from jax.sharding import PartitionSpec as P

STEPS = 2
ADAPTER_SCALE = 2.0
LEARN_RATE = 0.05
EPSILON = 1e-06

SUB = 8
LANES = 128
BOTH = ("grp", "fsdp")
VMEM_BYTES = 56 * 1024 * 1024

F32 = jnp.float32
BF16 = jnp.bfloat16


def dot(left, right, contract=((1,), (0,))):
    return lax.dot_general(left, right, (contract, ((), ())), preferred_element_type=F32)


def iota(shape, axis):
    return lax.broadcasted_iota(jnp.int32, shape, axis)


def pack_kernel(users, most, count_ref, owner_ref, tokens_ref, targets_ref, out_ref):
    rows = tokens_ref.shape[0]
    groups, rest = divmod(most, SUB)
    owner_row = owner_ref[...]
    first, second = (iota((rows, rows), 0), iota((rows, rows), 1))
    owner = jnp.sum(jnp.where(first == second, owner_row, 0), axis=1, keepdims=True)
    same = (owner == owner_row) & (first < second)
    rank = jnp.sum(same.astype(jnp.int32), axis=0, keepdims=True)
    line = iota((users * SUB, rows), 0)
    mine = line // SUB == owner_row
    slot = line % SUB
    column = 0
    for source in (tokens_ref, targets_ref):
        width = source.shape[1]
        for group in range(groups):
            pick = (mine & (rank == slot + group * SUB)).astype(BF16)
            step = min(width, 1024)
            for at in range(0, width, step):
                out_ref[:, column + at : column + at + step] = dot(
                    pick, source[:, at : at + step]
                ).astype(BF16)
            column += width
        piece = width // SUB
        for extra in range(rest):
            here = mine & (rank == groups * SUB + extra)
            total = None
            for part in range(SUB):
                pick = (here & (slot == part)).astype(BF16)
                term = dot(pick, source[:, part * piece : (part + 1) * piece])
                total = term if total is None else total + term
            out_ref[:, column : column + piece] = total.astype(BF16)
            column += piece
    used = mine & (iota((users * SUB, rows), 1) < count_ref[0])
    number = jnp.sum(used.astype(F32), axis=1, keepdims=True)
    out_ref[:, column : column + LANES] = jnp.broadcast_to(number, (users * SUB, LANES)).astype(
        BF16
    )


def weight_rings(groups, members):
    round_trip = [(at, 0) for at in range(groups // 2)]
    round_trip += [(at, 1) for at in reversed(range(groups // 2))]
    length, layers = (len(round_trip), members // 2)
    rings = []
    for core in range(2):
        up, down = ([], [])
        low, high = (list(range(length // 2)), list(range(length // 2, length)))
        for layer in range(1, layers):
            turned = layer % 2 == 0
            up += [(layer, at) for at in (low[::-1] if turned else low)]
            down += [(layer, at) for at in (high if turned else high[::-1])]
        path = [(0, at) for at in reversed(range(length))] + up + down[::-1]
        ring = []
        for layer, at in path:
            pair, inner = round_trip[(at + core * length // 2) % length]
            ring.append((2 * pair + core) * members + 2 * layer + inner)
        rings.append(ring)
    return rings


def weight_copies(ring_of, groups, members, source, target, sems):
    pairs = groups // 2
    columns = source.shape[2]
    side = lax.rem(lax.axis_index("grp"), 2)
    rings = weight_rings(groups, members)

    def copy(member, pair):
        spots = [ring.index((2 * pair + core) * members + member) for core, ring in enumerate(rings)]
        spot = jnp.where(side == ring_of, spots[0], spots[1])
        return pltpu.make_async_copy(
            source.at[spot],
            target.at[member, :, pl.ds(pair * columns, columns)],
            sems.at[member, pair],
        )

    return [[copy(member, pair) for pair in range(pairs)] for member in range(members)]


def wait_block(target, place, pairs, sems):
    columns = target.shape[2] // pairs
    for pair in range(pairs):
        block = target.at[place, :, pl.ds(pair * columns, columns)]
        pltpu.make_async_copy(block, block, sems.at[place, pair]).wait()


def near_kernel(
    groups_of,
    members,
    most,
    got_ref,
    near_ref,
    down_ref,
    x_out_ref,
    frozen_ref,
    hidden_ref,
    x_ref,
    cut_ref,
    w_ref,
    got_sem,
    out_sem,
    w_sem,
):
    groups, rest = divmod(most, SUB)
    devices = groups_of * members
    width = x_ref.shape[1]
    whole = devices * SUB
    half = w_ref.shape[1]
    copies = []
    column = 0
    for group in range(groups):
        copies.append(
            (got_ref.at[:, pl.ds(column, width)], x_ref.at[pl.ds(group * whole, whole), :])
        )
        column += width
    for extra in range(rest):
        copies.append((got_ref.at[:, pl.ds(column, width // SUB)], cut_ref.at[extra]))
        column += width // SUB
    copies = [
        pltpu.make_async_copy(source, target, got_sem.at[place])
        for place, (source, target) in enumerate(copies)
    ]
    for copy in copies:
        copy.start()
    weights = weight_copies(0, groups_of, members, near_ref, w_ref, w_sem)
    for place, pieces in enumerate(weights):
        if place == 2:
            for copy in copies:
                copy.wait()
        for copy in pieces:
            copy.start()
    join_pieces(devices, groups * whole, rest, x_ref, cut_ref)
    out = pltpu.make_async_copy(x_ref, x_out_ref, out_sem)
    out.start()

    frozen_ref[...] = jnp.zeros_like(frozen_ref)
    hidden_ref[...] = jnp.zeros_like(hidden_ref)
    side = lax.rem(lax.axis_index("grp"), 2)

    def add_shard(shard, unused):
        wait_block(w_ref, shard, groups_of // 2, w_sem)
        near = pl.ds(pl.multiple_of((2 * shard + side) * half, half), half)
        both = pl.ds(pl.multiple_of(2 * shard * half, 2 * half), 2 * half)
        frozen_ref[...] += dot(x_ref[:, near], w_ref[shard])
        hidden_ref[...] += dot(x_ref[:, both], down_ref[:, both], ((1,), (1,)))
        return unused

    lax.fori_loop(0, members, add_shard, 0)
    out.wait()


def join_pieces(devices, bottom, rest, full, cut):
    line, other = (iota((devices, devices * SUB), 0), iota((devices, devices * SUB), 1))
    piece = full.shape[1] // SUB
    for extra in range(rest):
        first = bottom + extra * devices
        for part in range(SUB):
            pick = (other == line * SUB + part).astype(BF16)
            full[first : first + devices, part * piece : (part + 1) * piece] = dot(
                pick, cut[extra]
            ).astype(BF16)


def user_kernel(
    groups_of,
    members,
    most,
    cap_ref,
    clip_ref,
    got_ref,
    rows_ref,
    near_frozen_ref,
    near_hidden_ref,
    far_ref,
    down_ref,
    up_ref,
    *refs,
):
    keep_refs, send_refs = (refs[0:2], refs[2:4])
    (
        x_ref,
        goal_ref,
        cut_goal_ref,
        used_ref,
        w_ref,
        frozen_ref,
        hidden_ref,
        delta_ref,
        got_sem,
        w_sem,
    ) = refs[4:]
    groups, rest = divmod(most, SUB)
    devices = groups_of * members
    rank, width = down_ref.shape
    kv_width = up_ref.shape[1]
    whole = devices * SUB
    half = w_ref.shape[1]
    copies = [(rows_ref, x_ref)]
    column = groups * width + rest * width // SUB
    for group in range(groups):
        copies.append(
            (got_ref.at[:, pl.ds(column, kv_width)], goal_ref.at[pl.ds(group * whole, whole), :])
        )
        column += kv_width
    for extra in range(rest):
        copies.append((got_ref.at[:, pl.ds(column, kv_width // SUB)], cut_goal_ref.at[extra]))
        column += kv_width // SUB
    copies.append((got_ref.at[:, pl.ds(column, LANES)], used_ref))
    copies = [
        pltpu.make_async_copy(source, target, got_sem.at[place])
        for place, (source, target) in enumerate(copies)
    ]
    for copy in copies[1:] + copies[:1]:
        copy.start()
    for pieces in weight_copies(1, groups_of, members, far_ref, w_ref, w_sem):
        for copy in pieces:
            copy.start()
    for copy in copies[1:]:
        copy.wait()
    join_pieces(devices, groups * whole, rest, goal_ref, cut_goal_ref)

    cap = cap_ref[lax.axis_index("grp") * members + lax.axis_index("fsdp")].astype(F32)
    used = used_ref[...]
    pieces = []
    if groups:
        line, other = (iota((whole, whole), 0), iota((whole, whole), 1))
        earlier = dot(((other // SUB < line // SUB) & (other % SUB == 0)).astype(BF16), used)
        own = used.astype(F32)
        for group in range(groups):
            spot = (iota((whole, LANES), 0) % SUB + group * SUB).astype(F32)
            live = (spot < own) & (earlier + spot < cap)
            pieces.append(jnp.where(live, 1.0 / cap, 0.0)[:, :1])
    line, other = (iota((devices, whole), 0), iota((devices, whole), 1))
    earlier = dot((other < line * SUB).astype(BF16) * (other % SUB == 0).astype(BF16), used)
    own = dot((other == line * SUB).astype(BF16), used)
    for extra in range(rest):
        spot = float(groups * SUB + extra)
        live = (own > spot) & (earlier + spot < cap)
        pieces.append(jnp.where(live, 1.0 / cap, 0.0)[:, :1])
    scale = jnp.concatenate(pieces, axis=0) if len(pieces) > 1 else pieces[0]

    frozen_ref[...] = near_frozen_ref[...]
    hidden_ref[...] = near_hidden_ref[...]
    side = lax.rem(lax.axis_index("grp"), 2)
    copies[0].wait()

    def add_shard(shard, unused):
        wait_block(w_ref, shard, groups_of // 2, w_sem)
        far = pl.ds(pl.multiple_of((2 * shard + 1 - side) * half, half), half)
        frozen_ref[...] += dot(x_ref[:, far], w_ref[shard])
        return unused

    lax.fori_loop(0, members, add_shard, 0)

    rate = ADAPTER_SCALE * LEARN_RATE
    block = min(width, 1024)
    up = up_ref[...].astype(F32)
    up_half = up_ref[...]
    up_delta = jnp.zeros((rank, kv_width), F32)
    for step in range(STEPS):
        hidden = hidden_ref[...].astype(BF16)
        error = frozen_ref[...] + ADAPTER_SCALE * dot(hidden, up_half) - goal_ref[...].astype(F32)
        residual = (scale * error).astype(BF16)
        back = dot(residual, up_half, ((1,), (1,))).astype(BF16)
        up_delta = up_delta - rate * dot(hidden, residual, ((0,), (0,)))
        last = step == STEPS - 1
        if not last:
            up_half = (up + up_delta).astype(BF16)
            hidden_ref[...] = jnp.zeros_like(hidden_ref)

        def down_block(at, unused):
            lanes = pl.ds(pl.multiple_of(at * block, block), block)
            moved = -rate * dot(back, x_ref[:, lanes], ((0,), (0,)))
            if step:
                moved = moved + delta_ref[:, lanes]
            delta_ref[:, lanes] = moved
            if not last:
                half_down = (down_ref[:, lanes].astype(F32) + moved).astype(BF16)
                hidden_ref[...] += dot(x_ref[:, lanes], half_down, ((1,), (1,)))
                return unused
            return unused + jnp.sum(moved * moved)

        squares = lax.fori_loop(0, width // block, down_block, jnp.zeros((), F32))

    total = squares + jnp.sum(up_delta * up_delta) + EPSILON
    total = jnp.full((1, LANES), total, F32)
    factor = jnp.minimum(1.0, clip_ref[0] / jnp.sqrt(total))[:, :1]
    share = width // devices
    up_share = kv_width // devices
    up_turned = (factor * up_delta).T
    pieces = share // rank
    tall = up_share // pieces

    def write(core, targets):
        edge = targets[0].shape[3]
        for pair in range(devices // members // 2):
            for member in range(members):
                device = (2 * pair + core) * members + member
                spot = lax.bitwise_xor(lax.div(lax.axis_index("grp"), 2), pair)
                inner = lax.bitwise_xor(lax.rem(lax.axis_index("fsdp"), 2), member % 2)
                outer = member // 2
                moved = factor * delta_ref[:, device * share : (device + 1) * share]
                targets[0][spot, inner, outer] = moved[:edge]
                targets[1][spot, inner, outer, : rank - edge, :] = moved[edge:]
                first = device * up_share
                parts = [
                    up_turned[first + at * tall : first + (at + 1) * tall] for at in range(pieces)
                ]
                targets[1][spot, inner, outer, rank - edge :, :] = (
                    jnp.concatenate(parts, axis=1) if pieces > 1 else parts[0]
                )

    for core in range(2):
        mine = side == core

        @pl.when(mine)
        def _():
            write(core, keep_refs)

        @pl.when(jnp.logical_not(mine))
        def _():
            write(core, send_refs)


def halve(package, axis, bits, partner):
    bit = package.shape[bits] // 2
    while bit:
        keep = lax.slice_in_dim(package, 0, bit, axis=bits)
        send = lax.slice_in_dim(package, bit, 2 * bit, axis=bits)
        pairs = [(at, at ^ (partner * bit)) for at in range(lax.axis_size(axis))]
        package = lax.ppermute(send, axis, pairs) + keep
        bit //= 2
    return package


def body(
    tokens,
    targets,
    row_owner_user,
    device_row_count,
    user_row_cap,
    value_weight,
    adapter_down,
    adapter_up,
    clip_norm_bound,
    down_noise,
    up_noise,
):
    groups, members = (lax.axis_size("grp"), lax.axis_size("fsdp"))
    devices = groups * members
    side = lax.axis_index("grp") % 2
    per_dev, width = tokens.shape
    kv_width = targets.shape[1]
    rank = adapter_down.shape[1]
    users = user_row_cap.shape[0]
    most = 3 * per_dev // (2 * devices)
    slots = devices * most
    whole = devices * SUB
    whole_groups, rest = divmod(most, SUB)
    smem = pl.BlockSpec(memory_space=pltpu.SMEM)
    vmem = pl.BlockSpec(memory_space=pltpu.VMEM)
    anywhere = pl.BlockSpec(memory_space=pl.ANY)

    half = value_weight.shape[0] // 2
    piece = kv_width // (groups // 2)
    pair = lax.axis_index("grp") // 2
    mine = lax.dynamic_slice(value_weight, (side * half, pair * piece), (half, piece))
    near = lax.all_gather(mine, BOTH, axis=0, axis_index_groups=weight_rings(groups, members))
    swap = [(at, at ^ 1) for at in range(groups)]
    far = lax.ppermute(near, "grp", swap)

    columns = whole_groups * (width + kv_width) + rest * (width + kv_width) // SUB + LANES
    packed = pl.pallas_call(
        lambda *refs: pack_kernel(users, most, *refs),
        out_shape=jax.ShapeDtypeStruct((users * SUB, columns), BF16),
        in_specs=[smem, vmem, vmem, vmem],
        out_specs=vmem,
        compiler_params=pltpu.CompilerParams(vmem_limit_bytes=VMEM_BYTES),
        name="pack_rows",
    )(device_row_count, row_owner_user.reshape(1, per_dev), tokens, targets)
    got = lax.all_to_all(
        packed.reshape(users, SUB, columns), BOTH, split_axis=0, concat_axis=0, tiled=True
    ).reshape(whole, columns)
    share = width // devices
    tall = rank + kv_width // devices * rank // share
    down = adapter_down.T
    rows, near_frozen, near_hidden = pl.pallas_call(
        lambda *refs: near_kernel(groups, members, most, *refs),
        out_shape=[
            jax.ShapeDtypeStruct((slots, width), BF16),
            jax.ShapeDtypeStruct((slots, kv_width), F32),
            jax.ShapeDtypeStruct((slots, rank), F32),
        ],
        in_specs=[anywhere, anywhere, vmem],
        out_specs=[anywhere, vmem, vmem],
        scratch_shapes=[
            pltpu.VMEM((slots, width), BF16),
            pltpu.VMEM((max(rest, 1), whole, width // SUB), BF16),
            pltpu.VMEM((members, half, kv_width), BF16),
            pltpu.SemaphoreType.DMA((whole_groups + rest,)),
            pltpu.SemaphoreType.DMA,
            pltpu.SemaphoreType.DMA((members, groups // 2)),
        ],
        compiler_params=pltpu.CompilerParams(vmem_limit_bytes=VMEM_BYTES),
        cost_estimate=pl.CostEstimate(
            flops=slots * width * kv_width, bytes_accessed=3 * 10**7, transcendentals=0
        ),
        name="near_product",
    )(got, near, down)

    edge = tall // (2 * SUB) * SUB
    grid = (groups // 2, 2, members // 2)
    streams = [jax.ShapeDtypeStruct(grid + (size, share), F32) for size in (edge, tall - edge)]
    kept_y, kept_x, sent_y, sent_x = pl.pallas_call(
        lambda *refs: user_kernel(groups, members, most, *refs),
        out_shape=streams * 2,
        in_specs=[smem, smem, anywhere, anywhere, vmem, vmem, anywhere, vmem, vmem],
        out_specs=[vmem] * 4,
        scratch_shapes=[
            pltpu.VMEM((slots, width), BF16),
            pltpu.VMEM((slots, kv_width), BF16),
            pltpu.VMEM((max(rest, 1), whole, kv_width // SUB), BF16),
            pltpu.VMEM((whole, LANES), BF16),
            pltpu.VMEM((members, half, kv_width), BF16),
            pltpu.VMEM((slots, kv_width), F32),
            pltpu.VMEM((slots, rank), F32),
            pltpu.VMEM((rank, width), F32),
            pltpu.SemaphoreType.DMA((whole_groups + rest + 2,)),
            pltpu.SemaphoreType.DMA((members, groups // 2)),
        ],
        compiler_params=pltpu.CompilerParams(vmem_limit_bytes=VMEM_BYTES),
        name="user_steps",
    )(user_row_cap, clip_norm_bound, got, rows, near_frozen, near_hidden, far, down, adapter_up)

    first = kept_y + lax.ppermute(sent_y, "grp", swap)
    second = kept_x + lax.ppermute(sent_x, "grp", swap)
    first = halve(halve(first, "grp", 0, 2), "fsdp", 1, 1)
    second = halve(halve(second, "fsdp", 1, 1), "grp", 0, 2)
    package = jnp.concatenate([first[0, 0], second[0, 0]], axis=1)
    lines = [list(range(one, members, 2)) for one in range(2)]
    package = lax.all_to_all(
        package, "fsdp", split_axis=0, concat_axis=0, axis_index_groups=lines, tiled=True
    )
    package = jnp.sum(package, axis=0)
    clip = clip_norm_bound[0]
    update_a = package[:rank].T + clip * down_noise
    pieces = share // rank
    up_sum = package[rank:].reshape(tall - rank, pieces, rank).transpose(1, 0, 2)
    update_b = up_sum.reshape(kv_width // devices, rank).T + clip * up_noise
    return (update_a, update_b)


def solution(mesh):
    in_specs = (
        P(BOTH, None),
        P(BOTH, None),
        P(BOTH, None),
        P(BOTH),
        P(),
        P("fsdp", None),
        P(),
        P(),
        P(),
        P(BOTH, None),
        P(None, BOTH),
    )
    out_specs = (P(BOTH, None), P(None, BOTH))
    return jax.shard_map(body, mesh=mesh, in_specs=in_specs, out_specs=out_specs, check_vma=False)
```

```python
import jax
import jax.numpy as jnp
from jax import lax
from jax.experimental import pallas as pl
from jax.experimental.pallas import tpu as pltpu
from jax.sharding import PartitionSpec as P

STEPS = 2
ADAPTER_SCALE = 2.0
LEARN_RATE = 0.05
EPSILON = 1e-06

SUB = 8
LANES = 128
BOTH = ("grp", "fsdp")
VMEM_BYTES = 56 * 1024 * 1024

F32 = jnp.float32
BF16 = jnp.bfloat16


def dot(left, right, contract=((1,), (0,))):
    return lax.dot_general(left, right, (contract, ((), ())), preferred_element_type=F32)


def iota(shape, axis):
    return lax.broadcasted_iota(jnp.int32, shape, axis)


def pack_kernel(users, most, count_ref, owner_ref, tokens_ref, targets_ref, out_ref):
    rows = tokens_ref.shape[0]
    groups, rest = divmod(most, SUB)
    owner_row = owner_ref[...]
    first, second = (iota((rows, rows), 0), iota((rows, rows), 1))
    owner = jnp.sum(jnp.where(first == second, owner_row, 0), axis=1, keepdims=True)
    same = (owner == owner_row) & (first < second)
    rank = jnp.sum(same.astype(jnp.int32), axis=0, keepdims=True)
    line = iota((users * SUB, rows), 0)
    mine = line // SUB == owner_row
    slot = line % SUB
    column = 0
    for source in (tokens_ref, targets_ref):
        width = source.shape[1]
        for group in range(groups):
            pick = (mine & (rank == slot + group * SUB)).astype(BF16)
            step = min(width, 1024)
            for at in range(0, width, step):
                out_ref[:, column + at : column + at + step] = dot(
                    pick, source[:, at : at + step]
                ).astype(BF16)
            column += width
        piece = width // SUB
        for extra in range(rest):
            here = mine & (rank == groups * SUB + extra)
            total = None
            for part in range(SUB):
                pick = (here & (slot == part)).astype(BF16)
                term = dot(pick, source[:, part * piece : (part + 1) * piece])
                total = term if total is None else total + term
            out_ref[:, column : column + piece] = total.astype(BF16)
            column += piece
    used = mine & (iota((users * SUB, rows), 1) < count_ref[0])
    number = jnp.sum(used.astype(F32), axis=1, keepdims=True)
    out_ref[:, column : column + LANES] = jnp.broadcast_to(number, (users * SUB, LANES)).astype(
        BF16
    )


def weight_rings(groups, members):
    round_trip = [(at, 0) for at in range(groups // 2)]
    round_trip += [(at, 1) for at in reversed(range(groups // 2))]
    length, layers = (len(round_trip), members // 2)
    rings = []
    for core in range(2):
        up, down = ([], [])
        low, high = (list(range(length // 2)), list(range(length // 2, length)))
        for layer in range(1, layers):
            turned = layer % 2 == 0
            up += [(layer, at) for at in (low[::-1] if turned else low)]
            down += [(layer, at) for at in (high if turned else high[::-1])]
        path = [(0, at) for at in reversed(range(length))] + up + down[::-1]
        ring = []
        for layer, at in path:
            pair, inner = round_trip[(at + core * length // 2) % length]
            ring.append((2 * pair + core) * members + 2 * layer + inner)
        rings.append(ring)
    return rings


def weight_copies(ring_of, groups, members, source, target, sems):
    pairs = groups // 2
    columns = source.shape[2]
    side = lax.rem(lax.axis_index("grp"), 2)
    rings = weight_rings(groups, members)

    def copy(member, pair):
        spots = [ring.index((2 * pair + core) * members + member) for core, ring in enumerate(rings)]
        spot = jnp.where(side == ring_of, spots[0], spots[1])
        return pltpu.make_async_copy(
            source.at[spot],
            target.at[member, :, pl.ds(pair * columns, columns)],
            sems.at[member, pair],
        )

    return [[copy(member, pair) for pair in range(pairs)] for member in range(members)]


def wait_block(target, place, pairs, sems):
    columns = target.shape[2] // pairs
    for pair in range(pairs):
        block = target.at[place, :, pl.ds(pair * columns, columns)]
        pltpu.make_async_copy(block, block, sems.at[place, pair]).wait()


def near_kernel(
    groups_of,
    members,
    most,
    got_ref,
    near_ref,
    down_ref,
    x_out_ref,
    frozen_ref,
    hidden_ref,
    x_ref,
    cut_ref,
    w_ref,
    got_sem,
    out_sem,
    w_sem,
):
    groups, rest = divmod(most, SUB)
    devices = groups_of * members
    width = x_ref.shape[1]
    whole = devices * SUB
    half = w_ref.shape[1]
    copies = []
    column = 0
    for group in range(groups):
        copies.append(
            (got_ref.at[:, pl.ds(column, width)], x_ref.at[pl.ds(group * whole, whole), :])
        )
        column += width
    for extra in range(rest):
        copies.append((got_ref.at[:, pl.ds(column, width // SUB)], cut_ref.at[extra]))
        column += width // SUB
    copies = [
        pltpu.make_async_copy(source, target, got_sem.at[place])
        for place, (source, target) in enumerate(copies)
    ]
    for copy in copies:
        copy.start()
    weights = weight_copies(0, groups_of, members, near_ref, w_ref, w_sem)
    for place, pieces in enumerate(weights):
        if place == 2:
            for copy in copies:
                copy.wait()
        for copy in pieces:
            copy.start()
    join_pieces(devices, groups * whole, rest, x_ref, cut_ref)
    out = pltpu.make_async_copy(x_ref, x_out_ref, out_sem)
    out.start()

    frozen_ref[...] = jnp.zeros_like(frozen_ref)
    hidden_ref[...] = jnp.zeros_like(hidden_ref)
    side = lax.rem(lax.axis_index("grp"), 2)

    def add_shard(shard, unused):
        wait_block(w_ref, shard, groups_of // 2, w_sem)
        near = pl.ds(pl.multiple_of((2 * shard + side) * half, half), half)
        both = pl.ds(pl.multiple_of(2 * shard * half, 2 * half), 2 * half)
        frozen_ref[...] += dot(x_ref[:, near], w_ref[shard])
        hidden_ref[...] += dot(x_ref[:, both], down_ref[:, both], ((1,), (1,)))
        return unused

    lax.fori_loop(0, members, add_shard, 0, unroll=2)
    out.wait()


def join_pieces(devices, bottom, rest, full, cut):
    line, other = (iota((devices, devices * SUB), 0), iota((devices, devices * SUB), 1))
    piece = full.shape[1] // SUB
    for extra in range(rest):
        first = bottom + extra * devices
        for part in range(SUB):
            pick = (other == line * SUB + part).astype(BF16)
            full[first : first + devices, part * piece : (part + 1) * piece] = dot(
                pick, cut[extra]
            ).astype(BF16)


def user_kernel(
    groups_of,
    members,
    most,
    cap_ref,
    clip_ref,
    got_ref,
    rows_ref,
    near_frozen_ref,
    near_hidden_ref,
    far_ref,
    down_ref,
    up_ref,
    *refs,
):
    keep_ref, send_ref = refs[:2]
    (
        x_ref,
        goal_ref,
        cut_goal_ref,
        used_ref,
        w_ref,
        frozen_ref,
        hidden_ref,
        delta_ref,
        got_sem,
        w_sem,
    ) = refs[2:]
    groups, rest = divmod(most, SUB)
    devices = groups_of * members
    rank, width = down_ref.shape
    kv_width = up_ref.shape[1]
    whole = devices * SUB
    half = w_ref.shape[1]
    copies = [(rows_ref, x_ref)]
    column = groups * width + rest * width // SUB
    for group in range(groups):
        copies.append(
            (got_ref.at[:, pl.ds(column, kv_width)], goal_ref.at[pl.ds(group * whole, whole), :])
        )
        column += kv_width
    for extra in range(rest):
        copies.append((got_ref.at[:, pl.ds(column, kv_width // SUB)], cut_goal_ref.at[extra]))
        column += kv_width // SUB
    copies.append((got_ref.at[:, pl.ds(column, LANES)], used_ref))
    copies = [
        pltpu.make_async_copy(source, target, got_sem.at[place])
        for place, (source, target) in enumerate(copies)
    ]
    for copy in copies[1:] + copies[:1]:
        copy.start()
    for pieces in weight_copies(1, groups_of, members, far_ref, w_ref, w_sem):
        for copy in pieces:
            copy.start()
    for copy in copies[1:]:
        copy.wait()
    join_pieces(devices, groups * whole, rest, goal_ref, cut_goal_ref)

    cap = cap_ref[lax.axis_index("grp") * members + lax.axis_index("fsdp")].astype(F32)
    used = used_ref[...]
    pieces = []
    if groups:
        line, other = (iota((whole, whole), 0), iota((whole, whole), 1))
        earlier = dot(((other // SUB < line // SUB) & (other % SUB == 0)).astype(BF16), used)
        own = used.astype(F32)
        for group in range(groups):
            spot = (iota((whole, LANES), 0) % SUB + group * SUB).astype(F32)
            live = (spot < own) & (earlier + spot < cap)
            pieces.append(jnp.where(live, 1.0 / cap, 0.0)[:, :1])
    line, other = (iota((devices, whole), 0), iota((devices, whole), 1))
    earlier = dot((other < line * SUB).astype(BF16) * (other % SUB == 0).astype(BF16), used)
    own = dot((other == line * SUB).astype(BF16), used)
    for extra in range(rest):
        spot = float(groups * SUB + extra)
        live = (own > spot) & (earlier + spot < cap)
        pieces.append(jnp.where(live, 1.0 / cap, 0.0)[:, :1])
    scale = jnp.concatenate(pieces, axis=0) if len(pieces) > 1 else pieces[0]

    frozen_ref[...] = near_frozen_ref[...]
    hidden_ref[...] = near_hidden_ref[...]
    side = lax.rem(lax.axis_index("grp"), 2)
    copies[0].wait()

    def add_shard(shard, unused):
        wait_block(w_ref, shard, groups_of // 2, w_sem)
        far = pl.ds(pl.multiple_of((2 * shard + 1 - side) * half, half), half)
        frozen_ref[...] += dot(x_ref[:, far], w_ref[shard])
        return unused

    lax.fori_loop(0, members, add_shard, 0, unroll=2)

    rate = ADAPTER_SCALE * LEARN_RATE
    block = min(width, 1024)
    up = up_ref[...].astype(F32)
    up_half = up_ref[...]
    up_delta = jnp.zeros((rank, kv_width), F32)
    for step in range(STEPS):
        hidden = hidden_ref[...].astype(BF16)
        error = frozen_ref[...] + ADAPTER_SCALE * dot(hidden, up_half) - goal_ref[...].astype(F32)
        residual = (scale * error).astype(BF16)
        back = dot(residual, up_half, ((1,), (1,))).astype(BF16)
        up_delta = up_delta - rate * dot(hidden, residual, ((0,), (0,)))
        last = step == STEPS - 1
        if not last:
            up_half = (up + up_delta).astype(BF16)
            hidden_ref[...] = jnp.zeros_like(hidden_ref)

        def down_block(at, unused):
            lanes = pl.ds(pl.multiple_of(at * block, block), block)
            moved = -rate * dot(back, x_ref[:, lanes], ((0,), (0,)))
            if step:
                moved = moved + delta_ref[:, lanes]
            delta_ref[:, lanes] = moved
            if not last:
                half_down = (down_ref[:, lanes].astype(F32) + moved).astype(BF16)
                hidden_ref[...] += dot(x_ref[:, lanes], half_down, ((1,), (1,)))
                return unused
            square = moved * moved
            for at in range(0, block, LANES):
                unused = unused + square[:, at : at + LANES]
            return unused

        squares = lax.fori_loop(
            0, width // block, down_block, jnp.zeros((rank, LANES), F32), unroll=2
        )

    total = jnp.sum(squares) + jnp.sum(up_delta * up_delta) + EPSILON
    total = jnp.full((1, LANES), total, F32)
    factor = jnp.minimum(1.0, clip_ref[0] / jnp.sqrt(total))[:, :1]
    share = width // devices
    up_share = kv_width // devices
    up_turned = (factor * up_delta).T
    pieces = share // rank
    tall = up_share // pieces

    def write(core, target):
        for pair in range(groups_of // 2):
            for member in range(members):
                device = (2 * pair + core) * members + member
                spot = lax.bitwise_xor(lax.div(lax.axis_index("grp"), 2), pair)
                place = lax.bitwise_xor(lax.axis_index("fsdp"), member)
                moved = delta_ref[:, device * share : (device + 1) * share]
                target[spot, place, :rank, :] = factor * moved
                first = device * up_share
                parts = [
                    up_turned[first + at * tall : first + (at + 1) * tall] for at in range(pieces)
                ]
                target[spot, place, rank:, :] = (
                    jnp.concatenate(parts, axis=1) if pieces > 1 else parts[0]
                )

    for core in range(2):
        mine = side == core

        @pl.when(mine)
        def _():
            write(core, keep_ref)

        @pl.when(jnp.logical_not(mine))
        def _():
            write(core, send_ref)


def exchange(blocks, partner_of):
    devices = lax.axis_size("grp") * lax.axis_size("fsdp")
    total = blocks[0]
    for place in range(1, len(blocks)):
        pairs = [(at, partner_of(at, place)) for at in range(devices)]
        total = total + lax.ppermute(blocks[place], BOTH, pairs)
    return total


def body(
    tokens,
    targets,
    row_owner_user,
    device_row_count,
    user_row_cap,
    value_weight,
    adapter_down,
    adapter_up,
    clip_norm_bound,
    down_noise,
    up_noise,
):
    groups, members = (lax.axis_size("grp"), lax.axis_size("fsdp"))
    devices = groups * members
    side = lax.axis_index("grp") % 2
    per_dev, width = tokens.shape
    kv_width = targets.shape[1]
    rank = adapter_down.shape[1]
    users = user_row_cap.shape[0]
    most = 3 * per_dev // (2 * devices)
    slots = devices * most
    whole = devices * SUB
    whole_groups, rest = divmod(most, SUB)
    smem = pl.BlockSpec(memory_space=pltpu.SMEM)
    vmem = pl.BlockSpec(memory_space=pltpu.VMEM)
    anywhere = pl.BlockSpec(memory_space=pl.ANY)

    half = value_weight.shape[0] // 2
    piece = kv_width // (groups // 2)
    pair = lax.axis_index("grp") // 2
    mine = lax.dynamic_slice(value_weight, (side * half, pair * piece), (half, piece))
    near = lax.all_gather(mine, BOTH, axis=0, axis_index_groups=weight_rings(groups, members))
    swap = [(at, at ^ 1) for at in range(groups)]
    far = lax.ppermute(near, "grp", swap)

    columns = whole_groups * (width + kv_width) + rest * (width + kv_width) // SUB + LANES
    packed = pl.pallas_call(
        lambda *refs: pack_kernel(users, most, *refs),
        out_shape=jax.ShapeDtypeStruct((users * SUB, columns), BF16),
        in_specs=[smem, vmem, vmem, vmem],
        out_specs=vmem,
        compiler_params=pltpu.CompilerParams(vmem_limit_bytes=VMEM_BYTES),
        name="pack_rows",
    )(device_row_count, row_owner_user.reshape(1, per_dev), tokens, targets)
    got = lax.all_to_all(
        packed.reshape(users, SUB, columns), BOTH, split_axis=0, concat_axis=0, tiled=True
    ).reshape(whole, columns)
    share = width // devices
    tall = rank + kv_width // devices * rank // share
    down = adapter_down.T
    rows, near_frozen, near_hidden = pl.pallas_call(
        lambda *refs: near_kernel(groups, members, most, *refs),
        out_shape=[
            jax.ShapeDtypeStruct((slots, width), BF16),
            jax.ShapeDtypeStruct((slots, kv_width), F32),
            jax.ShapeDtypeStruct((slots, rank), F32),
        ],
        in_specs=[anywhere, anywhere, vmem],
        out_specs=[anywhere, vmem, vmem],
        scratch_shapes=[
            pltpu.VMEM((slots, width), BF16),
            pltpu.VMEM((max(rest, 1), whole, width // SUB), BF16),
            pltpu.VMEM((members, half, kv_width), BF16),
            pltpu.SemaphoreType.DMA((whole_groups + rest,)),
            pltpu.SemaphoreType.DMA,
            pltpu.SemaphoreType.DMA((members, groups // 2)),
        ],
        compiler_params=pltpu.CompilerParams(vmem_limit_bytes=VMEM_BYTES),
        cost_estimate=pl.CostEstimate(
            flops=slots * width * kv_width, bytes_accessed=3 * 10**7, transcendentals=0
        ),
        name="near_product",
    )(got, near, down)

    package = jax.ShapeDtypeStruct((groups // 2, members, tall, share), F32)
    keep, send = pl.pallas_call(
        lambda *refs: user_kernel(groups, members, most, *refs),
        out_shape=[package] * 2,
        in_specs=[smem, smem, anywhere, anywhere, vmem, vmem, anywhere, vmem, vmem],
        out_specs=[vmem] * 2,
        scratch_shapes=[
            pltpu.VMEM((slots, width), BF16),
            pltpu.VMEM((slots, kv_width), BF16),
            pltpu.VMEM((max(rest, 1), whole, kv_width // SUB), BF16),
            pltpu.VMEM((whole, LANES), BF16),
            pltpu.VMEM((members, half, kv_width), BF16),
            pltpu.VMEM((slots, kv_width), F32),
            pltpu.VMEM((slots, rank), F32),
            pltpu.VMEM((rank, width), F32),
            pltpu.SemaphoreType.DMA((whole_groups + rest + 2,)),
            pltpu.SemaphoreType.DMA((members, groups // 2)),
        ],
        compiler_params=pltpu.CompilerParams(vmem_limit_bytes=VMEM_BYTES),
        name="user_steps",
    )(user_row_cap, clip_norm_bound, got, rows, near_frozen, near_hidden, far, down, adapter_up)

    other = lax.ppermute(send, "grp", swap)
    keep = keep.reshape(groups // 2, members // 2, 2, tall, share)
    other = other.reshape(keep.shape)
    square = [(pair, inner) for pair in range(groups // 2) for inner in range(2)]

    def in_square(at, place):
        pair, inner = square[place]
        return at ^ (2 * pair * members) ^ inner

    package = exchange(
        [keep[pair, :, inner] + other[pair, :, inner] for pair, inner in square], in_square
    )
    package = exchange(
        [package[place] for place in range(members // 2)], lambda at, place: at ^ (2 * place)
    )
    clip = clip_norm_bound[0]
    update_a = package[:rank].T + clip * down_noise
    pieces = share // rank
    up_sum = package[rank:].reshape(tall - rank, pieces, rank).transpose(1, 0, 2)
    update_b = up_sum.reshape(kv_width // devices, rank).T + clip * up_noise
    return (update_a, update_b)


def solution(mesh):
    in_specs = (
        P(BOTH, None),
        P(BOTH, None),
        P(BOTH, None),
        P(BOTH),
        P(),
        P("fsdp", None),
        P(),
        P(),
        P(),
        P(BOTH, None),
        P(None, BOTH),
    )
    out_specs = (P(BOTH, None), P(None, BOTH))
    return jax.shard_map(body, mesh=mesh, in_specs=in_specs, out_specs=out_specs, check_vma=False)
```

```python
import jax
import jax.numpy as jnp
from jax import lax
from jax.experimental import pallas as pl
from jax.experimental.pallas import tpu as pltpu
from jax.sharding import PartitionSpec as P

STEPS = 2
ADAPTER_SCALE = 2.0
LEARN_RATE = 0.05
EPSILON = 1e-06

SUB = 8
LANES = 128
BOTH = ("grp", "fsdp")
VMEM_BYTES = 56 * 1024 * 1024

F32 = jnp.float32
BF16 = jnp.bfloat16


def dot(left, right, contract=((1,), (0,))):
    return lax.dot_general(left, right, (contract, ((), ())), preferred_element_type=F32)


def iota(shape, axis):
    return lax.broadcasted_iota(jnp.int32, shape, axis)


def pack_kernel(
    users, most, count_ref, owner_ref, tokens_ref, targets_ref, out_ref, rows_ref, goals_ref,
    packed_ref, in_sem, out_sem,
):
    rows = tokens_ref.shape[0]
    groups, rest = divmod(most, SUB)
    chunks = [
        (source, held, source.shape[1] // SUB, part)
        for source, held in ((tokens_ref, rows_ref), (targets_ref, goals_ref))
        for part in range(SUB)
    ]
    loads = []
    for place, (source, held, piece, part) in enumerate(chunks):
        lanes = pl.ds(part * piece, piece)
        copy = pltpu.make_async_copy(source.at[:, lanes], held.at[:, lanes], in_sem.at[place])
        copy.start()
        loads.append(copy)
    owner_row = owner_ref[...]
    first, second = (iota((rows, rows), 0), iota((rows, rows), 1))
    owner = jnp.sum(jnp.where(first == second, owner_row, 0), axis=1, keepdims=True)
    same = (owner == owner_row) & (first < second)
    rank = jnp.sum(same.astype(jnp.int32), axis=0, keepdims=True)
    line = iota((users * SUB, rows), 0)
    mine = line // SUB == owner_row
    slot = line % SUB
    stores = []

    def store(first, size):
        lanes = pl.ds(first, size)
        copy = pltpu.make_async_copy(
            packed_ref.at[:, lanes], out_ref.at[:, lanes], out_sem.at[len(stores)]
        )
        copy.start()
        stores.append(copy)

    column = 0
    place = 0
    for source in (rows_ref, goals_ref):
        width = source.shape[1]
        piece = width // SUB
        totals = [None] * rest
        for part in range(SUB):
            loads[place].wait()
            place += 1
            values = source[:, part * piece : (part + 1) * piece]
            for group in range(groups):
                pick = (mine & (rank == slot + group * SUB)).astype(BF16)
                spot = column + group * width + part * piece
                packed_ref[:, spot : spot + piece] = dot(pick, values).astype(BF16)
                store(spot, piece)
            for extra in range(rest):
                here = mine & (rank == groups * SUB + extra)
                term = dot((here & (slot == part)).astype(BF16), values)
                totals[extra] = term if totals[extra] is None else totals[extra] + term
        column += groups * width
        for total in totals:
            packed_ref[:, column : column + piece] = total.astype(BF16)
            store(column, piece)
            column += piece
    used = mine & (iota((users * SUB, rows), 1) < count_ref[0])
    number = jnp.sum(used.astype(F32), axis=1, keepdims=True)
    packed_ref[:, column : column + LANES] = jnp.broadcast_to(
        number, (users * SUB, LANES)
    ).astype(BF16)
    store(column, LANES)
    for copy in stores:
        copy.wait()


def weight_rings(groups, members):
    round_trip = [(at, 0) for at in range(groups // 2)]
    round_trip += [(at, 1) for at in reversed(range(groups // 2))]
    length, layers = (len(round_trip), members // 2)
    rings = []
    for core in range(2):
        up, down = ([], [])
        low, high = (list(range(length // 2)), list(range(length // 2, length)))
        for layer in range(1, layers):
            turned = layer % 2 == 0
            up += [(layer, at) for at in (low[::-1] if turned else low)]
            down += [(layer, at) for at in (high if turned else high[::-1])]
        path = [(0, at) for at in reversed(range(length))] + up + down[::-1]
        ring = []
        for layer, at in path:
            pair, inner = round_trip[(at + core * length // 2) % length]
            ring.append((2 * pair + core) * members + 2 * layer + inner)
        rings.append(ring)
    return rings


def weight_copies(ring_of, groups, members, source, target, sems):
    pairs = groups // 2
    columns = source.shape[2]
    side = lax.rem(lax.axis_index("grp"), 2)
    rings = weight_rings(groups, members)

    def copy(member, pair):
        spots = [ring.index((2 * pair + core) * members + member) for core, ring in enumerate(rings)]
        spot = jnp.where(side == ring_of, spots[0], spots[1])
        return pltpu.make_async_copy(
            source.at[spot],
            target.at[member, :, pl.ds(pair * columns, columns)],
            sems.at[member, pair],
        )

    return [[copy(member, pair) for pair in range(pairs)] for member in range(members)]


def wait_block(target, place, pairs, sems):
    columns = target.shape[2] // pairs
    for pair in range(pairs):
        block = target.at[place, :, pl.ds(pair * columns, columns)]
        pltpu.make_async_copy(block, block, sems.at[place, pair]).wait()


def rows_kernel(
    devices, most, got_ref, down_ref, x_out_ref, hidden_ref, x_ref, cut_ref, got_sem, out_sem
):
    groups, rest = divmod(most, SUB)
    width = x_ref.shape[1]
    whole = devices * SUB
    copies = []
    column = 0
    for group in range(groups):
        copies.append(
            (got_ref.at[:, pl.ds(column, width)], x_ref.at[pl.ds(group * whole, whole), :])
        )
        column += width
    for extra in range(rest):
        copies.append((got_ref.at[:, pl.ds(column, width // SUB)], cut_ref.at[extra]))
        column += width // SUB
    copies = [
        pltpu.make_async_copy(source, target, got_sem.at[place])
        for place, (source, target) in enumerate(copies)
    ]
    for copy in copies:
        copy.start()
    for copy in copies:
        copy.wait()
    join_pieces(devices, groups * whole, rest, x_ref, cut_ref)
    out = pltpu.make_async_copy(x_ref, x_out_ref, out_sem)
    out.start()
    hidden_ref[...] = jnp.zeros_like(hidden_ref)
    block = min(width, 1024)

    def add_block(at, unused):
        lanes = pl.ds(pl.multiple_of(at * block, block), block)
        hidden_ref[...] += dot(x_ref[:, lanes], down_ref[:, lanes], ((1,), (1,)))
        return unused

    lax.fori_loop(0, width // block, add_block, 0, unroll=4)
    out.wait()


def near_kernel(groups_of, members, rows_ref, near_ref, frozen_ref, x_ref, w_ref, x_sem, w_sem):
    half = w_ref.shape[1]
    side = lax.rem(lax.axis_index("grp"), 2)
    weights = weight_copies(0, groups_of, members, near_ref, w_ref, w_sem)

    def row_copy(shard):
        lanes = pl.ds(pl.multiple_of((2 * shard + side) * half, half), half)
        return pltpu.make_async_copy(rows_ref.at[:, lanes], x_ref.at[:, lanes], x_sem.at[shard])

    for shard, copies in enumerate(weights):
        row_copy(shard).start()
        for copy in copies:
            copy.start()
    frozen_ref[...] = jnp.zeros_like(frozen_ref)

    def add_shard(shard, unused):
        row_copy(shard).wait()
        wait_block(w_ref, shard, groups_of // 2, w_sem)
        near = pl.ds(pl.multiple_of((2 * shard + side) * half, half), half)
        frozen_ref[...] += dot(x_ref[:, near], w_ref[shard])
        return unused

    lax.fori_loop(0, members, add_shard, 0, unroll=4)


def join_pieces(devices, bottom, rest, full, cut):
    line, other = (iota((devices, devices * SUB), 0), iota((devices, devices * SUB), 1))
    piece = full.shape[1] // SUB
    for extra in range(rest):
        first = bottom + extra * devices
        for part in range(SUB):
            pick = (other == line * SUB + part).astype(BF16)
            full[first : first + devices, part * piece : (part + 1) * piece] = dot(
                pick, cut[extra]
            ).astype(BF16)


def user_kernel(
    groups_of,
    members,
    most,
    cap_ref,
    clip_ref,
    got_ref,
    rows_ref,
    near_frozen_ref,
    near_hidden_ref,
    far_ref,
    down_ref,
    up_ref,
    *refs,
):
    keep_ref, send_ref = refs[:2]
    (
        x_ref,
        goal_ref,
        cut_goal_ref,
        used_ref,
        w_ref,
        frozen_ref,
        hidden_ref,
        delta_ref,
        got_sem,
        w_sem,
    ) = refs[2:]
    groups, rest = divmod(most, SUB)
    devices = groups_of * members
    rank, width = down_ref.shape
    kv_width = up_ref.shape[1]
    whole = devices * SUB
    half = w_ref.shape[1]
    copies = [(rows_ref, x_ref)]
    column = groups * width + rest * width // SUB
    for group in range(groups):
        copies.append(
            (got_ref.at[:, pl.ds(column, kv_width)], goal_ref.at[pl.ds(group * whole, whole), :])
        )
        column += kv_width
    for extra in range(rest):
        copies.append((got_ref.at[:, pl.ds(column, kv_width // SUB)], cut_goal_ref.at[extra]))
        column += kv_width // SUB
    copies.append((got_ref.at[:, pl.ds(column, LANES)], used_ref))
    copies = [
        pltpu.make_async_copy(source, target, got_sem.at[place])
        for place, (source, target) in enumerate(copies)
    ]
    for copy in copies[1:] + copies[:1]:
        copy.start()
    for pieces in weight_copies(1, groups_of, members, far_ref, w_ref, w_sem):
        for copy in pieces:
            copy.start()
    for copy in copies[1:]:
        copy.wait()
    join_pieces(devices, groups * whole, rest, goal_ref, cut_goal_ref)

    cap = cap_ref[lax.axis_index("grp") * members + lax.axis_index("fsdp")].astype(F32)
    used = used_ref[...]
    pieces = []
    if groups:
        line, other = (iota((whole, whole), 0), iota((whole, whole), 1))
        earlier = dot(((other // SUB < line // SUB) & (other % SUB == 0)).astype(BF16), used)
        own = used.astype(F32)
        for group in range(groups):
            spot = (iota((whole, LANES), 0) % SUB + group * SUB).astype(F32)
            live = (spot < own) & (earlier + spot < cap)
            pieces.append(jnp.where(live, 1.0 / cap, 0.0)[:, :1])
    line, other = (iota((devices, whole), 0), iota((devices, whole), 1))
    earlier = dot((other < line * SUB).astype(BF16) * (other % SUB == 0).astype(BF16), used)
    own = dot((other == line * SUB).astype(BF16), used)
    for extra in range(rest):
        spot = float(groups * SUB + extra)
        live = (own > spot) & (earlier + spot < cap)
        pieces.append(jnp.where(live, 1.0 / cap, 0.0)[:, :1])
    scale = jnp.concatenate(pieces, axis=0) if len(pieces) > 1 else pieces[0]

    frozen_ref[...] = near_frozen_ref[...]
    hidden_ref[...] = near_hidden_ref[...]
    side = lax.rem(lax.axis_index("grp"), 2)
    copies[0].wait()

    def add_shard(shard, unused):
        wait_block(w_ref, shard, groups_of // 2, w_sem)
        far = pl.ds(pl.multiple_of((2 * shard + 1 - side) * half, half), half)
        frozen_ref[...] += dot(x_ref[:, far], w_ref[shard])
        return unused

    lax.fori_loop(0, members, add_shard, 0, unroll=4)

    rate = ADAPTER_SCALE * LEARN_RATE
    block = min(width, 1024)
    up = up_ref[...].astype(F32)
    up_half = up_ref[...]
    up_delta = jnp.zeros((rank, kv_width), F32)
    for step in range(STEPS):
        hidden = hidden_ref[...].astype(BF16)
        error = frozen_ref[...] + ADAPTER_SCALE * dot(hidden, up_half) - goal_ref[...].astype(F32)
        residual = (scale * error).astype(BF16)
        back = dot(residual, up_half, ((1,), (1,))).astype(BF16)
        up_delta = up_delta - rate * dot(hidden, residual, ((0,), (0,)))
        last = step == STEPS - 1
        if not last:
            up_half = (up + up_delta).astype(BF16)
            hidden_ref[...] = jnp.zeros_like(hidden_ref)

        def down_block(at, unused):
            lanes = pl.ds(pl.multiple_of(at * block, block), block)
            moved = -rate * dot(back, x_ref[:, lanes], ((0,), (0,)))
            if step:
                moved = moved + delta_ref[:, lanes]
            delta_ref[:, lanes] = moved
            if not last:
                half_down = (down_ref[:, lanes].astype(F32) + moved).astype(BF16)
                hidden_ref[...] += dot(x_ref[:, lanes], half_down, ((1,), (1,)))
                return unused
            square = moved * moved
            for at in range(0, block, LANES):
                unused = unused + square[:, at : at + LANES]
            return unused

        squares = lax.fori_loop(
            0, width // block, down_block, jnp.zeros((rank, LANES), F32), unroll=4
        )

    total = jnp.sum(squares) + jnp.sum(up_delta * up_delta) + EPSILON
    total = jnp.full((1, LANES), total, F32)
    factor = jnp.minimum(1.0, clip_ref[0] / jnp.sqrt(total))[:, :1]
    share = width // devices
    up_share = kv_width // devices
    up_turned = (factor * up_delta).T
    pieces = share // rank
    tall = up_share // pieces

    def write(core, target):
        for pair in range(groups_of // 2):
            for member in range(members):
                device = (2 * pair + core) * members + member
                spot = lax.bitwise_xor(lax.div(lax.axis_index("grp"), 2), pair)
                place = lax.bitwise_xor(lax.axis_index("fsdp"), member)
                moved = delta_ref[:, device * share : (device + 1) * share]
                target[spot, place, :rank, :] = factor * moved
                first = device * up_share
                parts = [
                    up_turned[first + at * tall : first + (at + 1) * tall] for at in range(pieces)
                ]
                target[spot, place, rank:, :] = (
                    jnp.concatenate(parts, axis=1) if pieces > 1 else parts[0]
                )

    for core in range(2):
        mine = side == core

        @pl.when(mine)
        def _():
            write(core, keep_ref)

        @pl.when(jnp.logical_not(mine))
        def _():
            write(core, send_ref)


def exchange(blocks, partner_of):
    devices = lax.axis_size("grp") * lax.axis_size("fsdp")
    total = blocks[0]
    for place in range(1, len(blocks)):
        pairs = [(at, partner_of(at, place)) for at in range(devices)]
        total = total + lax.ppermute(blocks[place], BOTH, pairs)
    return total


def body(
    tokens,
    targets,
    row_owner_user,
    device_row_count,
    user_row_cap,
    value_weight,
    adapter_down,
    adapter_up,
    clip_norm_bound,
    down_noise,
    up_noise,
):
    groups, members = (lax.axis_size("grp"), lax.axis_size("fsdp"))
    devices = groups * members
    side = lax.axis_index("grp") % 2
    per_dev, width = tokens.shape
    kv_width = targets.shape[1]
    rank = adapter_down.shape[1]
    users = user_row_cap.shape[0]
    most = 3 * per_dev // (2 * devices)
    slots = devices * most
    whole = devices * SUB
    whole_groups, rest = divmod(most, SUB)
    smem = pl.BlockSpec(memory_space=pltpu.SMEM)
    vmem = pl.BlockSpec(memory_space=pltpu.VMEM)
    anywhere = pl.BlockSpec(memory_space=pl.ANY)

    params = pltpu.CompilerParams(vmem_limit_bytes=VMEM_BYTES)
    half = value_weight.shape[0] // 2
    piece = kv_width // (groups // 2)
    pair = lax.axis_index("grp") // 2
    mine = lax.dynamic_slice(value_weight, (side * half, pair * piece), (half, piece))
    near = lax.all_gather(mine, BOTH, axis=0, axis_index_groups=weight_rings(groups, members))
    swap = [(at, at ^ 1) for at in range(groups)]
    far = lax.ppermute(near, "grp", swap)

    columns = whole_groups * (width + kv_width) + rest * (width + kv_width) // SUB + LANES
    packed = pl.pallas_call(
        lambda *refs: pack_kernel(users, most, *refs),
        out_shape=jax.ShapeDtypeStruct((users * SUB, columns), BF16),
        in_specs=[smem, vmem, anywhere, anywhere],
        out_specs=anywhere,
        scratch_shapes=[
            pltpu.VMEM((per_dev, width), BF16),
            pltpu.VMEM((per_dev, kv_width), BF16),
            pltpu.VMEM((users * SUB, columns), BF16),
            pltpu.SemaphoreType.DMA((2 * SUB,)),
            pltpu.SemaphoreType.DMA((2 * (SUB * whole_groups + rest) + 1,)),
        ],
        compiler_params=params,
        name="pack_rows",
    )(device_row_count, row_owner_user.reshape(1, per_dev), tokens, targets)
    got = lax.all_to_all(
        packed.reshape(users, SUB, columns), BOTH, split_axis=0, concat_axis=0, tiled=True
    ).reshape(whole, columns)
    share = width // devices
    tall = rank + kv_width // devices * rank // share
    down = adapter_down.T
    rows, hidden = pl.pallas_call(
        lambda *refs: rows_kernel(devices, most, *refs),
        out_shape=[
            jax.ShapeDtypeStruct((slots, width), BF16),
            jax.ShapeDtypeStruct((slots, rank), F32),
        ],
        in_specs=[anywhere, vmem],
        out_specs=[anywhere, vmem],
        scratch_shapes=[
            pltpu.VMEM((slots, width), BF16),
            pltpu.VMEM((max(rest, 1), whole, width // SUB), BF16),
            pltpu.SemaphoreType.DMA((whole_groups + rest,)),
            pltpu.SemaphoreType.DMA,
        ],
        compiler_params=params,
        name="join_rows",
    )(got, down)
    near_frozen = pl.pallas_call(
        lambda *refs: near_kernel(groups, members, *refs),
        out_shape=jax.ShapeDtypeStruct((slots, kv_width), F32),
        in_specs=[anywhere, anywhere],
        out_specs=vmem,
        scratch_shapes=[
            pltpu.VMEM((slots, width), BF16),
            pltpu.VMEM((members, half, kv_width), BF16),
            pltpu.SemaphoreType.DMA((members,)),
            pltpu.SemaphoreType.DMA((members, groups // 2)),
        ],
        compiler_params=params,
        cost_estimate=pl.CostEstimate(
            flops=slots * width * kv_width, bytes_accessed=3 * 10**7, transcendentals=0
        ),
        name="near_product",
    )(rows, near)

    package = jax.ShapeDtypeStruct((groups // 2, members, tall, share), F32)
    keep, send = pl.pallas_call(
        lambda *refs: user_kernel(groups, members, most, *refs),
        out_shape=[package] * 2,
        in_specs=[smem, smem, anywhere, anywhere, vmem, vmem, anywhere, vmem, vmem],
        out_specs=[vmem] * 2,
        scratch_shapes=[
            pltpu.VMEM((slots, width), BF16),
            pltpu.VMEM((slots, kv_width), BF16),
            pltpu.VMEM((max(rest, 1), whole, kv_width // SUB), BF16),
            pltpu.VMEM((whole, LANES), BF16),
            pltpu.VMEM((members, half, kv_width), BF16),
            pltpu.VMEM((slots, kv_width), F32),
            pltpu.VMEM((slots, rank), F32),
            pltpu.VMEM((rank, width), F32),
            pltpu.SemaphoreType.DMA((whole_groups + rest + 2,)),
            pltpu.SemaphoreType.DMA((members, groups // 2)),
        ],
        compiler_params=params,
        name="user_steps",
    )(user_row_cap, clip_norm_bound, got, rows, near_frozen, hidden, far, down, adapter_up)

    other = lax.ppermute(send, "grp", swap)
    keep = keep.reshape(groups // 2, members // 2, 2, tall, share)
    other = other.reshape(keep.shape)
    square = [(pair, inner) for pair in range(groups // 2) for inner in range(2)]

    def in_square(at, place):
        pair, inner = square[place]
        return at ^ (2 * pair * members) ^ inner

    package = exchange(
        [keep[pair, :, inner] + other[pair, :, inner] for pair, inner in square], in_square
    )
    package = exchange(
        [package[place] for place in range(members // 2)], lambda at, place: at ^ (2 * place)
    )
    clip = clip_norm_bound[0]
    update_a = package[:rank].T + clip * down_noise
    pieces = share // rank
    up_sum = package[rank:].reshape(tall - rank, pieces, rank).transpose(1, 0, 2)
    update_b = up_sum.reshape(kv_width // devices, rank).T + clip * up_noise
    return (update_a, update_b)


def solution(mesh):
    in_specs = (
        P(BOTH, None),
        P(BOTH, None),
        P(BOTH, None),
        P(BOTH),
        P(),
        P("fsdp", None),
        P(),
        P(),
        P(),
        P(BOTH, None),
        P(None, BOTH),
    )
    out_specs = (P(BOTH, None), P(None, BOTH))
    return jax.shard_map(body, mesh=mesh, in_specs=in_specs, out_specs=out_specs, check_vma=False)
```

```python
import jax
import jax.numpy as jnp
from jax import lax
from jax.experimental import pallas as pl
from jax.experimental.pallas import tpu as pltpu
from jax.sharding import PartitionSpec as P

STEPS = 2
ADAPTER_SCALE = 2.0
LEARN_RATE = 0.05
EPSILON = 1e-06

SUB = 8
LANES = 128
BOTH = ("grp", "fsdp")
VMEM_BYTES = 56 * 1024 * 1024

F32 = jnp.float32
BF16 = jnp.bfloat16


def dot(left, right, contract=((1,), (0,))):
    return lax.dot_general(left, right, (contract, ((), ())), preferred_element_type=F32)


def iota(shape, axis):
    return lax.broadcasted_iota(jnp.int32, shape, axis)


def pack_kernel(users, most, part_of, with_goals, count_ref, owner_ref, *refs):
    tokens_ref, targets_ref, out_ref, rows_ref, sems = refs
    rows, size = rows_ref.shape
    block = size // sems.shape[0]
    loads = []
    for place in range(sems.shape[0]):
        copy = pltpu.make_async_copy(
            tokens_ref.at[:, pl.ds((2 * place + part_of) * block, block)],
            rows_ref.at[:, pl.ds(place * block, block)],
            sems.at[place],
        )
        copy.start()
        loads.append(copy)
    groups, rest = divmod(most, SUB)
    owner_row = owner_ref[...]
    first, second = (iota((rows, rows), 0), iota((rows, rows), 1))
    owner = jnp.sum(jnp.where(first == second, owner_row, 0), axis=1, keepdims=True)
    same = (owner == owner_row) & (first < second)
    rank = jnp.sum(same.astype(jnp.int32), axis=0, keepdims=True)
    line = iota((users * SUB, rows), 0)
    mine = line // SUB == owner_row
    slot = line % SUB
    whole_picks = [
        (mine & (rank == slot + group * SUB)).astype(BF16) for group in range(groups)
    ]
    rest_picks = [
        [(mine & (rank == groups * SUB + extra) & (slot == part)).astype(BF16) for part in range(SUB)]
        for extra in range(rest)
    ]
    for copy in loads:
        copy.wait()
    column = 0
    for source in (rows_ref, targets_ref) if with_goals else (rows_ref,):
        width = source.shape[1]
        piece = width // SUB
        totals = [None] * rest
        for part in range(SUB):
            values = source[:, part * piece : (part + 1) * piece]
            for group in range(groups):
                spot = column + group * width + part * piece
                out_ref[:, spot : spot + piece] = dot(whole_picks[group], values).astype(BF16)
            for extra in range(rest):
                term = dot(rest_picks[extra][part], values)
                totals[extra] = term if totals[extra] is None else totals[extra] + term
        column += groups * width
        for total in totals:
            out_ref[:, column : column + piece] = total.astype(BF16)
            column += piece
    if with_goals:
        used = mine & (iota((users * SUB, rows), 1) < count_ref[0])
        number = jnp.sum(used.astype(F32), axis=1, keepdims=True)
        out_ref[:, column : column + LANES] = jnp.broadcast_to(
            number, (users * SUB, LANES)
        ).astype(BF16)


def weight_rings(groups, members):
    round_trip = [(at, 0) for at in range(groups // 2)]
    round_trip += [(at, 1) for at in reversed(range(groups // 2))]
    length, layers = (len(round_trip), members // 2)
    rings = []
    for core in range(2):
        up, down = ([], [])
        low, high = (list(range(length // 2)), list(range(length // 2, length)))
        for layer in range(1, layers):
            turned = layer % 2 == 0
            up += [(layer, at) for at in (low[::-1] if turned else low)]
            down += [(layer, at) for at in (high if turned else high[::-1])]
        path = [(0, at) for at in reversed(range(length))] + up + down[::-1]
        ring = []
        for layer, at in path:
            pair, inner = round_trip[(at + core * length // 2) % length]
            ring.append((2 * pair + core) * members + 2 * layer + inner)
        rings.append(ring)
    return rings


def weight_copies(ring_of, groups, members, source, target, sems, first=0):
    pairs = groups // 2
    depth, columns = source.shape[1:]
    side = lax.rem(lax.axis_index("grp"), 2)
    rings = weight_rings(groups, members)

    def copy(member, pair):
        spots = [ring.index((2 * pair + core) * members + member) for core, ring in enumerate(rings)]
        spot = jnp.where(side == ring_of, spots[0], spots[1])
        return pltpu.make_async_copy(
            source.at[spot],
            target.at[member, pl.ds(first, depth), pl.ds(pair * columns, columns)],
            sems.at[member, pair],
        )

    return [[copy(member, pair) for pair in range(pairs)] for member in range(members)]


def wait_block(target, pairs, sems):
    columns = target.shape[1] // pairs
    for pair in range(pairs):
        block = target.at[:, pl.ds(pair * columns, columns)]
        pltpu.make_async_copy(block, block, sems.at[pair]).wait()


def rows_kernel(
    devices, most, got_ref, down_ref, x_out_ref, hidden_ref, x_ref, cut_ref, got_sem, out_sem
):
    groups, rest = divmod(most, SUB)
    width = x_ref.shape[1]
    whole = devices * SUB
    copies = []
    column = 0
    for group in range(groups):
        copies.append(
            (got_ref.at[:, pl.ds(column, width)], x_ref.at[pl.ds(group * whole, whole), :])
        )
        column += width
    for extra in range(rest):
        copies.append((got_ref.at[:, pl.ds(column, width // SUB)], cut_ref.at[extra]))
        column += width // SUB
    copies = [
        pltpu.make_async_copy(source, target, got_sem.at[place])
        for place, (source, target) in enumerate(copies)
    ]
    for copy in copies:
        copy.start()
    for copy in copies:
        copy.wait()
    join_pieces(devices, groups * whole, rest, x_ref, cut_ref)
    out = pltpu.make_async_copy(x_ref, x_out_ref, out_sem)
    out.start()
    hidden_ref[...] = jnp.zeros_like(hidden_ref)
    block = min(width, 1024)

    def add_block(at, unused):
        lanes = pl.ds(pl.multiple_of(at * block, block), block)
        hidden_ref[...] += dot(x_ref[:, lanes], down_ref[:, lanes], ((1,), (1,)))
        return unused

    lax.fori_loop(0, width // block, add_block, 0, unroll=4)
    out.wait()


def near_kernel(groups_of, members, *refs):
    *before, rows_ref, near_ref, frozen_ref, x_ref, w_ref, x_sem, w_sem = refs
    depth = w_ref.shape[1]
    side = lax.rem(lax.axis_index("grp"), 2)
    weights = weight_copies(0, groups_of, members, near_ref, w_ref, w_sem)

    def near(shard):
        return pl.ds(pl.multiple_of((2 * shard + side) * depth, depth), depth)

    def row_copy(shard):
        lanes = near(shard)
        return pltpu.make_async_copy(rows_ref.at[:, lanes], x_ref.at[:, lanes], x_sem.at[shard])

    for shard, copies in enumerate(weights):
        row_copy(shard).start()
        for copy in copies:
            copy.start()
    frozen_ref[...] = before[0][...] if before else jnp.zeros_like(frozen_ref)

    def add_shards(pair, unused):
        total = None
        for shard in (2 * pair, 2 * pair + 1):
            row_copy(shard).wait()
            wait_block(w_ref.at[shard], groups_of // 2, w_sem.at[shard])
            term = dot(x_ref[:, near(shard)], w_ref[shard])
            total = term if total is None else total + term
        frozen_ref[...] += total
        return unused

    lax.fori_loop(0, members // 2, add_shards, 0, unroll=2)


def join_pieces(devices, bottom, rest, full, cut):
    line, other = (iota((devices, devices * SUB), 0), iota((devices, devices * SUB), 1))
    piece = full.shape[1] // SUB
    for extra in range(rest):
        first = bottom + extra * devices
        for part in range(SUB):
            pick = (other == line * SUB + part).astype(BF16)
            full[first : first + devices, part * piece : (part + 1) * piece] = dot(
                pick, cut[extra]
            ).astype(BF16)


def user_kernel(
    groups_of,
    members,
    most,
    cap_ref,
    clip_ref,
    got_ref,
    rows_refs,
    near_frozen_ref,
    hidden_refs,
    far_refs,
    down_ref,
    up_ref,
    *refs,
):
    keep_ref, send_ref = refs[:2]
    (
        x_ref,
        goal_ref,
        cut_goal_ref,
        used_ref,
        w_ref,
        frozen_ref,
        hidden_ref,
        delta_ref,
        got_sem,
        w_sem,
    ) = refs[2:]
    groups, rest = divmod(most, SUB)
    devices = groups_of * members
    rank, width = down_ref.shape
    kv_width = up_ref.shape[1]
    whole = devices * SUB
    half = w_ref.shape[1]
    depth = half // 2
    size = width // 2
    copies = [
        (source, x_ref.at[:, pl.ds(place * size, size)]) for place, source in enumerate(rows_refs)
    ]
    column = groups * size + rest * size // SUB
    for group in range(groups):
        copies.append(
            (got_ref.at[:, pl.ds(column, kv_width)], goal_ref.at[pl.ds(group * whole, whole), :])
        )
        column += kv_width
    for extra in range(rest):
        copies.append((got_ref.at[:, pl.ds(column, kv_width // SUB)], cut_goal_ref.at[extra]))
        column += kv_width // SUB
    copies.append((got_ref.at[:, pl.ds(column, LANES)], used_ref))
    copies = [
        pltpu.make_async_copy(source, target, got_sem.at[place])
        for place, (source, target) in enumerate(copies)
    ]
    for copy in copies[2:] + copies[:2]:
        copy.start()
    weights = [
        weight_copies(1, groups_of, members, far, w_ref, w_sem.at[place], place * depth)
        for place, far in enumerate(far_refs)
    ]
    for shard in range(members):
        for copy in weights[0][shard] + weights[1][shard]:
            copy.start()
    for copy in copies[2:]:
        copy.wait()
    join_pieces(devices, groups * whole, rest, goal_ref, cut_goal_ref)

    cap = cap_ref[lax.axis_index("grp") * members + lax.axis_index("fsdp")].astype(F32)
    used = used_ref[...]
    pieces = []
    if groups:
        line, other = (iota((whole, whole), 0), iota((whole, whole), 1))
        earlier = dot(((other // SUB < line // SUB) & (other % SUB == 0)).astype(BF16), used)
        own = used.astype(F32)
        for group in range(groups):
            spot = (iota((whole, LANES), 0) % SUB + group * SUB).astype(F32)
            live = (spot < own) & (earlier + spot < cap)
            pieces.append(jnp.where(live, 1.0 / cap, 0.0)[:, :1])
    line, other = (iota((devices, whole), 0), iota((devices, whole), 1))
    earlier = dot((other < line * SUB).astype(BF16) * (other % SUB == 0).astype(BF16), used)
    own = dot((other == line * SUB).astype(BF16), used)
    for extra in range(rest):
        spot = float(groups * SUB + extra)
        live = (own > spot) & (earlier + spot < cap)
        pieces.append(jnp.where(live, 1.0 / cap, 0.0)[:, :1])
    scale = jnp.concatenate(pieces, axis=0) if len(pieces) > 1 else pieces[0]

    frozen_ref[...] = near_frozen_ref[...]
    hidden_ref[...] = hidden_refs[0][...] + hidden_refs[1][...]
    side = lax.rem(lax.axis_index("grp"), 2)
    copies[0].wait()
    copies[1].wait()

    def add_shard(shard, unused):
        total = None
        for place in range(2):
            target = w_ref.at[shard, pl.ds(place * depth, depth), :]
            wait_block(target, groups_of // 2, w_sem.at[place, shard])
            first = place * size + (2 * shard + 1 - side) * depth
            far = pl.ds(pl.multiple_of(first, depth), depth)
            term = dot(x_ref[:, far], w_ref[shard, place * depth : (place + 1) * depth])
            total = term if total is None else total + term
        frozen_ref[...] += total
        return unused

    lax.fori_loop(0, members, add_shard, 0, unroll=4)

    rate = ADAPTER_SCALE * LEARN_RATE
    block = min(width, 1024)
    up = up_ref[...].astype(F32)
    up_half = up_ref[...]
    up_delta = jnp.zeros((rank, kv_width), F32)
    for step in range(STEPS):
        hidden = hidden_ref[...].astype(BF16)
        error = frozen_ref[...] + ADAPTER_SCALE * dot(hidden, up_half) - goal_ref[...].astype(F32)
        residual = (scale * error).astype(BF16)
        back = dot(residual, up_half, ((1,), (1,))).astype(BF16)
        up_delta = up_delta - rate * dot(hidden, residual, ((0,), (0,)))
        last = step == STEPS - 1
        if not last:
            up_half = (up + up_delta).astype(BF16)
            hidden_ref[...] = jnp.zeros_like(hidden_ref)

        def down_block(at, unused):
            lanes = pl.ds(pl.multiple_of(at * block, block), block)
            moved = -rate * dot(back, x_ref[:, lanes], ((0,), (0,)))
            if step:
                moved = moved + delta_ref[:, lanes]
            delta_ref[:, lanes] = moved
            if not last:
                half_down = (down_ref[:, lanes].astype(F32) + moved).astype(BF16)
                hidden_ref[...] += dot(x_ref[:, lanes], half_down, ((1,), (1,)))
                return unused
            square = moved * moved
            for at in range(0, block, LANES):
                unused = unused + square[:, at : at + LANES]
            return unused

        squares = lax.fori_loop(
            0, width // block, down_block, jnp.zeros((rank, LANES), F32), unroll=4
        )

    total = jnp.sum(squares) + jnp.sum(up_delta * up_delta) + EPSILON
    total = jnp.full((1, LANES), total, F32)
    factor = jnp.minimum(1.0, clip_ref[0] / jnp.sqrt(total))[:, :1]
    share = width // devices
    up_share = kv_width // devices
    up_turned = (factor * up_delta).T
    pieces = share // rank
    tall = up_share // pieces

    def write(core, target):
        for pair in range(groups_of // 2):
            for member in range(members):
                device = (2 * pair + core) * members + member
                spot = lax.bitwise_xor(lax.div(lax.axis_index("grp"), 2), pair)
                place = lax.bitwise_xor(lax.axis_index("fsdp"), member)
                block = device * share // depth
                first = block % 2 * size + block // 2 * depth + device * share % depth
                moved = delta_ref[:, first : first + share]
                target[spot, place, :rank, :] = factor * moved
                first = device * up_share
                parts = [
                    up_turned[first + at * tall : first + (at + 1) * tall] for at in range(pieces)
                ]
                target[spot, place, rank:, :] = (
                    jnp.concatenate(parts, axis=1) if pieces > 1 else parts[0]
                )

    for core in range(2):
        mine = side == core

        @pl.when(mine)
        def _():
            write(core, keep_ref)

        @pl.when(jnp.logical_not(mine))
        def _():
            write(core, send_ref)


def exchange(blocks, partner_of):
    devices = lax.axis_size("grp") * lax.axis_size("fsdp")
    total = blocks[0]
    for place in range(1, len(blocks)):
        pairs = [(at, partner_of(at, place)) for at in range(devices)]
        total = total + lax.ppermute(blocks[place], BOTH, pairs)
    return total


def body(
    tokens,
    targets,
    row_owner_user,
    device_row_count,
    user_row_cap,
    value_weight,
    adapter_down,
    adapter_up,
    clip_norm_bound,
    down_noise,
    up_noise,
):
    groups, members = (lax.axis_size("grp"), lax.axis_size("fsdp"))
    devices = groups * members
    side = lax.axis_index("grp") % 2
    per_dev, width = tokens.shape
    kv_width = targets.shape[1]
    rank = adapter_down.shape[1]
    users = user_row_cap.shape[0]
    most = 3 * per_dev // (2 * devices)
    slots = devices * most
    whole = devices * SUB
    whole_groups, rest = divmod(most, SUB)
    smem = pl.BlockSpec(memory_space=pltpu.SMEM)
    vmem = pl.BlockSpec(memory_space=pltpu.VMEM)
    anywhere = pl.BlockSpec(memory_space=pl.ANY)

    params = pltpu.CompilerParams(vmem_limit_bytes=VMEM_BYTES)
    half = value_weight.shape[0] // 2
    depth = half // 2
    blocks = width // (2 * depth)
    piece = kv_width // (groups // 2)
    pair = lax.axis_index("grp") // 2
    swap = [(at, at ^ 1) for at in range(groups)]
    rings = weight_rings(groups, members)
    owners = row_owner_user.reshape(1, per_dev)
    near, far, got = ([], [], [])
    for part in range(2):
        columns = whole_groups * width // 2 + rest * width // 2 // SUB
        if part:
            columns += whole_groups * kv_width + rest * kv_width // SUB + LANES
        packed = pl.pallas_call(
            lambda *refs: pack_kernel(users, most, part, part == 1, *refs),
            out_shape=jax.ShapeDtypeStruct((users * SUB, columns), BF16),
            in_specs=[smem, vmem, anywhere, vmem],
            out_specs=vmem,
            scratch_shapes=[
                pltpu.VMEM((per_dev, width // 2), BF16),
                pltpu.SemaphoreType.DMA((blocks,)),
            ],
            compiler_params=params,
            name="pack_rows",
        )(device_row_count, owners, tokens, targets)
        got.append(
            lax.all_to_all(
                packed.reshape(users, SUB, columns), BOTH, split_axis=0, concat_axis=0, tiled=True
            ).reshape(whole, columns)
        )
        mine = lax.dynamic_slice(
            value_weight, (side * half + part * depth, pair * piece), (depth, piece)
        )
        near.append(lax.all_gather(mine, BOTH, axis=0, axis_index_groups=rings))
        far.append(lax.ppermute(near[-1], "grp", swap))

    share = width // devices
    tall = rank + kv_width // devices * rank // share
    down = adapter_down.T.reshape(rank, blocks, 2, depth)
    down = [down[:, :, part].reshape(rank, width // 2) for part in range(2)]
    frozen = []
    rows, hidden = ([], [])
    for part in range(2):
        joined, partial = pl.pallas_call(
            lambda *refs: rows_kernel(devices, most, *refs),
            out_shape=[
                jax.ShapeDtypeStruct((slots, width // 2), BF16),
                jax.ShapeDtypeStruct((slots, rank), F32),
            ],
            in_specs=[anywhere, vmem],
            out_specs=[anywhere, vmem],
            scratch_shapes=[
                pltpu.VMEM((slots, width // 2), BF16),
                pltpu.VMEM((max(rest, 1), whole, width // 2 // SUB), BF16),
                pltpu.SemaphoreType.DMA((whole_groups + rest,)),
                pltpu.SemaphoreType.DMA,
            ],
            compiler_params=params,
            name="join_rows",
        )(got[part], down[part])
        rows.append(joined)
        hidden.append(partial)
        frozen = [
            pl.pallas_call(
                lambda *refs: near_kernel(groups, members, *refs),
                out_shape=jax.ShapeDtypeStruct((slots, kv_width), F32),
                in_specs=[vmem] * len(frozen) + [anywhere, anywhere],
                out_specs=vmem,
                scratch_shapes=[
                    pltpu.VMEM((slots, width // 2), BF16),
                    pltpu.VMEM((members, depth, kv_width), BF16),
                    pltpu.SemaphoreType.DMA((members,)),
                    pltpu.SemaphoreType.DMA((members, groups // 2)),
                ],
                compiler_params=params,
                cost_estimate=pl.CostEstimate(
                    flops=slots * width * kv_width // 2, bytes_accessed=10**7, transcendentals=0
                ),
                name="near_product",
            )(*frozen, joined, near[part])
        ]

    package = jax.ShapeDtypeStruct((groups // 2, members, tall, share), F32)
    keep, send = pl.pallas_call(
        lambda cap, clip, got, x0, x1, frozen, h0, h1, w0, w1, *refs: user_kernel(
            groups, members, most, cap, clip, got, (x0, x1), frozen, (h0, h1), (w0, w1), *refs
        ),
        out_shape=[package] * 2,
        in_specs=[smem] * 2 + [anywhere] * 3 + [vmem] * 3 + [anywhere] * 2 + [vmem] * 2,
        out_specs=[vmem] * 2,
        scratch_shapes=[
            pltpu.VMEM((slots, width), BF16),
            pltpu.VMEM((slots, kv_width), BF16),
            pltpu.VMEM((max(rest, 1), whole, kv_width // SUB), BF16),
            pltpu.VMEM((whole, LANES), BF16),
            pltpu.VMEM((members, half, kv_width), BF16),
            pltpu.VMEM((slots, kv_width), F32),
            pltpu.VMEM((slots, rank), F32),
            pltpu.VMEM((rank, width), F32),
            pltpu.SemaphoreType.DMA((whole_groups + rest + 3,)),
            pltpu.SemaphoreType.DMA((2, members, groups // 2)),
        ],
        compiler_params=params,
        name="user_steps",
    )(
        user_row_cap,
        clip_norm_bound,
        got[1],
        *rows,
        *frozen,
        *hidden,
        *far,
        jnp.concatenate(down, axis=1),
        adapter_up,
    )

    other = lax.ppermute(send, "grp", swap)
    keep = keep.reshape(groups // 2, members // 2, 2, tall, share)
    other = other.reshape(keep.shape)
    square = [(pair, inner) for pair in range(groups // 2) for inner in range(2)]

    def in_square(at, place):
        pair, inner = square[place]
        return at ^ (2 * pair * members) ^ inner

    package = exchange(
        [keep[pair, :, inner] + other[pair, :, inner] for pair, inner in square], in_square
    )
    package = exchange(
        [package[place] for place in range(members // 2)], lambda at, place: at ^ (2 * place)
    )
    clip = clip_norm_bound[0]
    update_a = package[:rank].T + clip * down_noise
    pieces = share // rank
    up_sum = package[rank:].reshape(tall - rank, pieces, rank).transpose(1, 0, 2)
    update_b = up_sum.reshape(kv_width // devices, rank).T + clip * up_noise
    return (update_a, update_b)


def solution(mesh):
    in_specs = (
        P(BOTH, None),
        P(BOTH, None),
        P(BOTH, None),
        P(BOTH),
        P(),
        P("fsdp", None),
        P(),
        P(),
        P(),
        P(BOTH, None),
        P(None, BOTH),
    )
    out_specs = (P(BOTH, None), P(None, BOTH))
    return jax.shard_map(body, mesh=mesh, in_specs=in_specs, out_specs=out_specs, check_vma=False)
```

```python
import jax
import jax.numpy as jnp
from jax import lax
from jax.experimental import pallas as pl
from jax.experimental.pallas import tpu as pltpu
from jax.sharding import PartitionSpec as P

STEPS = 2
ADAPTER_SCALE = 2.0
LEARN_RATE = 0.05
EPSILON = 1e-06

SUB = 8
LANES = 128
BOTH = ("grp", "fsdp")
VMEM_BYTES = 56 * 1024 * 1024

F32 = jnp.float32
BF16 = jnp.bfloat16


def dot(left, right, contract=((1,), (0,))):
    return lax.dot_general(left, right, (contract, ((), ())), preferred_element_type=F32)


def iota(shape, axis):
    return lax.broadcasted_iota(jnp.int32, shape, axis)


def pack_kernel(
    users, most, count_ref, owner_ref, tokens_ref, targets_ref, out_ref, cut_ref, cut_goal_ref
):
    rows = tokens_ref.shape[0]
    groups, rest = divmod(most, SUB)
    owner_row = owner_ref[...]
    first, second = (iota((rows, rows), 0), iota((rows, rows), 1))
    owner = jnp.sum(jnp.where(first == second, owner_row, 0), axis=1, keepdims=True)
    same = (owner == owner_row) & (first < second)
    rank = jnp.sum(same.astype(jnp.int32), axis=0, keepdims=True)
    line = iota((users * SUB, rows), 0)
    mine = line // SUB == owner_row
    slot = line % SUB
    picks = [mine & (rank == slot + group * SUB) for group in range(groups)]
    user = iota((users, rows), 0) == owner_row
    picks += [user & (rank == groups * SUB + extra) for extra in range(rest)]
    pick = jnp.concatenate([one.astype(BF16) for one in picks], axis=0)
    whole = users * SUB
    line, other = (iota((whole, whole), 0), iota((whole, whole), 1))
    turn = (other == line % SUB * users + line // SUB).astype(BF16)
    column = 0
    for source, cut in ((tokens_ref, cut_ref), (targets_ref, cut_goal_ref)):
        width = source.shape[1]
        piece = width // SUB
        for part in range(SUB):
            found = dot(pick, source[:, part * piece : (part + 1) * piece]).astype(BF16)
            for group in range(groups):
                spot = column + group * width + part * piece
                out_ref[:, spot : spot + piece] = found[group * whole : (group + 1) * whole]
            for extra in range(rest):
                first = groups * whole + extra * users
                cut[extra, part * users : (part + 1) * users] = found[first : first + users]
        column += groups * width
        for extra in range(rest):
            out_ref[:, column : column + piece] = dot(turn, cut[extra]).astype(BF16)
            column += piece
    used = mine & (iota((users * SUB, rows), 1) < count_ref[0])
    number = jnp.sum(used.astype(F32), axis=1, keepdims=True)
    out_ref[:, column : column + LANES] = jnp.broadcast_to(number, (users * SUB, LANES)).astype(
        BF16
    )


def weight_rings(groups, members):
    round_trip = [(at, 0) for at in range(groups // 2)]
    round_trip += [(at, 1) for at in reversed(range(groups // 2))]
    length, layers = (len(round_trip), members // 2)
    rings = []
    for core in range(2):
        up, down = ([], [])
        low, high = (list(range(length // 2)), list(range(length // 2, length)))
        for layer in range(1, layers):
            turned = layer % 2 == 0
            up += [(layer, at) for at in (low[::-1] if turned else low)]
            down += [(layer, at) for at in (high if turned else high[::-1])]
        path = [(0, at) for at in reversed(range(length))] + up + down[::-1]
        ring = []
        for layer, at in path:
            pair, inner = round_trip[(at + core * length // 2) % length]
            ring.append((2 * pair + core) * members + 2 * layer + inner)
        rings.append(ring)
    return rings


def weight_copies(ring_of, groups, members, source, target, sems):
    pairs = groups // 2
    columns = source.shape[2]
    side = lax.rem(lax.axis_index("grp"), 2)
    rings = weight_rings(groups, members)

    def copy(member, pair):
        spots = [ring.index((2 * pair + core) * members + member) for core, ring in enumerate(rings)]
        spot = jnp.where(side == ring_of, spots[0], spots[1])
        return pltpu.make_async_copy(
            source.at[spot],
            target.at[member, :, pl.ds(pair * columns, columns)],
            sems.at[member, pair],
        )

    return [[copy(member, pair) for pair in range(pairs)] for member in range(members)]


def wait_block(target, place, pairs, sems):
    columns = target.shape[2] // pairs
    for pair in range(pairs):
        block = target.at[place, :, pl.ds(pair * columns, columns)]
        pltpu.make_async_copy(block, block, sems.at[place, pair]).wait()


def near_kernel(
    groups_of,
    members,
    most,
    got_ref,
    near_ref,
    down_ref,
    x_out_ref,
    frozen_ref,
    hidden_ref,
    x_ref,
    cut_ref,
    w_ref,
    got_sem,
    out_sem,
    w_sem,
):
    groups, rest = divmod(most, SUB)
    devices = groups_of * members
    width = x_ref.shape[1]
    whole = devices * SUB
    half = w_ref.shape[1]
    copies = []
    column = 0
    for group in range(groups):
        copies.append(
            (got_ref.at[:, pl.ds(column, width)], x_ref.at[pl.ds(group * whole, whole), :])
        )
        column += width
    for extra in range(rest):
        copies.append((got_ref.at[:, pl.ds(column, width // SUB)], cut_ref.at[extra]))
        column += width // SUB
    copies = [
        pltpu.make_async_copy(source, target, got_sem.at[place])
        for place, (source, target) in enumerate(copies)
    ]
    for copy in copies:
        copy.start()
    weights = weight_copies(0, groups_of, members, near_ref, w_ref, w_sem)
    for place, pieces in enumerate(weights):
        if place == 2:
            for copy in copies:
                copy.wait()
        for copy in pieces:
            copy.start()
    join_pieces(devices, groups * whole, rest, x_ref, cut_ref)
    out = pltpu.make_async_copy(x_ref, x_out_ref, out_sem)
    out.start()

    frozen_ref[...] = jnp.zeros_like(frozen_ref)
    hidden_ref[...] = jnp.zeros_like(hidden_ref)
    side = lax.rem(lax.axis_index("grp"), 2)

    def add_shard(shard, unused):
        wait_block(w_ref, shard, groups_of // 2, w_sem)
        near = pl.ds(pl.multiple_of((2 * shard + side) * half, half), half)
        both = pl.ds(pl.multiple_of(2 * shard * half, 2 * half), 2 * half)
        frozen_ref[...] += dot(x_ref[:, near], w_ref[shard])
        hidden_ref[...] += dot(x_ref[:, both], down_ref[:, both], ((1,), (1,)))
        return unused

    lax.fori_loop(0, members, add_shard, 0, unroll=4)
    out.wait()


def join_pieces(devices, bottom, rest, full, cut):
    whole = devices * SUB
    line, other = (iota((whole, whole), 0), iota((whole, whole), 1))
    turn = (other == line % devices * SUB + line // devices).astype(BF16)
    piece = full.shape[1] // SUB
    for extra in range(rest):
        first = bottom + extra * devices
        rows = dot(turn, cut[extra]).astype(BF16)
        for part in range(SUB):
            full[first : first + devices, part * piece : (part + 1) * piece] = rows[
                part * devices : (part + 1) * devices
            ]


def user_kernel(
    groups_of,
    members,
    most,
    cap_ref,
    clip_ref,
    got_ref,
    rows_ref,
    near_frozen_ref,
    near_hidden_ref,
    far_ref,
    down_ref,
    up_ref,
    *refs,
):
    keep_refs, send_refs = (refs[0:2], refs[2:4])
    (
        x_ref,
        goal_ref,
        cut_goal_ref,
        used_ref,
        w_ref,
        frozen_ref,
        hidden_ref,
        delta_ref,
        got_sem,
        w_sem,
    ) = refs[4:]
    groups, rest = divmod(most, SUB)
    devices = groups_of * members
    rank, width = down_ref.shape
    kv_width = up_ref.shape[1]
    whole = devices * SUB
    half = w_ref.shape[1]
    copies = [(rows_ref, x_ref)]
    column = groups * width + rest * width // SUB
    for group in range(groups):
        copies.append(
            (got_ref.at[:, pl.ds(column, kv_width)], goal_ref.at[pl.ds(group * whole, whole), :])
        )
        column += kv_width
    for extra in range(rest):
        copies.append((got_ref.at[:, pl.ds(column, kv_width // SUB)], cut_goal_ref.at[extra]))
        column += kv_width // SUB
    copies.append((got_ref.at[:, pl.ds(column, LANES)], used_ref))
    copies = [
        pltpu.make_async_copy(source, target, got_sem.at[place])
        for place, (source, target) in enumerate(copies)
    ]
    for copy in copies[1:] + copies[:1]:
        copy.start()
    for pieces in weight_copies(1, groups_of, members, far_ref, w_ref, w_sem):
        for copy in pieces:
            copy.start()
    for copy in copies[1:]:
        copy.wait()
    join_pieces(devices, groups * whole, rest, goal_ref, cut_goal_ref)

    cap = cap_ref[lax.axis_index("grp") * members + lax.axis_index("fsdp")].astype(F32)
    used = used_ref[...]
    pieces = []
    if groups:
        line, other = (iota((whole, whole), 0), iota((whole, whole), 1))
        earlier = dot(((other // SUB < line // SUB) & (other % SUB == 0)).astype(BF16), used)
        own = used.astype(F32)
        for group in range(groups):
            spot = (iota((whole, LANES), 0) % SUB + group * SUB).astype(F32)
            live = (spot < own) & (earlier + spot < cap)
            pieces.append(jnp.where(live, 1.0 / cap, 0.0)[:, :1])
    line, other = (iota((devices, whole), 0), iota((devices, whole), 1))
    earlier = dot((other < line * SUB).astype(BF16) * (other % SUB == 0).astype(BF16), used)
    own = dot((other == line * SUB).astype(BF16), used)
    for extra in range(rest):
        spot = float(groups * SUB + extra)
        live = (own > spot) & (earlier + spot < cap)
        pieces.append(jnp.where(live, 1.0 / cap, 0.0)[:, :1])
    scale = jnp.concatenate(pieces, axis=0) if len(pieces) > 1 else pieces[0]

    frozen_ref[...] = near_frozen_ref[...]
    hidden_ref[...] = near_hidden_ref[...]
    side = lax.rem(lax.axis_index("grp"), 2)
    copies[0].wait()

    def add_shard(shard, unused):
        wait_block(w_ref, shard, groups_of // 2, w_sem)
        far = pl.ds(pl.multiple_of((2 * shard + 1 - side) * half, half), half)
        frozen_ref[...] += dot(x_ref[:, far], w_ref[shard])
        return unused

    lax.fori_loop(0, members, add_shard, 0, unroll=4)

    rate = ADAPTER_SCALE * LEARN_RATE
    block = min(width, 1024)
    up = up_ref[...].astype(F32)
    up_half = up_ref[...]
    up_delta = jnp.zeros((rank, kv_width), F32)
    for step in range(STEPS):
        hidden = hidden_ref[...].astype(BF16)
        error = frozen_ref[...] + ADAPTER_SCALE * dot(hidden, up_half) - goal_ref[...].astype(F32)
        residual = (scale * error).astype(BF16)
        back = dot(residual, up_half, ((1,), (1,))).astype(BF16)
        up_delta = up_delta - rate * dot(hidden, residual, ((0,), (0,)))
        last = step == STEPS - 1
        if not last:
            up_half = (up + up_delta).astype(BF16)
            hidden_ref[...] = jnp.zeros_like(hidden_ref)

        def down_block(at, unused):
            lanes = pl.ds(pl.multiple_of(at * block, block), block)
            moved = -rate * dot(back, x_ref[:, lanes], ((0,), (0,)))
            if step:
                moved = moved + delta_ref[:, lanes]
            delta_ref[:, lanes] = moved
            if not last:
                half_down = (down_ref[:, lanes].astype(F32) + moved).astype(BF16)
                hidden_ref[...] += dot(x_ref[:, lanes], half_down, ((1,), (1,)))
                return unused
            square = moved * moved
            for at in range(0, block, LANES):
                unused = unused + square[:, at : at + LANES]
            return unused

        squares = lax.fori_loop(
            0, width // block, down_block, jnp.zeros((rank, LANES), F32), unroll=4
        )

    total = jnp.sum(squares) + jnp.sum(up_delta * up_delta) + EPSILON
    total = jnp.full((1, LANES), total, F32)
    factor = jnp.minimum(1.0, clip_ref[0] / jnp.sqrt(total))[:, :1]
    share = width // devices
    up_share = kv_width // devices
    up_turned = (factor * up_delta).T
    pieces = share // rank
    tall = up_share // pieces

    def write(core, targets):
        edge = targets[0].shape[3]
        for pair in range(devices // members // 2):
            for member in range(members):
                device = (2 * pair + core) * members + member
                spot = lax.bitwise_xor(lax.div(lax.axis_index("grp"), 2), pair)
                inner = lax.bitwise_xor(lax.rem(lax.axis_index("fsdp"), 2), member % 2)
                outer = member // 2
                moved = factor * delta_ref[:, device * share : (device + 1) * share]
                targets[0][spot, inner, outer] = moved[:edge]
                targets[1][spot, inner, outer, : rank - edge, :] = moved[edge:]
                first = device * up_share
                parts = [
                    up_turned[first + at * tall : first + (at + 1) * tall] for at in range(pieces)
                ]
                targets[1][spot, inner, outer, rank - edge :, :] = (
                    jnp.concatenate(parts, axis=1) if pieces > 1 else parts[0]
                )

    for core in range(2):
        mine = side == core

        @pl.when(mine)
        def _():
            write(core, keep_refs)

        @pl.when(jnp.logical_not(mine))
        def _():
            write(core, send_refs)


def halve(package, axis, bits, partner):
    bit = package.shape[bits] // 2
    while bit:
        keep = lax.slice_in_dim(package, 0, bit, axis=bits)
        send = lax.slice_in_dim(package, bit, 2 * bit, axis=bits)
        pairs = [(at, at ^ (partner * bit)) for at in range(lax.axis_size(axis))]
        package = lax.ppermute(send, axis, pairs) + keep
        bit //= 2
    return package


def body(
    tokens,
    targets,
    row_owner_user,
    device_row_count,
    user_row_cap,
    value_weight,
    adapter_down,
    adapter_up,
    clip_norm_bound,
    down_noise,
    up_noise,
):
    groups, members = (lax.axis_size("grp"), lax.axis_size("fsdp"))
    devices = groups * members
    side = lax.axis_index("grp") % 2
    per_dev, width = tokens.shape
    kv_width = targets.shape[1]
    rank = adapter_down.shape[1]
    users = user_row_cap.shape[0]
    most = 3 * per_dev // (2 * devices)
    slots = devices * most
    whole = devices * SUB
    whole_groups, rest = divmod(most, SUB)
    smem = pl.BlockSpec(memory_space=pltpu.SMEM)
    vmem = pl.BlockSpec(memory_space=pltpu.VMEM)
    anywhere = pl.BlockSpec(memory_space=pl.ANY)

    half = value_weight.shape[0] // 2
    piece = kv_width // (groups // 2)
    pair = lax.axis_index("grp") // 2
    mine = lax.dynamic_slice(value_weight, (side * half, pair * piece), (half, piece))
    near = lax.all_gather(mine, BOTH, axis=0, axis_index_groups=weight_rings(groups, members))
    swap = [(at, at ^ 1) for at in range(groups)]
    far = lax.ppermute(near, "grp", swap)

    columns = whole_groups * (width + kv_width) + rest * (width + kv_width) // SUB + LANES
    packed = pl.pallas_call(
        lambda *refs: pack_kernel(users, most, *refs),
        out_shape=jax.ShapeDtypeStruct((users * SUB, columns), BF16),
        in_specs=[smem, vmem, vmem, vmem],
        out_specs=vmem,
        scratch_shapes=[
            pltpu.VMEM((max(rest, 1), users * SUB, width // SUB), BF16),
            pltpu.VMEM((max(rest, 1), users * SUB, kv_width // SUB), BF16),
        ],
        compiler_params=pltpu.CompilerParams(vmem_limit_bytes=VMEM_BYTES),
        name="pack_rows",
    )(device_row_count, row_owner_user.reshape(1, per_dev), tokens, targets)
    got = lax.all_to_all(
        packed.reshape(users, SUB, columns), BOTH, split_axis=0, concat_axis=0, tiled=True
    ).reshape(whole, columns)
    share = width // devices
    tall = rank + kv_width // devices * rank // share
    down = adapter_down.T
    rows, near_frozen, near_hidden = pl.pallas_call(
        lambda *refs: near_kernel(groups, members, most, *refs),
        out_shape=[
            jax.ShapeDtypeStruct((slots, width), BF16),
            jax.ShapeDtypeStruct((slots, kv_width), F32),
            jax.ShapeDtypeStruct((slots, rank), F32),
        ],
        in_specs=[anywhere, anywhere, vmem],
        out_specs=[anywhere, vmem, vmem],
        scratch_shapes=[
            pltpu.VMEM((slots, width), BF16),
            pltpu.VMEM((max(rest, 1), whole, width // SUB), BF16),
            pltpu.VMEM((members, half, kv_width), BF16),
            pltpu.SemaphoreType.DMA((whole_groups + rest,)),
            pltpu.SemaphoreType.DMA,
            pltpu.SemaphoreType.DMA((members, groups // 2)),
        ],
        compiler_params=pltpu.CompilerParams(vmem_limit_bytes=VMEM_BYTES),
        cost_estimate=pl.CostEstimate(
            flops=slots * width * kv_width, bytes_accessed=3 * 10**7, transcendentals=0
        ),
        name="near_product",
    )(got, near, down)

    edge = tall // (2 * SUB) * SUB
    grid = (groups // 2, 2, members // 2)
    streams = [jax.ShapeDtypeStruct(grid + (size, share), F32) for size in (edge, tall - edge)]
    kept_y, kept_x, sent_y, sent_x = pl.pallas_call(
        lambda *refs: user_kernel(groups, members, most, *refs),
        out_shape=streams * 2,
        in_specs=[smem, smem, anywhere, anywhere, vmem, vmem, anywhere, vmem, vmem],
        out_specs=[vmem] * 4,
        scratch_shapes=[
            pltpu.VMEM((slots, width), BF16),
            pltpu.VMEM((slots, kv_width), BF16),
            pltpu.VMEM((max(rest, 1), whole, kv_width // SUB), BF16),
            pltpu.VMEM((whole, LANES), BF16),
            pltpu.VMEM((members, half, kv_width), BF16),
            pltpu.VMEM((slots, kv_width), F32),
            pltpu.VMEM((slots, rank), F32),
            pltpu.VMEM((rank, width), F32),
            pltpu.SemaphoreType.DMA((whole_groups + rest + 2,)),
            pltpu.SemaphoreType.DMA((members, groups // 2)),
        ],
        compiler_params=pltpu.CompilerParams(vmem_limit_bytes=VMEM_BYTES),
        name="user_steps",
    )(user_row_cap, clip_norm_bound, got, rows, near_frozen, near_hidden, far, down, adapter_up)

    first = kept_y + lax.ppermute(sent_y, "grp", swap)
    second = kept_x + lax.ppermute(sent_x, "grp", swap)
    first = halve(halve(first, "grp", 0, 2), "fsdp", 1, 1)
    second = halve(halve(second, "fsdp", 1, 1), "grp", 0, 2)
    package = jnp.concatenate([first[0, 0], second[0, 0]], axis=1)
    lines = [list(range(one, members, 2)) for one in range(2)]
    package = lax.all_to_all(
        package, "fsdp", split_axis=0, concat_axis=0, axis_index_groups=lines, tiled=True
    )
    package = jnp.sum(package, axis=0)
    clip = clip_norm_bound[0]
    update_a = package[:rank].T + clip * down_noise
    pieces = share // rank
    up_sum = package[rank:].reshape(tall - rank, pieces, rank).transpose(1, 0, 2)
    update_b = up_sum.reshape(kv_width // devices, rank).T + clip * up_noise
    return (update_a, update_b)


def solution(mesh):
    in_specs = (
        P(BOTH, None),
        P(BOTH, None),
        P(BOTH, None),
        P(BOTH),
        P(),
        P("fsdp", None),
        P(),
        P(),
        P(),
        P(BOTH, None),
        P(None, BOTH),
    )
    out_specs = (P(BOTH, None), P(None, BOTH))
    return jax.shard_map(body, mesh=mesh, in_specs=in_specs, out_specs=out_specs, check_vma=False)
```

```python
import jax
import jax.numpy as jnp
from jax import lax
from jax.experimental import pallas as pl
from jax.experimental.pallas import tpu as pltpu
from jax.sharding import PartitionSpec as P

STEPS = 2
ADAPTER_SCALE = 2.0
LEARN_RATE = 0.05
EPSILON = 1e-06

SUB = 8
LANES = 128
BOTH = ("grp", "fsdp")
VMEM_BYTES = 56 * 1024 * 1024

F32 = jnp.float32
BF16 = jnp.bfloat16


def dot(left, right, contract=((1,), (0,))):
    return lax.dot_general(left, right, (contract, ((), ())), preferred_element_type=F32)


def iota(shape, axis):
    return lax.broadcasted_iota(jnp.int32, shape, axis)


def pack_kernel(
    users, most, count_ref, owner_ref, tokens_ref, targets_ref, out_ref, cut_ref, cut_goal_ref
):
    rows = tokens_ref.shape[0]
    groups, rest = divmod(most, SUB)
    owner_row = owner_ref[...]
    first, second = (iota((rows, rows), 0), iota((rows, rows), 1))
    owner = jnp.sum(jnp.where(first == second, owner_row, 0), axis=1, keepdims=True)
    same = (owner == owner_row) & (first < second)
    rank = jnp.sum(same.astype(jnp.int32), axis=0, keepdims=True)
    line = iota((users * SUB, rows), 0)
    mine = line // SUB == owner_row
    slot = line % SUB
    picks = [mine & (rank == slot + group * SUB) for group in range(groups)]
    user = iota((users, rows), 0) == owner_row
    picks += [user & (rank == groups * SUB + extra) for extra in range(rest)]
    pick = jnp.concatenate([one.astype(BF16) for one in picks], axis=0)
    whole = users * SUB
    line, other = (iota((whole, whole), 0), iota((whole, whole), 1))
    turn = (other == line % SUB * users + line // SUB).astype(BF16)
    column = 0
    for source, cut in ((tokens_ref, cut_ref), (targets_ref, cut_goal_ref)):
        width = source.shape[1]
        piece = width // SUB
        for part in range(SUB):
            found = dot(pick, source[:, part * piece : (part + 1) * piece]).astype(BF16)
            for group in range(groups):
                spot = column + group * width + part * piece
                out_ref[:, spot : spot + piece] = found[group * whole : (group + 1) * whole]
            for extra in range(rest):
                first = groups * whole + extra * users
                cut[extra, part * users : (part + 1) * users] = found[first : first + users]
        column += groups * width
        for extra in range(rest):
            out_ref[:, column : column + piece] = dot(turn, cut[extra]).astype(BF16)
            column += piece
    used = mine & (iota((users * SUB, rows), 1) < count_ref[0])
    number = jnp.sum(used.astype(F32), axis=1, keepdims=True)
    out_ref[:, column : column + LANES] = jnp.broadcast_to(number, (users * SUB, LANES)).astype(
        BF16
    )


def weight_rings(groups, members):
    round_trip = [(at, 0) for at in range(groups // 2)]
    round_trip += [(at, 1) for at in reversed(range(groups // 2))]
    length, layers = (len(round_trip), members // 4)
    rings = []
    for core in range(2):
        up, down = ([], [])
        low, high = (list(range(length // 2)), list(range(length // 2, length)))
        for layer in range(1, layers):
            turned = layer % 2 == 0
            up += [(layer, at) for at in (low[::-1] if turned else low)]
            down += [(layer, at) for at in (high if turned else high[::-1])]
        path = [(0, at) for at in reversed(range(length))] + up + down[::-1]
        ring = []
        for layer, at in path:
            pair, inner = round_trip[(at + core * length // 2) % length]
            ring.append((2 * pair + core) * members + 2 * layer + inner)
        rings.append(ring)
    return rings


def weight_copies(ring_of, groups, members, source, target, sems):
    pairs = groups // 2
    depth = source.shape[2]
    side = lax.rem(lax.axis_index("grp"), 2)
    far_end = lax.div(lax.axis_index("fsdp"), members // 2)
    rings = weight_rings(groups, members)

    def copy(member, pair):
        holder = member % (members // 2)
        spots = [ring.index((2 * pair + core) * members + holder) for core, ring in enumerate(rings)]
        spot = jnp.where(side == ring_of, spots[0], spots[1])
        swapped = lax.bitwise_xor(far_end, member // (members // 2))
        return pltpu.make_async_copy(
            source.at[spot, swapped],
            target.at[member, pl.ds(pair * depth, depth), :],
            sems.at[member, pair],
        )

    return [[copy(member, pair) for pair in range(pairs)] for member in range(members)]


def wait_block(target, place, pairs, sems):
    depth = target.shape[1] // pairs
    for pair in range(pairs):
        block = target.at[place, pl.ds(pair * depth, depth), :]
        pltpu.make_async_copy(block, block, sems.at[place, pair]).wait()


def near_kernel(
    groups_of,
    members,
    most,
    got_ref,
    near_ref,
    down_ref,
    x_out_ref,
    frozen_ref,
    hidden_ref,
    x_ref,
    cut_ref,
    w_ref,
    got_sem,
    out_sem,
    w_sem,
):
    groups, rest = divmod(most, SUB)
    devices = groups_of * members
    width = x_ref.shape[1]
    whole = devices * SUB
    half = w_ref.shape[1]
    copies = []
    column = 0
    for group in range(groups):
        copies.append(
            (got_ref.at[:, pl.ds(column, width)], x_ref.at[pl.ds(group * whole, whole), :])
        )
        column += width
    for extra in range(rest):
        copies.append((got_ref.at[:, pl.ds(column, width // SUB)], cut_ref.at[extra]))
        column += width // SUB
    copies = [
        pltpu.make_async_copy(source, target, got_sem.at[place])
        for place, (source, target) in enumerate(copies)
    ]
    for copy in copies:
        copy.start()
    weights = weight_copies(0, groups_of, members, near_ref, w_ref, w_sem)
    for place, pieces in enumerate(weights):
        if place == 2:
            for copy in copies:
                copy.wait()
        for copy in pieces:
            copy.start()
    join_pieces(devices, groups * whole, rest, x_ref, cut_ref)
    out = pltpu.make_async_copy(x_ref, x_out_ref, out_sem)
    out.start()

    frozen_ref[...] = jnp.zeros_like(frozen_ref)
    hidden_ref[...] = jnp.zeros_like(hidden_ref)
    side = lax.rem(lax.axis_index("grp"), 2)

    def add_shard(shard, unused):
        wait_block(w_ref, shard, groups_of // 2, w_sem)
        near = pl.ds(pl.multiple_of((2 * shard + side) * half, half), half)
        both = pl.ds(pl.multiple_of(2 * shard * half, 2 * half), 2 * half)
        frozen_ref[...] += dot(x_ref[:, near], w_ref[shard])
        hidden_ref[...] += dot(x_ref[:, both], down_ref[:, both], ((1,), (1,)))
        return unused

    lax.fori_loop(0, members, add_shard, 0, unroll=4)
    out.wait()


def join_pieces(devices, bottom, rest, full, cut):
    whole = devices * SUB
    line, other = (iota((whole, whole), 0), iota((whole, whole), 1))
    turn = (other == line % devices * SUB + line // devices).astype(BF16)
    piece = full.shape[1] // SUB
    for extra in range(rest):
        first = bottom + extra * devices
        rows = dot(turn, cut[extra]).astype(BF16)
        for part in range(SUB):
            full[first : first + devices, part * piece : (part + 1) * piece] = rows[
                part * devices : (part + 1) * devices
            ]


def user_kernel(
    groups_of,
    members,
    most,
    cap_ref,
    clip_ref,
    got_ref,
    rows_ref,
    near_frozen_ref,
    near_hidden_ref,
    far_ref,
    down_ref,
    up_ref,
    *refs,
):
    keep_refs, send_refs = (refs[0:2], refs[2:4])
    (
        x_ref,
        goal_ref,
        cut_goal_ref,
        used_ref,
        w_ref,
        frozen_ref,
        hidden_ref,
        delta_ref,
        got_sem,
        w_sem,
    ) = refs[4:]
    groups, rest = divmod(most, SUB)
    devices = groups_of * members
    rank, width = down_ref.shape
    kv_width = up_ref.shape[1]
    whole = devices * SUB
    half = w_ref.shape[1]
    copies = [(rows_ref, x_ref)]
    column = groups * width + rest * width // SUB
    for group in range(groups):
        copies.append(
            (got_ref.at[:, pl.ds(column, kv_width)], goal_ref.at[pl.ds(group * whole, whole), :])
        )
        column += kv_width
    for extra in range(rest):
        copies.append((got_ref.at[:, pl.ds(column, kv_width // SUB)], cut_goal_ref.at[extra]))
        column += kv_width // SUB
    copies.append((got_ref.at[:, pl.ds(column, LANES)], used_ref))
    copies = [
        pltpu.make_async_copy(source, target, got_sem.at[place])
        for place, (source, target) in enumerate(copies)
    ]
    for copy in copies[1:] + copies[:1]:
        copy.start()
    for pieces in weight_copies(1, groups_of, members, far_ref, w_ref, w_sem):
        for copy in pieces:
            copy.start()
    for copy in copies[1:]:
        copy.wait()
    join_pieces(devices, groups * whole, rest, goal_ref, cut_goal_ref)

    cap = cap_ref[lax.axis_index("grp") * members + lax.axis_index("fsdp")].astype(F32)
    used = used_ref[...]
    pieces = []
    if groups:
        line, other = (iota((whole, whole), 0), iota((whole, whole), 1))
        earlier = dot(((other // SUB < line // SUB) & (other % SUB == 0)).astype(BF16), used)
        own = used.astype(F32)
        for group in range(groups):
            spot = (iota((whole, LANES), 0) % SUB + group * SUB).astype(F32)
            live = (spot < own) & (earlier + spot < cap)
            pieces.append(jnp.where(live, 1.0 / cap, 0.0)[:, :1])
    line, other = (iota((devices, whole), 0), iota((devices, whole), 1))
    earlier = dot((other < line * SUB).astype(BF16) * (other % SUB == 0).astype(BF16), used)
    own = dot((other == line * SUB).astype(BF16), used)
    for extra in range(rest):
        spot = float(groups * SUB + extra)
        live = (own > spot) & (earlier + spot < cap)
        pieces.append(jnp.where(live, 1.0 / cap, 0.0)[:, :1])
    scale = jnp.concatenate(pieces, axis=0) if len(pieces) > 1 else pieces[0]

    frozen_ref[...] = near_frozen_ref[...]
    hidden_ref[...] = near_hidden_ref[...]
    side = lax.rem(lax.axis_index("grp"), 2)
    copies[0].wait()

    def add_shard(shard, unused):
        wait_block(w_ref, shard, groups_of // 2, w_sem)
        far = pl.ds(pl.multiple_of((2 * shard + 1 - side) * half, half), half)
        frozen_ref[...] += dot(x_ref[:, far], w_ref[shard])
        return unused

    lax.fori_loop(0, members, add_shard, 0, unroll=4)

    rate = ADAPTER_SCALE * LEARN_RATE
    block = min(width, 1024)
    up = up_ref[...].astype(F32)
    up_half = up_ref[...]
    up_delta = jnp.zeros((rank, kv_width), F32)
    for step in range(STEPS):
        hidden = hidden_ref[...].astype(BF16)
        error = frozen_ref[...] + ADAPTER_SCALE * dot(hidden, up_half) - goal_ref[...].astype(F32)
        residual = (scale * error).astype(BF16)
        back = dot(residual, up_half, ((1,), (1,))).astype(BF16)
        up_delta = up_delta - rate * dot(hidden, residual, ((0,), (0,)))
        last = step == STEPS - 1
        if not last:
            up_half = (up + up_delta).astype(BF16)
            hidden_ref[...] = jnp.zeros_like(hidden_ref)

        def down_block(at, unused):
            lanes = pl.ds(pl.multiple_of(at * block, block), block)
            moved = -rate * dot(back, x_ref[:, lanes], ((0,), (0,)))
            if step:
                moved = moved + delta_ref[:, lanes]
            delta_ref[:, lanes] = moved
            if not last:
                half_down = (down_ref[:, lanes].astype(F32) + moved).astype(BF16)
                hidden_ref[...] += dot(x_ref[:, lanes], half_down, ((1,), (1,)))
                return unused
            square = moved * moved
            for at in range(0, block, LANES):
                unused = unused + square[:, at : at + LANES]
            return unused

        squares = lax.fori_loop(
            0, width // block, down_block, jnp.zeros((rank, LANES), F32), unroll=4
        )

    total = jnp.sum(squares) + jnp.sum(up_delta * up_delta) + EPSILON
    total = jnp.full((1, LANES), total, F32)
    factor = jnp.minimum(1.0, clip_ref[0] / jnp.sqrt(total))[:, :1]
    share = width // devices
    up_share = kv_width // devices
    up_turned = (factor * up_delta).T
    pieces = share // rank
    tall = up_share // pieces

    def write(core, targets):
        edge = targets[0].shape[3]
        for pair in range(devices // members // 2):
            for member in range(members):
                device = (2 * pair + core) * members + member
                spot = lax.bitwise_xor(lax.div(lax.axis_index("grp"), 2), pair)
                inner = lax.bitwise_xor(lax.rem(lax.axis_index("fsdp"), 2), member % 2)
                outer = member // 2
                moved = factor * delta_ref[:, device * share : (device + 1) * share]
                targets[0][spot, inner, outer] = moved[:edge]
                targets[1][spot, inner, outer, : rank - edge, :] = moved[edge:]
                first = device * up_share
                parts = [
                    up_turned[first + at * tall : first + (at + 1) * tall] for at in range(pieces)
                ]
                targets[1][spot, inner, outer, rank - edge :, :] = (
                    jnp.concatenate(parts, axis=1) if pieces > 1 else parts[0]
                )

    for core in range(2):
        mine = side == core

        @pl.when(mine)
        def _():
            write(core, keep_refs)

        @pl.when(jnp.logical_not(mine))
        def _():
            write(core, send_refs)


def halve(package, axis, bits, partner):
    bit = package.shape[bits] // 2
    while bit:
        keep = lax.slice_in_dim(package, 0, bit, axis=bits)
        send = lax.slice_in_dim(package, bit, 2 * bit, axis=bits)
        pairs = [(at, at ^ (partner * bit)) for at in range(lax.axis_size(axis))]
        package = lax.ppermute(send, axis, pairs) + keep
        bit //= 2
    return package


def body(
    tokens,
    targets,
    row_owner_user,
    device_row_count,
    user_row_cap,
    value_weight,
    adapter_down,
    adapter_up,
    clip_norm_bound,
    down_noise,
    up_noise,
):
    groups, members = (lax.axis_size("grp"), lax.axis_size("fsdp"))
    devices = groups * members
    side = lax.axis_index("grp") % 2
    per_dev, width = tokens.shape
    kv_width = targets.shape[1]
    rank = adapter_down.shape[1]
    users = user_row_cap.shape[0]
    most = 3 * per_dev // (2 * devices)
    slots = devices * most
    whole = devices * SUB
    whole_groups, rest = divmod(most, SUB)
    smem = pl.BlockSpec(memory_space=pltpu.SMEM)
    vmem = pl.BlockSpec(memory_space=pltpu.VMEM)
    anywhere = pl.BlockSpec(memory_space=pl.ANY)

    half = value_weight.shape[0] // 2
    depth = half // (groups // 2)
    pair = lax.axis_index("grp") // 2
    mine = lax.dynamic_slice_in_dim(value_weight, side * half + pair * depth, depth, axis=0)
    across = [(at, at ^ (members // 2)) for at in range(members)]
    both = jnp.stack([mine, lax.ppermute(mine, "fsdp", across)])
    rings = weight_rings(groups, members)
    rings += [[at + members // 2 for at in ring] for ring in rings]
    near = lax.all_gather(both, BOTH, axis=0, axis_index_groups=rings)
    swap = [(at, at ^ 1) for at in range(groups)]
    far = lax.ppermute(near, "grp", swap)

    columns = whole_groups * (width + kv_width) + rest * (width + kv_width) // SUB + LANES
    packed = pl.pallas_call(
        lambda *refs: pack_kernel(users, most, *refs),
        out_shape=jax.ShapeDtypeStruct((users * SUB, columns), BF16),
        in_specs=[smem, vmem, vmem, vmem],
        out_specs=vmem,
        scratch_shapes=[
            pltpu.VMEM((max(rest, 1), users * SUB, width // SUB), BF16),
            pltpu.VMEM((max(rest, 1), users * SUB, kv_width // SUB), BF16),
        ],
        compiler_params=pltpu.CompilerParams(vmem_limit_bytes=VMEM_BYTES),
        name="pack_rows",
    )(device_row_count, row_owner_user.reshape(1, per_dev), tokens, targets)
    got = lax.all_to_all(
        packed.reshape(users, SUB, columns), BOTH, split_axis=0, concat_axis=0, tiled=True
    ).reshape(whole, columns)
    share = width // devices
    tall = rank + kv_width // devices * rank // share
    down = adapter_down.T
    rows, near_frozen, near_hidden = pl.pallas_call(
        lambda *refs: near_kernel(groups, members, most, *refs),
        out_shape=[
            jax.ShapeDtypeStruct((slots, width), BF16),
            jax.ShapeDtypeStruct((slots, kv_width), F32),
            jax.ShapeDtypeStruct((slots, rank), F32),
        ],
        in_specs=[anywhere, anywhere, vmem],
        out_specs=[anywhere, vmem, vmem],
        scratch_shapes=[
            pltpu.VMEM((slots, width), BF16),
            pltpu.VMEM((max(rest, 1), whole, width // SUB), BF16),
            pltpu.VMEM((members, half, kv_width), BF16),
            pltpu.SemaphoreType.DMA((whole_groups + rest,)),
            pltpu.SemaphoreType.DMA,
            pltpu.SemaphoreType.DMA((members, groups // 2)),
        ],
        compiler_params=pltpu.CompilerParams(vmem_limit_bytes=VMEM_BYTES),
        cost_estimate=pl.CostEstimate(
            flops=slots * width * kv_width, bytes_accessed=3 * 10**7, transcendentals=0
        ),
        name="near_product",
    )(got, near, down)

    edge = tall // (2 * SUB) * SUB
    grid = (groups // 2, 2, members // 2)
    streams = [jax.ShapeDtypeStruct(grid + (size, share), F32) for size in (edge, tall - edge)]
    kept_y, kept_x, sent_y, sent_x = pl.pallas_call(
        lambda *refs: user_kernel(groups, members, most, *refs),
        out_shape=streams * 2,
        in_specs=[smem, smem, anywhere, anywhere, vmem, vmem, anywhere, vmem, vmem],
        out_specs=[vmem] * 4,
        scratch_shapes=[
            pltpu.VMEM((slots, width), BF16),
            pltpu.VMEM((slots, kv_width), BF16),
            pltpu.VMEM((max(rest, 1), whole, kv_width // SUB), BF16),
            pltpu.VMEM((whole, LANES), BF16),
            pltpu.VMEM((members, half, kv_width), BF16),
            pltpu.VMEM((slots, kv_width), F32),
            pltpu.VMEM((slots, rank), F32),
            pltpu.VMEM((rank, width), F32),
            pltpu.SemaphoreType.DMA((whole_groups + rest + 2,)),
            pltpu.SemaphoreType.DMA((members, groups // 2)),
        ],
        compiler_params=pltpu.CompilerParams(vmem_limit_bytes=VMEM_BYTES),
        name="user_steps",
    )(user_row_cap, clip_norm_bound, got, rows, near_frozen, near_hidden, far, down, adapter_up)

    first = kept_y + lax.ppermute(sent_y, "grp", swap)
    second = kept_x + lax.ppermute(sent_x, "grp", swap)
    first = halve(halve(first, "grp", 0, 2), "fsdp", 1, 1)
    second = halve(halve(second, "fsdp", 1, 1), "grp", 0, 2)
    package = jnp.concatenate([first[0, 0], second[0, 0]], axis=1)
    lines = [list(range(one, members, 2)) for one in range(2)]
    package = lax.all_to_all(
        package, "fsdp", split_axis=0, concat_axis=0, axis_index_groups=lines, tiled=True
    )
    package = jnp.sum(package, axis=0)
    clip = clip_norm_bound[0]
    update_a = package[:rank].T + clip * down_noise
    pieces = share // rank
    up_sum = package[rank:].reshape(tall - rank, pieces, rank).transpose(1, 0, 2)
    update_b = up_sum.reshape(kv_width // devices, rank).T + clip * up_noise
    return (update_a, update_b)


def solution(mesh):
    in_specs = (
        P(BOTH, None),
        P(BOTH, None),
        P(BOTH, None),
        P(BOTH),
        P(),
        P("fsdp", None),
        P(),
        P(),
        P(),
        P(BOTH, None),
        P(None, BOTH),
    )
    out_specs = (P(BOTH, None), P(None, BOTH))
    return jax.shard_map(body, mesh=mesh, in_specs=in_specs, out_specs=out_specs, check_vma=False)
```

```python
import jax
import jax.numpy as jnp
from jax import lax
from jax.experimental import pallas as pl
from jax.experimental.pallas import tpu as pltpu
from jax.sharding import PartitionSpec as P

STEPS = 2
ADAPTER_SCALE = 2.0
LEARN_RATE = 0.05
EPSILON = 1e-06

SUB = 8
LANES = 128
BOTH = ("grp", "fsdp")
VMEM_BYTES = 56 * 1024 * 1024

F32 = jnp.float32
BF16 = jnp.bfloat16


def dot(left, right, contract=((1,), (0,))):
    return lax.dot_general(left, right, (contract, ((), ())), preferred_element_type=F32)


def iota(shape, axis):
    return lax.broadcasted_iota(jnp.int32, shape, axis)


def pack_kernel(
    users, most, count_ref, owner_ref, tokens_ref, targets_ref, out_ref, cut_ref, cut_goal_ref
):
    rows = tokens_ref.shape[0]
    groups, rest = divmod(most, SUB)
    owner_row = owner_ref[...]
    first, second = (iota((rows, rows), 0), iota((rows, rows), 1))
    owner = jnp.sum(jnp.where(first == second, owner_row, 0), axis=1, keepdims=True)
    same = (owner == owner_row) & (first < second)
    rank = jnp.sum(same.astype(jnp.int32), axis=0, keepdims=True)
    line = iota((users * SUB, rows), 0)
    mine = line // SUB == owner_row
    slot = line % SUB
    picks = [mine & (rank == slot + group * SUB) for group in range(groups)]
    user = iota((users, rows), 0) == owner_row
    picks += [user & (rank == groups * SUB + extra) for extra in range(rest)]
    pick = jnp.concatenate([one.astype(BF16) for one in picks], axis=0)
    whole = users * SUB
    line, other = (iota((whole, whole), 0), iota((whole, whole), 1))
    turn = (other == line % SUB * users + line // SUB).astype(BF16)
    column = 0
    for source, cut in ((tokens_ref, cut_ref), (targets_ref, cut_goal_ref)):
        width = source.shape[1]
        piece = width // SUB
        for part in range(SUB):
            found = dot(pick, source[:, part * piece : (part + 1) * piece]).astype(BF16)
            for group in range(groups):
                spot = column + group * width + part * piece
                out_ref[:, spot : spot + piece] = found[group * whole : (group + 1) * whole]
            for extra in range(rest):
                first = groups * whole + extra * users
                cut[extra, part * users : (part + 1) * users] = found[first : first + users]
        column += groups * width
        for extra in range(rest):
            out_ref[:, column : column + piece] = dot(turn, cut[extra]).astype(BF16)
            column += piece
    used = mine & (iota((users * SUB, rows), 1) < count_ref[0])
    number = jnp.sum(used.astype(F32), axis=1, keepdims=True)
    out_ref[:, column : column + LANES] = jnp.broadcast_to(number, (users * SUB, LANES)).astype(
        BF16
    )


def weight_rings(groups, members):
    round_trip = [(at, 0) for at in range(groups // 2)]
    round_trip += [(at, 1) for at in reversed(range(groups // 2))]
    length, layers = (len(round_trip), members // 4)
    rings = []
    for core in range(2):
        up, down = ([], [])
        low, high = (list(range(length // 2)), list(range(length // 2, length)))
        for layer in range(1, layers):
            turned = layer % 2 == 0
            up += [(layer, at) for at in (low[::-1] if turned else low)]
            down += [(layer, at) for at in (high if turned else high[::-1])]
        path = [(0, at) for at in reversed(range(length))] + up + down[::-1]
        ring = []
        for layer, at in path:
            pair, inner = round_trip[(at + core * length // 2) % length]
            ring.append((2 * pair + core) * members + 2 * layer + inner)
        rings.append(ring)
    return rings


def start_weights(ring_of, groups, members, sources, target, sems):
    pairs = groups // 2
    depth = sources[0].shape[1]
    side = lax.rem(lax.axis_index("grp"), 2)
    far_end = lax.div(lax.axis_index("fsdp"), members // 2)
    rings = weight_rings(groups, members)

    def start(member):
        end, holder = divmod(member, members // 2)
        for swapped, source in enumerate(sources):

            @pl.when(far_end == (1 - end if swapped else end))
            def _():
                for pair in range(pairs):
                    spots = [
                        ring.index((2 * pair + core) * members + holder)
                        for core, ring in enumerate(rings)
                    ]
                    spot = jnp.where(side == ring_of, spots[0], spots[1])
                    pltpu.make_async_copy(
                        source.at[spot],
                        target.at[member, pl.ds(pair * depth, depth), :],
                        sems.at[member, pair],
                    ).start()

    return start


def wait_block(target, place, pairs, sems):
    depth = target.shape[1] // pairs
    for pair in range(pairs):
        block = target.at[place, pl.ds(pair * depth, depth), :]
        pltpu.make_async_copy(block, block, sems.at[place, pair]).wait()


def near_kernel(
    groups_of,
    members,
    most,
    got_ref,
    near_ref,
    near_swapped_ref,
    down_ref,
    x_out_ref,
    frozen_ref,
    hidden_ref,
    x_ref,
    cut_ref,
    w_ref,
    got_sem,
    out_sem,
    w_sem,
):
    groups, rest = divmod(most, SUB)
    devices = groups_of * members
    width = x_ref.shape[1]
    whole = devices * SUB
    half = w_ref.shape[1]
    copies = []
    column = 0
    for group in range(groups):
        copies.append(
            (got_ref.at[:, pl.ds(column, width)], x_ref.at[pl.ds(group * whole, whole), :])
        )
        column += width
    for extra in range(rest):
        copies.append((got_ref.at[:, pl.ds(column, width // SUB)], cut_ref.at[extra]))
        column += width // SUB
    copies = [
        pltpu.make_async_copy(source, target, got_sem.at[place])
        for place, (source, target) in enumerate(copies)
    ]
    for copy in copies:
        copy.start()
    start = start_weights(0, groups_of, members, (near_ref, near_swapped_ref), w_ref, w_sem)
    for member in range(members):
        if member == 2:
            for copy in copies:
                copy.wait()
        start(member)
    join_pieces(devices, groups * whole, rest, x_ref, cut_ref)
    out = pltpu.make_async_copy(x_ref, x_out_ref, out_sem)
    out.start()

    frozen_ref[...] = jnp.zeros_like(frozen_ref)
    hidden_ref[...] = jnp.zeros_like(hidden_ref)
    side = lax.rem(lax.axis_index("grp"), 2)

    def add_shard(shard, unused):
        wait_block(w_ref, shard, groups_of // 2, w_sem)
        near = pl.ds(pl.multiple_of((2 * shard + side) * half, half), half)
        both = pl.ds(pl.multiple_of(2 * shard * half, 2 * half), 2 * half)
        frozen_ref[...] += dot(x_ref[:, near], w_ref[shard])
        hidden_ref[...] += dot(x_ref[:, both], down_ref[:, both], ((1,), (1,)))
        return unused

    lax.fori_loop(0, members, add_shard, 0, unroll=4)
    out.wait()


def join_pieces(devices, bottom, rest, full, cut):
    whole = devices * SUB
    line, other = (iota((whole, whole), 0), iota((whole, whole), 1))
    turn = (other == line % devices * SUB + line // devices).astype(BF16)
    piece = full.shape[1] // SUB
    for extra in range(rest):
        first = bottom + extra * devices
        rows = dot(turn, cut[extra]).astype(BF16)
        for part in range(SUB):
            full[first : first + devices, part * piece : (part + 1) * piece] = rows[
                part * devices : (part + 1) * devices
            ]


def user_kernel(
    groups_of,
    members,
    most,
    cap_ref,
    clip_ref,
    got_ref,
    rows_ref,
    near_frozen_ref,
    near_hidden_ref,
    far_ref,
    far_swapped_ref,
    down_ref,
    up_ref,
    *refs,
):
    keep_refs, send_refs = (refs[0:2], refs[2:4])
    (
        x_ref,
        goal_ref,
        cut_goal_ref,
        used_ref,
        w_ref,
        frozen_ref,
        hidden_ref,
        delta_ref,
        got_sem,
        w_sem,
    ) = refs[4:]
    groups, rest = divmod(most, SUB)
    devices = groups_of * members
    rank, width = down_ref.shape
    kv_width = up_ref.shape[1]
    whole = devices * SUB
    half = w_ref.shape[1]
    copies = [(rows_ref, x_ref)]
    column = groups * width + rest * width // SUB
    for group in range(groups):
        copies.append(
            (got_ref.at[:, pl.ds(column, kv_width)], goal_ref.at[pl.ds(group * whole, whole), :])
        )
        column += kv_width
    for extra in range(rest):
        copies.append((got_ref.at[:, pl.ds(column, kv_width // SUB)], cut_goal_ref.at[extra]))
        column += kv_width // SUB
    copies.append((got_ref.at[:, pl.ds(column, LANES)], used_ref))
    copies = [
        pltpu.make_async_copy(source, target, got_sem.at[place])
        for place, (source, target) in enumerate(copies)
    ]
    for copy in copies[1:] + copies[:1]:
        copy.start()
    start = start_weights(1, groups_of, members, (far_ref, far_swapped_ref), w_ref, w_sem)
    for member in range(members):
        start(member)
    for copy in copies[1:]:
        copy.wait()
    join_pieces(devices, groups * whole, rest, goal_ref, cut_goal_ref)

    cap = cap_ref[lax.axis_index("grp") * members + lax.axis_index("fsdp")].astype(F32)
    used = used_ref[...]
    pieces = []
    if groups:
        line, other = (iota((whole, whole), 0), iota((whole, whole), 1))
        earlier = dot(((other // SUB < line // SUB) & (other % SUB == 0)).astype(BF16), used)
        own = used.astype(F32)
        for group in range(groups):
            spot = (iota((whole, LANES), 0) % SUB + group * SUB).astype(F32)
            live = (spot < own) & (earlier + spot < cap)
            pieces.append(jnp.where(live, 1.0 / cap, 0.0)[:, :1])
    line, other = (iota((devices, whole), 0), iota((devices, whole), 1))
    earlier = dot((other < line * SUB).astype(BF16) * (other % SUB == 0).astype(BF16), used)
    own = dot((other == line * SUB).astype(BF16), used)
    for extra in range(rest):
        spot = float(groups * SUB + extra)
        live = (own > spot) & (earlier + spot < cap)
        pieces.append(jnp.where(live, 1.0 / cap, 0.0)[:, :1])
    scale = jnp.concatenate(pieces, axis=0) if len(pieces) > 1 else pieces[0]

    frozen_ref[...] = near_frozen_ref[...]
    hidden_ref[...] = near_hidden_ref[...]
    side = lax.rem(lax.axis_index("grp"), 2)
    copies[0].wait()

    def add_shard(shard, unused):
        wait_block(w_ref, shard, groups_of // 2, w_sem)
        far = pl.ds(pl.multiple_of((2 * shard + 1 - side) * half, half), half)
        frozen_ref[...] += dot(x_ref[:, far], w_ref[shard])
        return unused

    lax.fori_loop(0, members, add_shard, 0, unroll=4)

    rate = ADAPTER_SCALE * LEARN_RATE
    block = min(width, 1024)
    up = up_ref[...].astype(F32)
    up_half = up_ref[...]
    up_delta = jnp.zeros((rank, kv_width), F32)
    for step in range(STEPS):
        hidden = hidden_ref[...].astype(BF16)
        error = frozen_ref[...] + ADAPTER_SCALE * dot(hidden, up_half) - goal_ref[...].astype(F32)
        residual = (scale * error).astype(BF16)
        back = dot(residual, up_half, ((1,), (1,))).astype(BF16)
        up_delta = up_delta - rate * dot(hidden, residual, ((0,), (0,)))
        last = step == STEPS - 1
        if not last:
            up_half = (up + up_delta).astype(BF16)
            hidden_ref[...] = jnp.zeros_like(hidden_ref)

        def down_block(at, unused):
            lanes = pl.ds(pl.multiple_of(at * block, block), block)
            moved = -rate * dot(back, x_ref[:, lanes], ((0,), (0,)))
            if step:
                moved = moved + delta_ref[:, lanes]
            delta_ref[:, lanes] = moved
            if not last:
                half_down = (down_ref[:, lanes].astype(F32) + moved).astype(BF16)
                hidden_ref[...] += dot(x_ref[:, lanes], half_down, ((1,), (1,)))
                return unused
            square = moved * moved
            for at in range(0, block, LANES):
                unused = unused + square[:, at : at + LANES]
            return unused

        squares = lax.fori_loop(
            0, width // block, down_block, jnp.zeros((rank, LANES), F32), unroll=4
        )

    total = jnp.sum(squares) + jnp.sum(up_delta * up_delta) + EPSILON
    total = jnp.full((1, LANES), total, F32)
    factor = jnp.minimum(1.0, clip_ref[0] / jnp.sqrt(total))[:, :1]
    share = width // devices
    up_share = kv_width // devices
    up_turned = (factor * up_delta).T
    pieces = share // rank
    tall = up_share // pieces

    def write(core, targets):
        edge = targets[0].shape[3]
        for pair in range(devices // members // 2):
            for member in range(members):
                device = (2 * pair + core) * members + member
                spot = lax.bitwise_xor(lax.div(lax.axis_index("grp"), 2), pair)
                inner = lax.bitwise_xor(lax.rem(lax.axis_index("fsdp"), 2), member % 2)
                outer = member // 2
                moved = factor * delta_ref[:, device * share : (device + 1) * share]
                targets[0][spot, inner, outer] = moved[:edge]
                targets[1][spot, inner, outer, : rank - edge, :] = moved[edge:]
                first = device * up_share
                parts = [
                    up_turned[first + at * tall : first + (at + 1) * tall] for at in range(pieces)
                ]
                targets[1][spot, inner, outer, rank - edge :, :] = (
                    jnp.concatenate(parts, axis=1) if pieces > 1 else parts[0]
                )

    for core in range(2):
        mine = side == core

        @pl.when(mine)
        def _():
            write(core, keep_refs)

        @pl.when(jnp.logical_not(mine))
        def _():
            write(core, send_refs)


def halve(package, axis, bits, partner):
    bit = package.shape[bits] // 2
    while bit:
        keep = lax.slice_in_dim(package, 0, bit, axis=bits)
        send = lax.slice_in_dim(package, bit, 2 * bit, axis=bits)
        pairs = [(at, at ^ (partner * bit)) for at in range(lax.axis_size(axis))]
        package = lax.ppermute(send, axis, pairs) + keep
        bit //= 2
    return package


def body(
    tokens,
    targets,
    row_owner_user,
    device_row_count,
    user_row_cap,
    value_weight,
    adapter_down,
    adapter_up,
    clip_norm_bound,
    down_noise,
    up_noise,
):
    groups, members = (lax.axis_size("grp"), lax.axis_size("fsdp"))
    devices = groups * members
    side = lax.axis_index("grp") % 2
    per_dev, width = tokens.shape
    kv_width = targets.shape[1]
    rank = adapter_down.shape[1]
    users = user_row_cap.shape[0]
    most = 3 * per_dev // (2 * devices)
    slots = devices * most
    whole = devices * SUB
    whole_groups, rest = divmod(most, SUB)
    smem = pl.BlockSpec(memory_space=pltpu.SMEM)
    vmem = pl.BlockSpec(memory_space=pltpu.VMEM)
    anywhere = pl.BlockSpec(memory_space=pl.ANY)

    half = value_weight.shape[0] // 2
    depth = half // (groups // 2)
    pair = lax.axis_index("grp") // 2
    mine = lax.dynamic_slice_in_dim(value_weight, side * half + pair * depth, depth, axis=0)
    across = [(at, at ^ (members // 2)) for at in range(members)]
    swapped = lax.ppermute(mine, "fsdp", across)
    rings = weight_rings(groups, members)
    rings += [[at + members // 2 for at in ring] for ring in rings]
    swap = [(at, at ^ 1) for at in range(groups)]

    columns = whole_groups * (width + kv_width) + rest * (width + kv_width) // SUB + LANES
    packed = pl.pallas_call(
        lambda *refs: pack_kernel(users, most, *refs),
        out_shape=jax.ShapeDtypeStruct((users * SUB, columns), BF16),
        in_specs=[smem, vmem, vmem, vmem],
        out_specs=vmem,
        scratch_shapes=[
            pltpu.VMEM((max(rest, 1), users * SUB, width // SUB), BF16),
            pltpu.VMEM((max(rest, 1), users * SUB, kv_width // SUB), BF16),
        ],
        compiler_params=pltpu.CompilerParams(vmem_limit_bytes=VMEM_BYTES),
        name="pack_rows",
    )(device_row_count, row_owner_user.reshape(1, per_dev), tokens, targets)
    near = lax.all_gather(mine, BOTH, axis=0, axis_index_groups=rings)
    packed, swapped = lax.optimization_barrier((packed, swapped))
    near_swapped = lax.all_gather(swapped, BOTH, axis=0, axis_index_groups=rings)
    far = lax.ppermute(near, "grp", swap)
    far_swapped = lax.ppermute(near_swapped, "grp", swap)
    got = lax.all_to_all(
        packed.reshape(users, SUB, columns), BOTH, split_axis=0, concat_axis=0, tiled=True
    ).reshape(whole, columns)
    share = width // devices
    tall = rank + kv_width // devices * rank // share
    down = adapter_down.T
    rows, near_frozen, near_hidden = pl.pallas_call(
        lambda *refs: near_kernel(groups, members, most, *refs),
        out_shape=[
            jax.ShapeDtypeStruct((slots, width), BF16),
            jax.ShapeDtypeStruct((slots, kv_width), F32),
            jax.ShapeDtypeStruct((slots, rank), F32),
        ],
        in_specs=[anywhere, anywhere, anywhere, vmem],
        out_specs=[anywhere, vmem, vmem],
        scratch_shapes=[
            pltpu.VMEM((slots, width), BF16),
            pltpu.VMEM((max(rest, 1), whole, width // SUB), BF16),
            pltpu.VMEM((members, half, kv_width), BF16),
            pltpu.SemaphoreType.DMA((whole_groups + rest,)),
            pltpu.SemaphoreType.DMA,
            pltpu.SemaphoreType.DMA((members, groups // 2)),
        ],
        compiler_params=pltpu.CompilerParams(vmem_limit_bytes=VMEM_BYTES),
        cost_estimate=pl.CostEstimate(
            flops=slots * width * kv_width, bytes_accessed=3 * 10**7, transcendentals=0
        ),
        name="near_product",
    )(got, near, near_swapped, down)

    edge = tall // (2 * SUB) * SUB
    grid = (groups // 2, 2, members // 2)
    streams = [jax.ShapeDtypeStruct(grid + (size, share), F32) for size in (edge, tall - edge)]
    kept_y, kept_x, sent_y, sent_x = pl.pallas_call(
        lambda *refs: user_kernel(groups, members, most, *refs),
        out_shape=streams * 2,
        in_specs=[smem] * 2 + [anywhere] * 2 + [vmem] * 2 + [anywhere] * 2 + [vmem] * 2,
        out_specs=[vmem] * 4,
        scratch_shapes=[
            pltpu.VMEM((slots, width), BF16),
            pltpu.VMEM((slots, kv_width), BF16),
            pltpu.VMEM((max(rest, 1), whole, kv_width // SUB), BF16),
            pltpu.VMEM((whole, LANES), BF16),
            pltpu.VMEM((members, half, kv_width), BF16),
            pltpu.VMEM((slots, kv_width), F32),
            pltpu.VMEM((slots, rank), F32),
            pltpu.VMEM((rank, width), F32),
            pltpu.SemaphoreType.DMA((whole_groups + rest + 2,)),
            pltpu.SemaphoreType.DMA((members, groups // 2)),
        ],
        compiler_params=pltpu.CompilerParams(vmem_limit_bytes=VMEM_BYTES),
        name="user_steps",
    )(
        user_row_cap,
        clip_norm_bound,
        got,
        rows,
        near_frozen,
        near_hidden,
        far,
        far_swapped,
        down,
        adapter_up,
    )

    first = kept_y + lax.ppermute(sent_y, "grp", swap)
    second = kept_x + lax.ppermute(sent_x, "grp", swap)
    first = halve(halve(first, "grp", 0, 2), "fsdp", 1, 1)
    second = halve(halve(second, "fsdp", 1, 1), "grp", 0, 2)
    package = jnp.concatenate([first[0, 0], second[0, 0]], axis=1)
    lines = [list(range(one, members, 2)) for one in range(2)]
    package = lax.all_to_all(
        package, "fsdp", split_axis=0, concat_axis=0, axis_index_groups=lines, tiled=True
    )
    package = jnp.sum(package, axis=0)
    clip = clip_norm_bound[0]
    update_a = package[:rank].T + clip * down_noise
    pieces = share // rank
    up_sum = package[rank:].reshape(tall - rank, pieces, rank).transpose(1, 0, 2)
    update_b = up_sum.reshape(kv_width // devices, rank).T + clip * up_noise
    return (update_a, update_b)


def solution(mesh):
    in_specs = (
        P(BOTH, None),
        P(BOTH, None),
        P(BOTH, None),
        P(BOTH),
        P(),
        P("fsdp", None),
        P(),
        P(),
        P(),
        P(BOTH, None),
        P(None, BOTH),
    )
    out_specs = (P(BOTH, None), P(None, BOTH))
    return jax.shard_map(body, mesh=mesh, in_specs=in_specs, out_specs=out_specs, check_vma=False)
```

```python
import jax
import jax.numpy as jnp
from jax import lax
from jax.experimental import pallas as pl
from jax.experimental.pallas import tpu as pltpu
from jax.sharding import PartitionSpec as P

STEPS = 2
ADAPTER_SCALE = 2.0
LEARN_RATE = 0.05
EPSILON = 1e-06

SUB = 8
LANES = 128
BOTH = ("grp", "fsdp")
VMEM_BYTES = 56 * 1024 * 1024

F32 = jnp.float32
BF16 = jnp.bfloat16


def dot(left, right, contract=((1,), (0,))):
    return lax.dot_general(left, right, (contract, ((), ())), preferred_element_type=F32)


def iota(shape, axis):
    return lax.broadcasted_iota(jnp.int32, shape, axis)


def pack_kernel(
    users, most, count_ref, owner_ref, tokens_ref, targets_ref, out_ref, cut_ref, cut_goal_ref
):
    rows = tokens_ref.shape[0]
    groups, rest = divmod(most, SUB)
    owner_row = owner_ref[...]
    first, second = (iota((rows, rows), 0), iota((rows, rows), 1))
    owner = jnp.sum(jnp.where(first == second, owner_row, 0), axis=1, keepdims=True)
    same = (owner == owner_row) & (first < second)
    rank = jnp.sum(same.astype(jnp.int32), axis=0, keepdims=True)
    line = iota((users * SUB, rows), 0)
    mine = line // SUB == owner_row
    slot = line % SUB
    picks = [mine & (rank == slot + group * SUB) for group in range(groups)]
    user = iota((users, rows), 0) == owner_row
    picks += [user & (rank == groups * SUB + extra) for extra in range(rest)]
    pick = jnp.concatenate([one.astype(BF16) for one in picks], axis=0)
    whole = users * SUB
    line, other = (iota((whole, whole), 0), iota((whole, whole), 1))
    turn = (other == line % SUB * users + line // SUB).astype(BF16)
    column = 0
    for source, cut in ((tokens_ref, cut_ref), (targets_ref, cut_goal_ref)):
        width = source.shape[1]
        piece = width // SUB
        for part in range(SUB):
            found = dot(pick, source[:, part * piece : (part + 1) * piece]).astype(BF16)
            for group in range(groups):
                spot = column + group * width + part * piece
                out_ref[:, spot : spot + piece] = found[group * whole : (group + 1) * whole]
            for extra in range(rest):
                first = groups * whole + extra * users
                cut[extra, part * users : (part + 1) * users] = found[first : first + users]
        column += groups * width
        for extra in range(rest):
            out_ref[:, column : column + piece] = dot(turn, cut[extra]).astype(BF16)
            column += piece
    used = mine & (iota((users * SUB, rows), 1) < count_ref[0])
    number = jnp.sum(used.astype(F32), axis=1, keepdims=True)
    out_ref[:, column : column + LANES] = jnp.broadcast_to(number, (users * SUB, LANES)).astype(
        BF16
    )


def weight_rings(groups, members):
    round_trip = [(at, 0) for at in range(groups // 2)]
    round_trip += [(at, 1) for at in reversed(range(groups // 2))]
    length, layers = (len(round_trip), members // 4)
    rings = []
    for core in range(2):
        up, down = ([], [])
        low, high = (list(range(length // 2)), list(range(length // 2, length)))
        for layer in range(1, layers):
            turned = layer % 2 == 0
            up += [(layer, at) for at in (low[::-1] if turned else low)]
            down += [(layer, at) for at in (high if turned else high[::-1])]
        path = [(0, at) for at in reversed(range(length))] + up + down[::-1]
        ring = []
        for layer, at in path:
            pair, inner = round_trip[(at + core * length // 2) % length]
            ring.append((2 * pair + core) * members + 2 * layer + inner)
        rings.append(ring)
    return rings


def start_weights(ring_of, groups, members, sources, target, sems):
    pairs = groups // 2
    depth = sources[0].shape[1]
    side = lax.rem(lax.axis_index("grp"), 2)
    far_end = lax.div(lax.axis_index("fsdp"), members // 2)
    rings = weight_rings(groups, members)

    def start(member):
        end, holder = divmod(member, members // 2)
        for swapped, source in enumerate(sources):

            @pl.when(far_end == (1 - end if swapped else end))
            def _():
                for pair in range(pairs):
                    spots = [
                        ring.index((2 * pair + core) * members + holder)
                        for core, ring in enumerate(rings)
                    ]
                    spot = jnp.where(side == ring_of, spots[0], spots[1])
                    pltpu.make_async_copy(
                        source.at[spot],
                        target.at[member, pl.ds(pair * depth, depth), :],
                        sems.at[member, pair],
                    ).start()

    return start


def wait_block(target, place, pairs, sems):
    depth = target.shape[1] // pairs
    for pair in range(pairs):
        block = target.at[place, pl.ds(pair * depth, depth), :]
        pltpu.make_async_copy(block, block, sems.at[place, pair]).wait()


def near_kernel(
    groups_of,
    members,
    most,
    got_ref,
    near_ref,
    near_swapped_ref,
    down_ref,
    x_out_ref,
    frozen_ref,
    hidden_ref,
    x_ref,
    cut_ref,
    w_ref,
    got_sem,
    out_sem,
    w_sem,
):
    groups, rest = divmod(most, SUB)
    devices = groups_of * members
    width = x_ref.shape[1]
    whole = devices * SUB
    half = w_ref.shape[1]
    copies = []
    column = 0
    for group in range(groups):
        copies.append(
            (got_ref.at[:, pl.ds(column, width)], x_ref.at[pl.ds(group * whole, whole), :])
        )
        column += width
    for extra in range(rest):
        copies.append((got_ref.at[:, pl.ds(column, width // SUB)], cut_ref.at[extra]))
        column += width // SUB
    copies = [
        pltpu.make_async_copy(source, target, got_sem.at[place])
        for place, (source, target) in enumerate(copies)
    ]
    for copy in copies:
        copy.start()
    start = start_weights(0, groups_of, members, (near_ref, near_swapped_ref), w_ref, w_sem)
    for member in range(members):
        if member == 2:
            for copy in copies:
                copy.wait()
        start(member)
    join_pieces(devices, groups * whole, rest, x_ref, cut_ref)
    out = pltpu.make_async_copy(x_ref, x_out_ref, out_sem)
    out.start()

    frozen_ref[...] = jnp.zeros_like(frozen_ref)
    hidden_ref[...] = jnp.zeros_like(hidden_ref)
    side = lax.rem(lax.axis_index("grp"), 2)

    def add_shard(shard, unused):
        wait_block(w_ref, shard, groups_of // 2, w_sem)
        near = pl.ds(pl.multiple_of((2 * shard + side) * half, half), half)
        both = pl.ds(pl.multiple_of(2 * shard * half, 2 * half), 2 * half)
        frozen_ref[...] += dot(x_ref[:, near], w_ref[shard])
        hidden_ref[...] += dot(x_ref[:, both], down_ref[:, both], ((1,), (1,)))
        return unused

    lax.fori_loop(0, members, add_shard, 0, unroll=8)
    out.wait()


def join_pieces(devices, bottom, rest, full, cut):
    whole = devices * SUB
    line, other = (iota((whole, whole), 0), iota((whole, whole), 1))
    turn = (other == line % devices * SUB + line // devices).astype(BF16)
    piece = full.shape[1] // SUB
    for extra in range(rest):
        first = bottom + extra * devices
        rows = dot(turn, cut[extra]).astype(BF16)
        for part in range(SUB):
            full[first : first + devices, part * piece : (part + 1) * piece] = rows[
                part * devices : (part + 1) * devices
            ]


def user_kernel(
    groups_of,
    members,
    most,
    cap_ref,
    clip_ref,
    got_ref,
    rows_ref,
    near_frozen_ref,
    near_hidden_ref,
    far_ref,
    far_swapped_ref,
    down_ref,
    up_ref,
    *refs,
):
    keep_refs, send_refs = (refs[0:2], refs[2:4])
    (
        x_ref,
        goal_ref,
        cut_goal_ref,
        used_ref,
        w_ref,
        frozen_ref,
        hidden_ref,
        delta_ref,
        got_sem,
        w_sem,
    ) = refs[4:]
    groups, rest = divmod(most, SUB)
    devices = groups_of * members
    rank, width = down_ref.shape
    kv_width = up_ref.shape[1]
    whole = devices * SUB
    half = w_ref.shape[1]
    copies = [(rows_ref, x_ref)]
    column = groups * width + rest * width // SUB
    for group in range(groups):
        copies.append(
            (got_ref.at[:, pl.ds(column, kv_width)], goal_ref.at[pl.ds(group * whole, whole), :])
        )
        column += kv_width
    for extra in range(rest):
        copies.append((got_ref.at[:, pl.ds(column, kv_width // SUB)], cut_goal_ref.at[extra]))
        column += kv_width // SUB
    copies.append((got_ref.at[:, pl.ds(column, LANES)], used_ref))
    copies = [
        pltpu.make_async_copy(source, target, got_sem.at[place])
        for place, (source, target) in enumerate(copies)
    ]
    for copy in copies[1:] + copies[:1]:
        copy.start()
    start = start_weights(1, groups_of, members, (far_ref, far_swapped_ref), w_ref, w_sem)
    for member in range(members):
        start(member)
    for copy in copies[1:]:
        copy.wait()
    join_pieces(devices, groups * whole, rest, goal_ref, cut_goal_ref)

    cap = cap_ref[lax.axis_index("grp") * members + lax.axis_index("fsdp")].astype(F32)
    used = used_ref[...]
    pieces = []
    if groups:
        line, other = (iota((whole, whole), 0), iota((whole, whole), 1))
        earlier = dot(((other // SUB < line // SUB) & (other % SUB == 0)).astype(BF16), used)
        own = used.astype(F32)
        for group in range(groups):
            spot = (iota((whole, LANES), 0) % SUB + group * SUB).astype(F32)
            live = (spot < own) & (earlier + spot < cap)
            pieces.append(jnp.where(live, 1.0 / cap, 0.0)[:, :1])
    line, other = (iota((devices, whole), 0), iota((devices, whole), 1))
    earlier = dot((other < line * SUB).astype(BF16) * (other % SUB == 0).astype(BF16), used)
    own = dot((other == line * SUB).astype(BF16), used)
    for extra in range(rest):
        spot = float(groups * SUB + extra)
        live = (own > spot) & (earlier + spot < cap)
        pieces.append(jnp.where(live, 1.0 / cap, 0.0)[:, :1])
    scale = jnp.concatenate(pieces, axis=0) if len(pieces) > 1 else pieces[0]

    frozen_ref[...] = near_frozen_ref[...]
    hidden_ref[...] = near_hidden_ref[...]
    side = lax.rem(lax.axis_index("grp"), 2)
    copies[0].wait()

    def add_shard(shard, unused):
        wait_block(w_ref, shard, groups_of // 2, w_sem)
        far = pl.ds(pl.multiple_of((2 * shard + 1 - side) * half, half), half)
        frozen_ref[...] += dot(x_ref[:, far], w_ref[shard])
        return unused

    lax.fori_loop(0, members, add_shard, 0, unroll=8)

    rate = ADAPTER_SCALE * LEARN_RATE
    block = min(width, 1024)
    up = up_ref[...].astype(F32)
    up_half = up_ref[...]
    up_delta = jnp.zeros((rank, kv_width), F32)
    for step in range(STEPS):
        hidden = hidden_ref[...].astype(BF16)
        error = frozen_ref[...] + ADAPTER_SCALE * dot(hidden, up_half) - goal_ref[...].astype(F32)
        residual = (scale * error).astype(BF16)
        back = dot(residual, up_half, ((1,), (1,))).astype(BF16)
        up_delta = up_delta - rate * dot(hidden, residual, ((0,), (0,)))
        last = step == STEPS - 1
        if not last:
            up_half = (up + up_delta).astype(BF16)
            hidden_ref[...] = jnp.zeros_like(hidden_ref)

        def down_block(at, unused):
            lanes = pl.ds(pl.multiple_of(at * block, block), block)
            moved = -rate * dot(back, x_ref[:, lanes], ((0,), (0,)))
            if step:
                moved = moved + delta_ref[:, lanes]
            delta_ref[:, lanes] = moved
            if not last:
                half_down = (down_ref[:, lanes].astype(F32) + moved).astype(BF16)
                hidden_ref[...] += dot(x_ref[:, lanes], half_down, ((1,), (1,)))
                return unused
            square = moved * moved
            for at in range(0, block, LANES):
                unused = unused + square[:, at : at + LANES]
            return unused

        squares = lax.fori_loop(
            0, width // block, down_block, jnp.zeros((rank, LANES), F32), unroll=8
        )

    total = jnp.sum(squares) + jnp.sum(up_delta * up_delta) + EPSILON
    total = jnp.full((1, LANES), total, F32)
    factor = jnp.minimum(1.0, clip_ref[0] / jnp.sqrt(total))[:, :1]
    share = width // devices
    up_share = kv_width // devices
    up_turned = (factor * up_delta).T
    pieces = share // rank
    tall = up_share // pieces

    def write(core, targets):
        edge = targets[0].shape[3]
        for pair in range(devices // members // 2):
            for member in range(members):
                device = (2 * pair + core) * members + member
                spot = lax.bitwise_xor(lax.div(lax.axis_index("grp"), 2), pair)
                inner = lax.bitwise_xor(lax.rem(lax.axis_index("fsdp"), 2), member % 2)
                outer = member // 2
                moved = factor * delta_ref[:, device * share : (device + 1) * share]
                targets[0][spot, inner, outer] = moved[:edge]
                targets[1][spot, inner, outer, : rank - edge, :] = moved[edge:]
                first = device * up_share
                parts = [
                    up_turned[first + at * tall : first + (at + 1) * tall] for at in range(pieces)
                ]
                targets[1][spot, inner, outer, rank - edge :, :] = (
                    jnp.concatenate(parts, axis=1) if pieces > 1 else parts[0]
                )

    for core in range(2):
        mine = side == core

        @pl.when(mine)
        def _():
            write(core, keep_refs)

        @pl.when(jnp.logical_not(mine))
        def _():
            write(core, send_refs)


def halve(terms, axis, bits, partner):
    bit = terms[0].shape[bits] // 2
    while bit:
        send = sum(lax.slice_in_dim(term, bit, 2 * bit, axis=bits) for term in terms)
        pairs = [(at, at ^ (partner * bit)) for at in range(lax.axis_size(axis))]
        sent = lax.ppermute(send, axis, pairs)
        terms = [lax.slice_in_dim(term, 0, bit, axis=bits) for term in terms] + [sent]
        bit //= 2
    return terms


def body(
    tokens,
    targets,
    row_owner_user,
    device_row_count,
    user_row_cap,
    value_weight,
    adapter_down,
    adapter_up,
    clip_norm_bound,
    down_noise,
    up_noise,
):
    groups, members = (lax.axis_size("grp"), lax.axis_size("fsdp"))
    devices = groups * members
    side = lax.axis_index("grp") % 2
    per_dev, width = tokens.shape
    kv_width = targets.shape[1]
    rank = adapter_down.shape[1]
    users = user_row_cap.shape[0]
    most = 3 * per_dev // (2 * devices)
    slots = devices * most
    whole = devices * SUB
    whole_groups, rest = divmod(most, SUB)
    smem = pl.BlockSpec(memory_space=pltpu.SMEM)
    vmem = pl.BlockSpec(memory_space=pltpu.VMEM)
    anywhere = pl.BlockSpec(memory_space=pl.ANY)

    half = value_weight.shape[0] // 2
    depth = half // (groups // 2)
    pair = lax.axis_index("grp") // 2
    mine = lax.dynamic_slice_in_dim(value_weight, side * half + pair * depth, depth, axis=0)
    across = [(at, at ^ (members // 2)) for at in range(members)]
    swapped = lax.ppermute(mine, "fsdp", across)
    rings = weight_rings(groups, members)
    rings += [[at + members // 2 for at in ring] for ring in rings]
    swap = [(at, at ^ 1) for at in range(groups)]

    columns = whole_groups * (width + kv_width) + rest * (width + kv_width) // SUB + LANES
    packed = pl.pallas_call(
        lambda *refs: pack_kernel(users, most, *refs),
        out_shape=jax.ShapeDtypeStruct((users * SUB, columns), BF16),
        in_specs=[smem, vmem, vmem, vmem],
        out_specs=vmem,
        scratch_shapes=[
            pltpu.VMEM((max(rest, 1), users * SUB, width // SUB), BF16),
            pltpu.VMEM((max(rest, 1), users * SUB, kv_width // SUB), BF16),
        ],
        compiler_params=pltpu.CompilerParams(vmem_limit_bytes=VMEM_BYTES),
        name="pack_rows",
    )(device_row_count, row_owner_user.reshape(1, per_dev), tokens, targets)
    near = lax.all_gather(mine, BOTH, axis=0, axis_index_groups=rings)
    packed, swapped = lax.optimization_barrier((packed, swapped))
    near_swapped = lax.all_gather(swapped, BOTH, axis=0, axis_index_groups=rings)
    far = lax.ppermute(near, "grp", swap)
    far_swapped = lax.ppermute(near_swapped, "grp", swap)
    got = lax.all_to_all(
        packed.reshape(users, SUB, columns), BOTH, split_axis=0, concat_axis=0, tiled=True
    ).reshape(whole, columns)
    share = width // devices
    tall = rank + kv_width // devices * rank // share
    down = adapter_down.T
    rows, near_frozen, near_hidden = pl.pallas_call(
        lambda *refs: near_kernel(groups, members, most, *refs),
        out_shape=[
            jax.ShapeDtypeStruct((slots, width), BF16),
            jax.ShapeDtypeStruct((slots, kv_width), F32),
            jax.ShapeDtypeStruct((slots, rank), F32),
        ],
        in_specs=[anywhere, anywhere, anywhere, vmem],
        out_specs=[anywhere, vmem, vmem],
        scratch_shapes=[
            pltpu.VMEM((slots, width), BF16),
            pltpu.VMEM((max(rest, 1), whole, width // SUB), BF16),
            pltpu.VMEM((members, half, kv_width), BF16),
            pltpu.SemaphoreType.DMA((whole_groups + rest,)),
            pltpu.SemaphoreType.DMA,
            pltpu.SemaphoreType.DMA((members, groups // 2)),
        ],
        compiler_params=pltpu.CompilerParams(vmem_limit_bytes=VMEM_BYTES),
        cost_estimate=pl.CostEstimate(
            flops=slots * width * kv_width, bytes_accessed=3 * 10**7, transcendentals=0
        ),
        name="near_product",
    )(got, near, near_swapped, down)

    edge = tall // (2 * SUB) * SUB
    grid = (groups // 2, 2, members // 2)
    streams = [jax.ShapeDtypeStruct(grid + (size, share), F32) for size in (edge, tall - edge)]
    kept_y, kept_x, sent_y, sent_x = pl.pallas_call(
        lambda *refs: user_kernel(groups, members, most, *refs),
        out_shape=streams * 2,
        in_specs=[smem] * 2 + [anywhere] * 2 + [vmem] * 2 + [anywhere] * 2 + [vmem] * 2,
        out_specs=[vmem] * 4,
        scratch_shapes=[
            pltpu.VMEM((slots, width), BF16),
            pltpu.VMEM((slots, kv_width), BF16),
            pltpu.VMEM((max(rest, 1), whole, kv_width // SUB), BF16),
            pltpu.VMEM((whole, LANES), BF16),
            pltpu.VMEM((members, half, kv_width), BF16),
            pltpu.VMEM((slots, kv_width), F32),
            pltpu.VMEM((slots, rank), F32),
            pltpu.VMEM((rank, width), F32),
            pltpu.SemaphoreType.DMA((whole_groups + rest + 2,)),
            pltpu.SemaphoreType.DMA((members, groups // 2)),
        ],
        compiler_params=pltpu.CompilerParams(vmem_limit_bytes=VMEM_BYTES),
        name="user_steps",
    )(
        user_row_cap,
        clip_norm_bound,
        got,
        rows,
        near_frozen,
        near_hidden,
        far,
        far_swapped,
        down,
        adapter_up,
    )

    first = [kept_y, lax.ppermute(sent_y, "grp", swap)]
    second = [kept_x, lax.ppermute(sent_x, "grp", swap)]
    first = sum(halve(halve(first, "grp", 0, 2), "fsdp", 1, 1))
    second = sum(halve(halve(second, "fsdp", 1, 1), "grp", 0, 2))
    package = jnp.concatenate([first[0, 0], second[0, 0]], axis=1)
    lines = [list(range(one, members, 2)) for one in range(2)]
    package = lax.all_to_all(
        package, "fsdp", split_axis=0, concat_axis=0, axis_index_groups=lines, tiled=True
    )
    package = jnp.sum(package, axis=0)
    clip = clip_norm_bound[0]
    update_a = package[:rank].T + clip * down_noise
    pieces = share // rank
    up_sum = package[rank:].reshape(tall - rank, pieces, rank).transpose(1, 0, 2)
    update_b = up_sum.reshape(kv_width // devices, rank).T + clip * up_noise
    return (update_a, update_b)


def solution(mesh):
    in_specs = (
        P(BOTH, None),
        P(BOTH, None),
        P(BOTH, None),
        P(BOTH),
        P(),
        P("fsdp", None),
        P(),
        P(),
        P(),
        P(BOTH, None),
        P(None, BOTH),
    )
    out_specs = (P(BOTH, None), P(None, BOTH))
    return jax.shard_map(body, mesh=mesh, in_specs=in_specs, out_specs=out_specs, check_vma=False)
```

```python
import jax
import jax.numpy as jnp
from jax import lax
from jax.experimental import pallas as pl
from jax.experimental.pallas import tpu as pltpu
from jax.sharding import PartitionSpec as P

STEPS = 2
ADAPTER_SCALE = 2.0
LEARN_RATE = 0.05
EPSILON = 1e-06

SUB = 8
LANES = 128
BOTH = ("grp", "fsdp")
VMEM_BYTES = 56 * 1024 * 1024

F32 = jnp.float32
BF16 = jnp.bfloat16


def dot(left, right, contract=((1,), (0,))):
    return lax.dot_general(left, right, (contract, ((), ())), preferred_element_type=F32)


def iota(shape, axis):
    return lax.broadcasted_iota(jnp.int32, shape, axis)


def pack_kernel(
    users, most, count_ref, owner_ref, tokens_ref, targets_ref, out_ref, cut_ref, cut_goal_ref
):
    rows = tokens_ref.shape[0]
    groups, rest = divmod(most, SUB)
    owner_row = owner_ref[...]
    first, second = (iota((rows, rows), 0), iota((rows, rows), 1))
    owner = jnp.sum(jnp.where(first == second, owner_row, 0), axis=1, keepdims=True)
    same = (owner == owner_row) & (first < second)
    rank = jnp.sum(same.astype(jnp.int32), axis=0, keepdims=True)
    line = iota((users * SUB, rows), 0)
    mine = line // SUB == owner_row
    slot = line % SUB
    picks = [mine & (rank == slot + group * SUB) for group in range(groups)]
    user = iota((users, rows), 0) == owner_row
    picks += [user & (rank == groups * SUB + extra) for extra in range(rest)]
    pick = jnp.concatenate([one.astype(BF16) for one in picks], axis=0)
    whole = users * SUB
    line, other = (iota((whole, whole), 0), iota((whole, whole), 1))
    turn = (other == line % SUB * users + line // SUB).astype(BF16)
    column = 0
    for source, cut in ((tokens_ref, cut_ref), (targets_ref, cut_goal_ref)):
        width = source.shape[1]
        piece = width // SUB
        for part in range(SUB):
            found = dot(pick, source[:, part * piece : (part + 1) * piece]).astype(BF16)
            for group in range(groups):
                spot = column + group * width + part * piece
                out_ref[:, spot : spot + piece] = found[group * whole : (group + 1) * whole]
            for extra in range(rest):
                first = groups * whole + extra * users
                cut[extra, part * users : (part + 1) * users] = found[first : first + users]
        column += groups * width
        for extra in range(rest):
            out_ref[:, column : column + piece] = dot(turn, cut[extra]).astype(BF16)
            column += piece
    used = mine & (iota((users * SUB, rows), 1) < count_ref[0])
    number = jnp.sum(used.astype(F32), axis=1, keepdims=True)
    out_ref[:, column : column + LANES] = jnp.broadcast_to(number, (users * SUB, LANES)).astype(
        BF16
    )


def weight_rings(groups, members):
    round_trip = [(at, 0) for at in range(groups // 2)]
    round_trip += [(at, 1) for at in reversed(range(groups // 2))]
    length, layers = (len(round_trip), members // 4)
    rings = []
    for core in range(2):
        up, down = ([], [])
        low, high = (list(range(length // 2)), list(range(length // 2, length)))
        for layer in range(1, layers):
            turned = layer % 2 == 0
            up += [(layer, at) for at in (low[::-1] if turned else low)]
            down += [(layer, at) for at in (high if turned else high[::-1])]
        path = [(0, at) for at in reversed(range(length))] + up + down[::-1]
        ring = []
        for layer, at in path:
            pair, inner = round_trip[(at + core * length // 2) % length]
            ring.append((2 * pair + core) * members + 2 * layer + inner)
        rings.append(ring)
    return rings


def start_weights(ring_of, groups, members, sources, target, sems):
    pairs = groups // 2
    depth = sources[0].shape[1]
    side = lax.rem(lax.axis_index("grp"), 2)
    far_end = lax.div(lax.axis_index("fsdp"), members // 2)
    rings = weight_rings(groups, members)

    def start(member):
        end, holder = divmod(member, members // 2)
        for swapped, source in enumerate(sources):

            @pl.when(far_end == (1 - end if swapped else end))
            def _():
                for pair in range(pairs):
                    spots = [
                        ring.index((2 * pair + core) * members + holder)
                        for core, ring in enumerate(rings)
                    ]
                    spot = jnp.where(side == ring_of, spots[0], spots[1])
                    pltpu.make_async_copy(
                        source.at[spot],
                        target.at[member, pl.ds(pair * depth, depth), :],
                        sems.at[member, pair],
                    ).start()

    return start


def wait_block(target, place, pairs, sems):
    depth = target.shape[1] // pairs
    for pair in range(pairs):
        block = target.at[place, pl.ds(pair * depth, depth), :]
        pltpu.make_async_copy(block, block, sems.at[place, pair]).wait()


def near_kernel(
    groups_of,
    members,
    most,
    got_ref,
    near_ref,
    near_swapped_ref,
    down_ref,
    x_out_ref,
    frozen_ref,
    hidden_ref,
    x_ref,
    cut_ref,
    w_ref,
    got_sem,
    out_sem,
    w_sem,
):
    groups, rest = divmod(most, SUB)
    devices = groups_of * members
    width = x_ref.shape[1]
    whole = devices * SUB
    half = w_ref.shape[1]
    copies = []
    column = 0
    for group in range(groups):
        copies.append(
            (got_ref.at[:, pl.ds(column, width)], x_ref.at[pl.ds(group * whole, whole), :])
        )
        column += width
    for extra in range(rest):
        copies.append((got_ref.at[:, pl.ds(column, width // SUB)], cut_ref.at[extra]))
        column += width // SUB
    copies = [
        pltpu.make_async_copy(source, target, got_sem.at[place])
        for place, (source, target) in enumerate(copies)
    ]
    for copy in copies:
        copy.start()
    start = start_weights(0, groups_of, members, (near_ref, near_swapped_ref), w_ref, w_sem)
    for member in range(members):
        if member == 2:
            for copy in copies:
                copy.wait()
        start(member)
    join_pieces(devices, groups * whole, rest, x_ref, cut_ref)
    out = pltpu.make_async_copy(x_ref, x_out_ref, out_sem)
    out.start()

    frozen_ref[...] = jnp.zeros_like(frozen_ref)
    hidden_ref[...] = jnp.zeros_like(hidden_ref)
    side = lax.rem(lax.axis_index("grp"), 2)

    def add_shard(shard, unused):
        wait_block(w_ref, shard, groups_of // 2, w_sem)
        near = pl.ds(pl.multiple_of((2 * shard + side) * half, half), half)
        both = pl.ds(pl.multiple_of(2 * shard * half, 2 * half), 2 * half)
        frozen_ref[...] += dot(x_ref[:, near], w_ref[shard])
        hidden_ref[...] += dot(x_ref[:, both], down_ref[:, both], ((1,), (1,)))
        return unused

    lax.fori_loop(0, members, add_shard, 0, unroll=8)
    out.wait()


def join_pieces(devices, bottom, rest, full, cut):
    whole = devices * SUB
    line, other = (iota((whole, whole), 0), iota((whole, whole), 1))
    turn = (other == line % devices * SUB + line // devices).astype(BF16)
    piece = full.shape[1] // SUB
    for extra in range(rest):
        first = bottom + extra * devices
        rows = dot(turn, cut[extra]).astype(BF16)
        for part in range(SUB):
            full[first : first + devices, part * piece : (part + 1) * piece] = rows[
                part * devices : (part + 1) * devices
            ]


def user_kernel(
    groups_of,
    members,
    most,
    cap_ref,
    clip_ref,
    got_ref,
    rows_ref,
    near_frozen_ref,
    near_hidden_ref,
    far_ref,
    far_swapped_ref,
    down_ref,
    up_ref,
    *refs,
):
    keep_refs, send_refs = (refs[0:2], refs[2:4])
    (
        x_ref,
        goal_ref,
        cut_goal_ref,
        used_ref,
        w_ref,
        frozen_ref,
        hidden_ref,
        delta_ref,
        got_sem,
        w_sem,
    ) = refs[4:]
    groups, rest = divmod(most, SUB)
    devices = groups_of * members
    rank, width = down_ref.shape
    kv_width = up_ref.shape[1]
    whole = devices * SUB
    half = w_ref.shape[1]
    copies = [(rows_ref, x_ref)]
    column = groups * width + rest * width // SUB
    for group in range(groups):
        copies.append(
            (got_ref.at[:, pl.ds(column, kv_width)], goal_ref.at[pl.ds(group * whole, whole), :])
        )
        column += kv_width
    for extra in range(rest):
        copies.append((got_ref.at[:, pl.ds(column, kv_width // SUB)], cut_goal_ref.at[extra]))
        column += kv_width // SUB
    copies.append((got_ref.at[:, pl.ds(column, LANES)], used_ref))
    copies = [
        pltpu.make_async_copy(source, target, got_sem.at[place])
        for place, (source, target) in enumerate(copies)
    ]
    for copy in copies[1:] + copies[:1]:
        copy.start()
    start = start_weights(1, groups_of, members, (far_ref, far_swapped_ref), w_ref, w_sem)
    for member in range(members):
        start(member)
    for copy in copies[1:]:
        copy.wait()
    join_pieces(devices, groups * whole, rest, goal_ref, cut_goal_ref)

    cap = cap_ref[lax.axis_index("grp") * members + lax.axis_index("fsdp")].astype(F32)
    used = used_ref[...]
    pieces = []
    if groups:
        line, other = (iota((whole, whole), 0), iota((whole, whole), 1))
        earlier = dot(((other // SUB < line // SUB) & (other % SUB == 0)).astype(BF16), used)
        own = used.astype(F32)
        for group in range(groups):
            spot = (iota((whole, LANES), 0) % SUB + group * SUB).astype(F32)
            live = (spot < own) & (earlier + spot < cap)
            pieces.append(jnp.where(live, 1.0 / cap, 0.0)[:, :1])
    line, other = (iota((devices, whole), 0), iota((devices, whole), 1))
    earlier = dot((other < line * SUB).astype(BF16) * (other % SUB == 0).astype(BF16), used)
    own = dot((other == line * SUB).astype(BF16), used)
    for extra in range(rest):
        spot = float(groups * SUB + extra)
        live = (own > spot) & (earlier + spot < cap)
        pieces.append(jnp.where(live, 1.0 / cap, 0.0)[:, :1])
    scale = jnp.concatenate(pieces, axis=0) if len(pieces) > 1 else pieces[0]

    frozen_ref[...] = near_frozen_ref[...]
    hidden_ref[...] = near_hidden_ref[...]
    side = lax.rem(lax.axis_index("grp"), 2)
    copies[0].wait()

    def add_shard(shard, unused):
        wait_block(w_ref, shard, groups_of // 2, w_sem)
        far = pl.ds(pl.multiple_of((2 * shard + 1 - side) * half, half), half)
        frozen_ref[...] += dot(x_ref[:, far], w_ref[shard])
        return unused

    lax.fori_loop(0, members, add_shard, 0, unroll=8)

    rate = ADAPTER_SCALE * LEARN_RATE
    block = min(width, 1024)
    up = up_ref[...].astype(F32)
    up_half = up_ref[...]
    up_delta = jnp.zeros((rank, kv_width), F32)
    for step in range(STEPS):
        hidden = hidden_ref[...].astype(BF16)
        error = frozen_ref[...] + ADAPTER_SCALE * dot(hidden, up_half) - goal_ref[...].astype(F32)
        residual = (scale * error).astype(BF16)
        back = dot(residual, up_half, ((1,), (1,))).astype(BF16)
        up_delta = up_delta - rate * dot(hidden, residual, ((0,), (0,)))
        last = step == STEPS - 1
        if not last:
            up_half = (up + up_delta).astype(BF16)
            hidden_ref[...] = jnp.zeros_like(hidden_ref)

        def down_block(at, unused):
            lanes = pl.ds(pl.multiple_of(at * block, block), block)
            moved = -rate * dot(back, x_ref[:, lanes], ((0,), (0,)))
            if step:
                moved = moved + delta_ref[:, lanes]
            delta_ref[:, lanes] = moved
            if not last:
                half_down = (down_ref[:, lanes].astype(F32) + moved).astype(BF16)
                hidden_ref[...] += dot(x_ref[:, lanes], half_down, ((1,), (1,)))
                return unused
            square = moved * moved
            for at in range(0, block, LANES):
                unused = unused + square[:, at : at + LANES]
            return unused

        squares = lax.fori_loop(
            0, width // block, down_block, jnp.zeros((rank, LANES), F32), unroll=8
        )

    total = jnp.sum(squares) + jnp.sum(up_delta * up_delta) + EPSILON
    total = jnp.full((1, LANES), total, F32)
    factor = jnp.minimum(1.0, clip_ref[0] / jnp.sqrt(total))[:, :1]
    share = width // devices
    up_share = kv_width // devices
    up_turned = (factor * up_delta).T
    pieces = share // rank
    tall = up_share // pieces

    def write(core, targets):
        edge = targets[0].shape[3]
        for pair in range(devices // members // 2):
            for member in range(members):
                device = (2 * pair + core) * members + member
                spot = lax.bitwise_xor(lax.div(lax.axis_index("grp"), 2), pair)
                inner = lax.bitwise_xor(lax.rem(lax.axis_index("fsdp"), 2), member % 2)
                outer = member // 2
                moved = factor * delta_ref[:, device * share : (device + 1) * share]
                targets[0][spot, inner, outer] = moved[:edge]
                targets[1][spot, inner, outer, : rank - edge, :] = moved[edge:]
                first = device * up_share
                parts = [
                    up_turned[first + at * tall : first + (at + 1) * tall] for at in range(pieces)
                ]
                targets[1][spot, inner, outer, rank - edge :, :] = (
                    jnp.concatenate(parts, axis=1) if pieces > 1 else parts[0]
                )

    for core in range(2):
        mine = side == core

        @pl.when(mine)
        def _():
            write(core, keep_refs)

        @pl.when(jnp.logical_not(mine))
        def _():
            write(core, send_refs)


def halve(package, axis, bits, partner):
    bit = package.shape[bits] // 2
    while bit:
        keep = lax.slice_in_dim(package, 0, bit, axis=bits)
        send = lax.slice_in_dim(package, bit, 2 * bit, axis=bits)
        pairs = [(at, at ^ (partner * bit)) for at in range(lax.axis_size(axis))]
        package = lax.ppermute(send, axis, pairs) + keep
        bit //= 2
    return package


def body(
    tokens,
    targets,
    row_owner_user,
    device_row_count,
    user_row_cap,
    value_weight,
    adapter_down,
    adapter_up,
    clip_norm_bound,
    down_noise,
    up_noise,
):
    groups, members = (lax.axis_size("grp"), lax.axis_size("fsdp"))
    devices = groups * members
    side = lax.axis_index("grp") % 2
    per_dev, width = tokens.shape
    kv_width = targets.shape[1]
    rank = adapter_down.shape[1]
    users = user_row_cap.shape[0]
    most = 3 * per_dev // (2 * devices)
    slots = devices * most
    whole = devices * SUB
    whole_groups, rest = divmod(most, SUB)
    smem = pl.BlockSpec(memory_space=pltpu.SMEM)
    vmem = pl.BlockSpec(memory_space=pltpu.VMEM)
    anywhere = pl.BlockSpec(memory_space=pl.ANY)

    half = value_weight.shape[0] // 2
    depth = half // (groups // 2)
    pair = lax.axis_index("grp") // 2
    mine = lax.dynamic_slice_in_dim(value_weight, side * half + pair * depth, depth, axis=0)
    across = [(at, at ^ (members // 2)) for at in range(members)]
    swapped = lax.ppermute(mine, "fsdp", across)
    rings = weight_rings(groups, members)
    rings += [[at + members // 2 for at in ring] for ring in rings]
    swap = [(at, at ^ 1) for at in range(groups)]

    columns = whole_groups * (width + kv_width) + rest * (width + kv_width) // SUB + LANES
    packed = pl.pallas_call(
        lambda *refs: pack_kernel(users, most, *refs),
        out_shape=jax.ShapeDtypeStruct((users * SUB, columns), BF16),
        in_specs=[smem, vmem, vmem, vmem],
        out_specs=vmem,
        scratch_shapes=[
            pltpu.VMEM((max(rest, 1), users * SUB, width // SUB), BF16),
            pltpu.VMEM((max(rest, 1), users * SUB, kv_width // SUB), BF16),
        ],
        compiler_params=pltpu.CompilerParams(vmem_limit_bytes=VMEM_BYTES),
        name="pack_rows",
    )(device_row_count, row_owner_user.reshape(1, per_dev), tokens, targets)
    near = lax.all_gather(mine, BOTH, axis=0, axis_index_groups=rings)
    swapped, unused = lax.optimization_barrier((swapped, packed))
    near_swapped = lax.all_gather(swapped, BOTH, axis=0, axis_index_groups=rings)
    far = lax.ppermute(near, "grp", swap)
    far_swapped = lax.ppermute(near_swapped, "grp", swap)
    got = lax.all_to_all(
        packed.reshape(users, SUB, columns), BOTH, split_axis=0, concat_axis=0, tiled=True
    ).reshape(whole, columns)
    share = width // devices
    tall = rank + kv_width // devices * rank // share
    down = adapter_down.T
    rows, near_frozen, near_hidden = pl.pallas_call(
        lambda *refs: near_kernel(groups, members, most, *refs),
        out_shape=[
            jax.ShapeDtypeStruct((slots, width), BF16),
            jax.ShapeDtypeStruct((slots, kv_width), F32),
            jax.ShapeDtypeStruct((slots, rank), F32),
        ],
        in_specs=[anywhere, anywhere, anywhere, vmem],
        out_specs=[anywhere, vmem, vmem],
        scratch_shapes=[
            pltpu.VMEM((slots, width), BF16),
            pltpu.VMEM((max(rest, 1), whole, width // SUB), BF16),
            pltpu.VMEM((members, half, kv_width), BF16),
            pltpu.SemaphoreType.DMA((whole_groups + rest,)),
            pltpu.SemaphoreType.DMA,
            pltpu.SemaphoreType.DMA((members, groups // 2)),
        ],
        compiler_params=pltpu.CompilerParams(vmem_limit_bytes=VMEM_BYTES),
        cost_estimate=pl.CostEstimate(
            flops=slots * width * kv_width, bytes_accessed=3 * 10**7, transcendentals=0
        ),
        name="near_product",
    )(got, near, near_swapped, down)

    edge = tall // (2 * SUB) * SUB
    grid = (groups // 2, 2, members // 2)
    streams = [jax.ShapeDtypeStruct(grid + (size, share), F32) for size in (edge, tall - edge)]
    kept_y, kept_x, sent_y, sent_x = pl.pallas_call(
        lambda *refs: user_kernel(groups, members, most, *refs),
        out_shape=streams * 2,
        in_specs=[smem] * 2 + [anywhere] * 2 + [vmem] * 2 + [anywhere] * 2 + [vmem] * 2,
        out_specs=[vmem] * 4,
        scratch_shapes=[
            pltpu.VMEM((slots, width), BF16),
            pltpu.VMEM((slots, kv_width), BF16),
            pltpu.VMEM((max(rest, 1), whole, kv_width // SUB), BF16),
            pltpu.VMEM((whole, LANES), BF16),
            pltpu.VMEM((members, half, kv_width), BF16),
            pltpu.VMEM((slots, kv_width), F32),
            pltpu.VMEM((slots, rank), F32),
            pltpu.VMEM((rank, width), F32),
            pltpu.SemaphoreType.DMA((whole_groups + rest + 2,)),
            pltpu.SemaphoreType.DMA((members, groups // 2)),
        ],
        compiler_params=pltpu.CompilerParams(vmem_limit_bytes=VMEM_BYTES),
        name="user_steps",
    )(
        user_row_cap,
        clip_norm_bound,
        got,
        rows,
        near_frozen,
        near_hidden,
        far,
        far_swapped,
        down,
        adapter_up,
    )

    first = kept_y + lax.ppermute(sent_y, "grp", swap)
    second = kept_x + lax.ppermute(sent_x, "grp", swap)
    first = halve(halve(first, "grp", 0, 2), "fsdp", 1, 1)
    second = halve(halve(second, "fsdp", 1, 1), "grp", 0, 2)
    package = jnp.concatenate([first[0, 0], second[0, 0]], axis=1)
    lines = [list(range(one, members, 2)) for one in range(2)]
    package = lax.all_to_all(
        package, "fsdp", split_axis=0, concat_axis=0, axis_index_groups=lines, tiled=True
    )
    package = jnp.sum(package, axis=0)
    clip = clip_norm_bound[0]
    update_a = package[:rank].T + clip * down_noise
    pieces = share // rank
    up_sum = package[rank:].reshape(tall - rank, pieces, rank).transpose(1, 0, 2)
    update_b = up_sum.reshape(kv_width // devices, rank).T + clip * up_noise
    return (update_a, update_b)


def solution(mesh):
    in_specs = (
        P(BOTH, None),
        P(BOTH, None),
        P(BOTH, None),
        P(BOTH),
        P(),
        P("fsdp", None),
        P(),
        P(),
        P(),
        P(BOTH, None),
        P(None, BOTH),
    )
    out_specs = (P(BOTH, None), P(None, BOTH))
    return jax.shard_map(body, mesh=mesh, in_specs=in_specs, out_specs=out_specs, check_vma=False)
```
